32 devices in a mesh: dp: 4 (over y, x), ctx: 8 (over z, core).
Axes of the slice: x: 2, y: 2, z: 4, core: 2. Of those that a mesh axis runs over, the one named last changes fastest.
Arguments:
- context: bfloat16 [4096, 4096], P('ctx'), may hold values from -6 to 6
- w_key: bfloat16 [4096, 1024], P('ctx', 'dp'), may hold values from -0.09375 to 0.09375
- w_value: bfloat16 [4096, 1024], P('ctx', 'dp'), may hold values from -0.09375 to 0.09375
- queries: bfloat16 [512, 1024], P('ctx', 'dp'), may hold values from -300 to 300
- offsets: int32 [512], replicated, may hold values from 3072 to 4095, as said below
- head_gain: bfloat16 [1024], P('dp'), may hold values from 0.099609375 to 1.8984375
- w_out: bfloat16 [1024, 4096], P('dp', 'ctx'), may hold values from -0.1875 to 0.1875
Outputs:
- mixed: bfloat16 [512, 4096], P('ctx', 'dp')
The draws below stay inside these ranges and needn't reach their ends.
Inputs may be any that keep to these rules, and one draw needn't show every extreme that they name: `offsets`: strictly increasing along the latents; latent l's offset is 4096 - 2 * 512 + 2 * l or one more, the last latent's offset is 4095.
All inputs are finite; a program needn't handle non-finite values.
Results may differ from the reference program's by a relative error of at most 0.012.
Values may be sent and summed in bfloat16 or wider, within the bound.
No kernel may reach another device: no remote copies, remote signals or barrier semaphores. Data moves between devices by JAX's collectives and lax.ppermute only.
A program may use at most 64 MiB of HBM per device.

```python
import math
import jax
import jax.numpy as jnp
from jax import lax

D = 4096
DH = 128
HEADS = 8
CONTEXT = 4096
LATENTS = 512


def draw_queries(key, part):
    key = jax.random.fold_in(key, 7)
    base_key, pick_key, boost_key = jax.random.split(key, 3)
    base_rows = jnp.clip(jax.random.normal(base_key, (LATENTS, HEADS * DH), jnp.float32), -5.0, 5.0)
    strong = jax.random.uniform(pick_key, (LATENTS, 1), jnp.float32) < 0.03125
    boost = jnp.exp(jax.random.uniform(boost_key, (LATENTS, 1), jnp.float32, math.log(20.0), math.log(60.0)))
    return jnp.where(strong, base_rows * boost, base_rows).astype(jnp.bfloat16)


def draw_offsets(key, part):
    key = jax.random.fold_in(key, 11)
    jitter = jax.random.randint(key, (LATENTS,), 0, 2, dtype=jnp.int32)
    jitter = jitter.at[0].set(0).at[LATENTS - 1].set(1)
    start = CONTEXT - 2 * LATENTS
    return (start + 2 * jnp.arange(LATENTS, dtype=jnp.int32) + jitter).astype(jnp.int32)


def level_of(key, extent, shards, low, largest):
    gain = 1.0
    for dim, parts in shards:
        steps = jax.random.uniform(jax.random.fold_in(jax.random.fold_in(key, 6), dim), (parts,), jnp.float32, low / len(shards), largest / len(shards))
        gain = gain * jnp.repeat(jnp.exp(steps), extent[dim] // parts).reshape((-1,) + (1,) * (len(extent) - 1 - dim))
    return gain


def noise(own_key, extent, deviation, most, shards=(), held_as=jnp.bfloat16):
    gain = level_of(own_key, extent, shards, -0.22, 0.18) if shards else 1.0
    entries = jax.random.normal(own_key, extent, jnp.float32) * deviation * gain
    return jnp.minimum(jnp.maximum(entries, -most), most).astype(held_as)


def setup_inputs(seed: int = 0) -> dict:
    streams_of = jax.random.split(jax.random.key(seed), 8)
    context = noise(streams_of[0], (CONTEXT, D), 1.0, 6.0, ((0, 8),))
    w_key = noise(streams_of[1], (D, HEADS * DH), D ** -0.5, 0.09375, ((0, 8), (1, 4)))
    w_value = noise(streams_of[2], (D, HEADS * DH), D ** -0.5, 0.09375, ((0, 8), (1, 4)))
    queries = draw_queries(jax.random.fold_in(streams_of[7], 71), 0)
    offsets = draw_offsets(jax.random.fold_in(streams_of[7], 71), 0)
    head_gain = jnp.clip(1.0 + 0.18 * jax.random.normal(streams_of[5], (HEADS * DH,), jnp.float32), 0.099609375, 1.8984375).astype(jnp.bfloat16)
    w_out = noise(streams_of[6], (HEADS * DH, D), (HEADS * DH) ** -0.5, 0.1875, ((0, 4), (1, 8)))
    return dict(context=context, w_key=w_key, w_value=w_value, queries=queries, offsets=offsets, head_gain=head_gain, w_out=w_out)


NEGATIVE = -1e+30

def reference(context, w_key, w_value, queries, offsets, head_gain, w_out):
    key_rows = jnp.dot(context, w_key, preferred_element_type=jnp.float32).astype(jnp.bfloat16)
    value_rows = jnp.dot(context, w_value, preferred_element_type=jnp.float32).astype(jnp.bfloat16)
    positions = jnp.arange(CONTEXT, dtype=jnp.int32)
    is_live = positions[None, :] <= offsets[:, None]
    score_scale = 1.0 / math.sqrt(DH)

    def one_head(head_index):
        first_col = (head_index * DH).astype(jnp.int32)
        query_h = lax.dynamic_slice_in_dim(queries, first_col, DH, 1)
        key_h = lax.dynamic_slice_in_dim(key_rows, first_col, DH, 1)
        value_h = lax.dynamic_slice_in_dim(value_rows, first_col, DH, 1)
        scores = jnp.dot(query_h, key_h.T, preferred_element_type=jnp.float32) * score_scale
        masked = jnp.where(is_live, scores, NEGATIVE)
        row_peak = lax.optimization_barrier(jnp.max(masked, axis=1, keepdims=True))
        weights = jnp.where(is_live, jnp.exp(masked - row_peak), 0.0).astype(jnp.bfloat16)
        numerator = jnp.dot(weights, value_h, preferred_element_type=jnp.float32)
        row_total = lax.optimization_barrier(jnp.sum(weights.astype(jnp.float32), axis=1, keepdims=True))
        attended = numerator / row_total
        gain_h = lax.dynamic_slice_in_dim(head_gain, first_col, DH, 0).astype(jnp.float32)
        mean_square = lax.optimization_barrier(jnp.mean(attended * attended, axis=1, keepdims=True))
        return (attended * lax.rsqrt(mean_square + 1e-05) * gain_h[None, :]).astype(jnp.bfloat16)
    normed = lax.map(one_head, jnp.arange(HEADS, dtype=jnp.int32))
    normed = jnp.transpose(normed, (1, 0, 2)).reshape(LATENTS, HEADS * DH)
    return jnp.dot(normed, w_out, preferred_element_type=jnp.float32).astype(jnp.bfloat16)
```

```python
import math

import jax
import jax.numpy as jnp
from jax import lax
from jax.sharding import PartitionSpec as P

DH = 128
NEGATIVE = -1e30
CORES = 2


def three_parts(value):
    high = value.astype(jnp.bfloat16)
    rest = value - high.astype(jnp.float32)
    middle = rest.astype(jnp.bfloat16)
    low = (rest - middle.astype(jnp.float32)).astype(jnp.bfloat16)
    return [high, middle, low]


def on_device(n_dp, n_ctx, context, w_key, w_value, queries, offsets, head_gain, w_out):
    chips = n_ctx // CORES
    rows, model = context.shape
    depth, panel = w_key.shape
    half = panel // CORES
    heads = half // DH
    lat_count = queries.shape[0]
    latents = offsets.shape[0]
    me = lax.axis_index("ctx")
    chip = me // CORES
    core = lax.rem(me, CORES)

    swap = [(i, i ^ 1) for i in range(n_ctx)]

    def line(shift, first, last):
        return [
            (z * CORES + k, (z + shift) * CORES + k)
            for z in range(first, last + 1)
            for k in range(CORES)
        ]

    def columns(array, which):
        return lax.dynamic_slice_in_dim(array, which * half, half, 1)

    def along_line(block):
        found = [[(chip, block)]]
        up = down = block
        for step in range(1, chips):
            up = lax.ppermute(up, "ctx", line(1, step - 1, chips - 2))
            down = lax.ppermute(down, "ctx", line(-1, 1, chips - step))
            if 2 * step < chips:
                found.append([(jnp.maximum(chip - step, 0), up), (jnp.minimum(chip + step, chips - 1), down)])
            else:
                below = chip >= step
                source = jnp.where(below, chip - step, jnp.minimum(chip + step, chips - 1))
                found.append([(source, jnp.where(below, up, down))])
        return found

    mine = jnp.concatenate([columns(w_key, core), columns(w_value, core)], axis=1)
    other = jnp.concatenate([columns(w_key, 1 - core), columns(w_value, 1 - core)], axis=1)
    sibling = lax.ppermute(other, "ctx", swap)
    context_sibling = lax.ppermute(context, "ctx", swap)
    query_rows = lax.all_gather(queries, "ctx", axis=0, tiled=True)
    query_rows = columns(query_rows, core)
    first_half = along_line(mine)
    second_half = along_line(sibling)

    own_sum = jnp.zeros((rows, 2 * half), jnp.float32)
    sibling_sum = jnp.zeros((rows, 2 * half), jnp.float32)
    for step in range(chips):
        for found, who in ((first_half, core), (second_half, 1 - core)):
            for source, block in found[step]:
                start = (source * CORES + who) * depth
                own_sum += jnp.dot(
                    lax.dynamic_slice_in_dim(context, start, depth, 1), block,
                    preferred_element_type=jnp.float32,
                )
                sibling_sum += jnp.dot(
                    lax.dynamic_slice_in_dim(context_sibling, start, depth, 1), block,
                    preferred_element_type=jnp.float32,
                )
    pairs = jnp.concatenate([own_sum, sibling_sum], axis=0).astype(jnp.bfloat16)
    own_first = me * rows
    sibling_first = (me + 1 - 2 * core) * rows
    within = jnp.arange(rows, dtype=jnp.int32)
    positions = jnp.concatenate([own_first + within, sibling_first + within])
    live = positions[:, None] <= offsets[None, :]

    w_all = lax.all_gather(w_out, "ctx", axis=1, tiled=True)

    score_scale = 1.0 / math.sqrt(DH)
    messages = []
    for h in range(heads):
        keys = pairs[:, h * DH : (h + 1) * DH]
        values = pairs[:, half + h * DH : half + (h + 1) * DH]
        query = query_rows[:, h * DH : (h + 1) * DH]
        scores = lax.dot_general(
            keys, query, (((1,), (1,)), ((), ())), preferred_element_type=jnp.float32
        ) * score_scale
        masked = jnp.where(live, scores, NEGATIVE)
        peak = jnp.max(masked, axis=0)
        weights = jnp.where(live, jnp.exp(masked - peak[None, :]), 0.0).astype(jnp.bfloat16)
        total = jnp.sum(weights.astype(jnp.float32), axis=0)
        numerator = lax.dot_general(
            values, weights, (((0,), (0,)), ((), ())), preferred_element_type=jnp.float32
        )
        stats = jnp.stack(three_parts(peak) + three_parts(total), axis=0)
        stats = jnp.concatenate([stats, jnp.zeros((10, latents), jnp.bfloat16)], axis=0)
        messages.append(jnp.concatenate([numerator.astype(jnp.bfloat16), stats], axis=0))
    message = jnp.stack(messages)
    message = message.reshape(heads, DH + 16, n_ctx, lat_count).transpose(2, 0, 1, 3)
    arrived = lax.all_to_all(message, "ctx", 0, 0, tiled=False)
    arrived = arrived.reshape(chips, CORES, heads, DH + 16, lat_count).astype(jnp.float32)
    peaks = jnp.sum(arrived[:, :, :, DH : DH + 3, :], axis=3)
    totals = jnp.sum(arrived[:, :, :, DH + 3 : DH + 6, :], axis=3)
    top = jnp.max(peaks, axis=0)
    scale = jnp.exp(peaks - top[None])
    total = jnp.sum(totals * scale, axis=0)
    attended = jnp.sum(arrived[:, :, :, :DH, :] * scale[:, :, :, None, :], axis=0) / total[:, :, None, :]
    mean_square = jnp.mean(attended * attended, axis=2, keepdims=True)
    gain = head_gain.astype(jnp.float32).reshape(CORES, heads, DH, 1)
    normed = (attended * lax.rsqrt(mean_square + 1e-05) * gain).astype(jnp.bfloat16)
    normed = normed.reshape(panel, lat_count)

    terms = lax.dot_general(
        normed, w_all, (((0,), (0,)), ((), ())), preferred_element_type=jnp.float32
    ).astype(jnp.bfloat16)
    wide = terms.shape[1] // n_dp
    terms = terms.reshape(lat_count, n_dp, wide).transpose(1, 0, 2)
    terms = lax.all_to_all(terms, "dp", 0, 0, tiled=False)
    return jnp.sum(terms.astype(jnp.float32), axis=0).astype(jnp.bfloat16)


def solution(mesh):
    n_dp, n_ctx = mesh.shape["dp"], mesh.shape["ctx"]
    placed = (
        P("ctx", None),
        P("ctx", "dp"),
        P("ctx", "dp"),
        P("ctx", "dp"),
        P(),
        P("dp"),
        P("dp", "ctx"),
    )

    def body(*args):
        return on_device(n_dp, n_ctx, *args)

    return jax.shard_map(
        body, mesh=mesh, in_specs=placed, out_specs=P("ctx", "dp"), check_vma=False
    )
```

```python
import functools
import math

import jax
import jax.numpy as jnp
from jax import lax
from jax.experimental import pallas as pl
from jax.experimental.pallas import tpu as pltpu
from jax.sharding import PartitionSpec as P

DH = 128
NEGATIVE = -1e30
CORES = 2
STATS = 16
VMEM = pl.BlockSpec(memory_space=pltpu.VMEM)
SMEM = pl.BlockSpec(memory_space=pltpu.SMEM)
ANY = pl.BlockSpec(memory_space=pl.ANY)
PARAMS = pltpu.CompilerParams(vmem_limit_bytes=40 * 2**20)


def three_parts(value):
    high = value.astype(jnp.bfloat16).astype(jnp.float32)
    rest = value - high
    middle = rest.astype(jnp.bfloat16).astype(jnp.float32)
    low = (rest - middle).astype(jnp.bfloat16).astype(jnp.float32)
    return [high, middle, low]


def start_slices(starts_ref, contexts, buffer, sems, count, depth):
    copies = []
    for b in range(count):
        for part in range(CORES):
            first = pl.multiple_of(starts_ref[b * CORES + part], DH)
            for which in range(CORES):
                slot = (b * CORES + part) * CORES + which
                copies.append(
                    pltpu.make_async_copy(
                        contexts[which].at[:, pl.ds(first, depth)], buffer.at[slot], sems.at[slot]
                    )
                )
    for copy in copies:
        copy.start()
    return copies


def add_products(copies, buffer, blocks, acc_ref, rows, depth, piece, fresh):
    for b, block in enumerate(blocks):
        for part in range(CORES):
            weight = block[part * piece : part * piece + depth, :]
            for which in range(CORES):
                slot = (b * CORES + part) * CORES + which
                copies[slot].wait()
                product = jnp.dot(buffer[slot], weight, preferred_element_type=jnp.float32)
                place = slice(which * rows, (which + 1) * rows)
                if fresh and b == 0 and part == 0:
                    acc_ref[place, :] = product
                else:
                    acc_ref[place, :] += product


def project_kernel(count, has_acc, depth, piece, *refs):
    starts_ref, own_ref, sibling_ref = refs[:3]
    blocks = refs[3 : 3 + count]
    acc_in = refs[3 + count] if has_acc else None
    acc_ref, buffer, sems = refs[-3:]
    rows = own_ref.shape[0]
    copies = start_slices(starts_ref, (own_ref, sibling_ref), buffer, sems, count, depth)
    if has_acc:
        acc_ref[...] = acc_in[...]
    add_products(copies, buffer, blocks, acc_ref, rows, depth, piece, not has_acc)


def project(starts, own, sibling, blocks, acc, depth, piece):
    count = len(blocks)
    rows = own.shape[0]
    width = blocks[0].shape[1]
    operands = [starts, own, sibling, *blocks] + ([acc] if acc is not None else [])
    return pl.pallas_call(
        functools.partial(project_kernel, count, acc is not None, depth, piece),
        out_shape=jax.ShapeDtypeStruct((CORES * rows, width), jnp.float32),
        in_specs=[SMEM, ANY, ANY] + [VMEM] * (len(operands) - 3),
        out_specs=VMEM,
        scratch_shapes=[
            pltpu.VMEM((count * CORES * CORES, rows, depth), own.dtype),
            pltpu.SemaphoreType.DMA((count * CORES * CORES,)),
        ],
        compiler_params=PARAMS,
        cost_estimate=pl.CostEstimate(
            flops=2 * count * CORES * CORES * rows * depth * width,
            bytes_accessed=2 * count * CORES * CORES * rows * depth,
            transcendentals=0,
        ),
    )(*operands)


def attend_kernel(chips, heads, depth, piece, *refs):
    starts_ref, firsts_ref, own_ref, sibling_ref = refs[:4]
    blocks = refs[4 : 4 + chips]
    acc_in, offsets_ref = refs[4 + chips : 6 + chips]
    messages = refs[6 + chips : 6 + 2 * chips]
    acc_ref, buffer, sems = refs[6 + 2 * chips :]
    rows = own_ref.shape[0]
    half = heads * DH
    copies = start_slices(starts_ref, (own_ref, sibling_ref), buffer, sems, 1, depth)
    acc_ref[...] = acc_in[...]
    add_products(copies, buffer, blocks[-1:], acc_ref, rows, depth, piece, False)
    score_scale = 1.0 / math.sqrt(DH)
    line = lax.broadcasted_iota(jnp.int32, (CORES * rows, 1), 0)
    positions = jnp.where(line < rows, firsts_ref[0] + line, firsts_ref[1] + line - rows)
    for h in range(heads):
        keys = acc_ref[:, h * DH : (h + 1) * DH].astype(jnp.bfloat16)
        values = acc_ref[:, half + h * DH : half + (h + 1) * DH].T.astype(jnp.bfloat16)
        for j in range(chips):
            parts = []
            for part in range(CORES):
                lines = slice(part * piece + depth, (part + 1) * piece)
                parts.append(blocks[j][lines, h * DH : (h + 1) * DH])
                parts.append(blocks[j][lines, half + h * DH : half + (h + 1) * DH])
            query = jnp.concatenate(parts, axis=0)
            scores = lax.dot_general(
                keys, query, (((1,), (1,)), ((), ())), preferred_element_type=jnp.float32
            ) * score_scale
            live = positions <= offsets_ref[j : j + 1, :]
            masked = jnp.where(live, scores, NEGATIVE)
            peak = jnp.max(masked, axis=0, keepdims=True)
            weights = jnp.where(live, jnp.exp(masked - peak), 0.0).astype(jnp.bfloat16)
            total = jnp.sum(weights.astype(jnp.float32), axis=0, keepdims=True)
            numerator = jnp.dot(values, weights, preferred_element_type=jnp.float32)
            stats = three_parts(peak) + three_parts(total)
            stats.append(jnp.zeros((STATS - len(stats), peak.shape[1]), jnp.float32))
            base = h * (DH + STATS)
            messages[j][base : base + DH, :] = numerator.astype(jnp.bfloat16)
            messages[j][base + DH : base + DH + STATS, :] = jnp.concatenate(stats, axis=0).astype(
                jnp.bfloat16
            )


def attend(starts, firsts, own, sibling, blocks, acc, offset_groups, heads, depth, piece):
    chips = len(blocks)
    rows, width = own.shape[0], blocks[0].shape[1]
    group = offset_groups.shape[1]
    message = jax.ShapeDtypeStruct((heads * (DH + STATS), group), jnp.bfloat16)
    return pl.pallas_call(
        functools.partial(attend_kernel, chips, heads, depth, piece),
        out_shape=[message] * chips,
        in_specs=[SMEM, SMEM, ANY, ANY] + [VMEM] * (chips + 2),
        out_specs=[VMEM] * chips,
        scratch_shapes=[
            pltpu.VMEM((CORES * rows, width), jnp.float32),
            pltpu.VMEM((CORES * CORES, rows, depth), own.dtype),
            pltpu.SemaphoreType.DMA((CORES * CORES,)),
        ],
        compiler_params=PARAMS,
        cost_estimate=pl.CostEstimate(
            flops=8 * CORES * rows * group * chips * heads * DH,
            bytes_accessed=2 * CORES * CORES * rows * depth,
            transcendentals=CORES * rows * group * chips * heads,
        ),
    )(starts, firsts, own, sibling, *blocks, acc, offset_groups)


def combine_kernel(chips, heads, count, *refs):
    messages, gain_ref = refs[:chips], refs[chips]
    own_ref, other_ref = refs[chips + 1 :]
    for h in range(heads):
        base = h * (DH + STATS)
        peaks, totals = [], []
        for j in range(chips):
            stats = messages[j][base + DH : base + DH + STATS, :].astype(jnp.float32)
            peaks.append(stats[0:1] + stats[1:2] + stats[2:3])
            totals.append(stats[3:4] + stats[4:5] + stats[5:6])
        top = functools.reduce(jnp.maximum, peaks)
        total, numerator = 0.0, 0.0
        for j in range(chips):
            scale = jnp.exp(peaks[j] - top)
            total += totals[j] * scale
            numerator += messages[j][base : base + DH, :].astype(jnp.float32) * scale
        attended = numerator / total
        mean_square = jnp.mean(attended * attended, axis=0, keepdims=True)
        normed = (attended * lax.rsqrt(mean_square + 1e-05)).T
        normed = (normed * gain_ref[:, h * DH : (h + 1) * DH].astype(jnp.float32)).astype(jnp.bfloat16)
        own_ref[:, h * DH : (h + 1) * DH] = normed[:count]
        other_ref[:, h * DH : (h + 1) * DH] = normed[count:]


def combine(messages, gain, heads, count):
    chips = len(messages)
    out = jax.ShapeDtypeStruct((count, heads * DH), jnp.bfloat16)
    return pl.pallas_call(
        functools.partial(combine_kernel, chips, heads, count),
        out_shape=[out, out],
        in_specs=[VMEM] * (chips + 1),
        out_specs=[VMEM, VMEM],
        compiler_params=PARAMS,
    )(*messages, gain)


def output_kernel(n_dp, wide, place_ref, own_ref, sibling_ref, w_ref, *refs):
    terms, (buffer, sems) = refs[:n_dp], refs[n_dp:]
    half = own_ref.shape[1]
    copies = []
    for i in range(n_dp):
        first = pl.multiple_of((place_ref[0] ^ i) * wide, DH)
        copies.append(
            pltpu.make_async_copy(w_ref.at[:, pl.ds(first, wide)], buffer.at[i], sems.at[i])
        )
        copies[-1].start()
    mine = pl.multiple_of(place_ref[1] * half, DH)
    other = pl.multiple_of((1 - place_ref[1]) * half, DH)
    for i in range(n_dp):
        copies[i].wait()
        total = jnp.dot(own_ref[...], buffer[i, pl.ds(mine, half), :], preferred_element_type=jnp.float32)
        total += jnp.dot(
            sibling_ref[...], buffer[i, pl.ds(other, half), :], preferred_element_type=jnp.float32
        )
        terms[i][...] = total.astype(jnp.bfloat16)


def output_terms(place, own, sibling, w_all, n_dp):
    wide = w_all.shape[1] // n_dp
    term = jax.ShapeDtypeStruct((own.shape[0], wide), jnp.bfloat16)
    return pl.pallas_call(
        functools.partial(output_kernel, n_dp, wide),
        out_shape=[term] * n_dp,
        in_specs=[SMEM, VMEM, VMEM, ANY],
        out_specs=[VMEM] * n_dp,
        scratch_shapes=[
            pltpu.VMEM((n_dp, w_all.shape[0], wide), w_all.dtype),
            pltpu.SemaphoreType.DMA((n_dp,)),
        ],
        compiler_params=PARAMS,
    )(place, own, sibling, w_all)


def on_device(n_dp, n_ctx, context, w_key, w_value, queries, offsets, head_gain, w_out):
    chips = n_ctx // CORES
    rows = context.shape[0]
    depth, panel = w_key.shape
    half = panel // CORES
    heads = half // DH
    lat_count = queries.shape[0]
    me = lax.axis_index("ctx")
    chip, core = me // CORES, lax.rem(me, CORES)

    def swap(array):
        return lax.ppermute(array, "ctx", [(i, i ^ 1) for i in range(n_ctx)])

    def across(array, bits):
        return lax.ppermute(array, "ctx", [(i, i ^ (bits * CORES)) for i in range(n_ctx)])

    def columns(array, which):
        return lax.dynamic_slice_in_dim(array, which * half, half, 1)

    def half_block(which):
        query = columns(queries, which)
        return jnp.concatenate(
            [
                jnp.concatenate([columns(w_key, which), columns(w_value, which)], axis=1),
                jnp.concatenate([query[: lat_count // 2], query[lat_count // 2 :]], axis=1),
            ],
            axis=0,
        )

    piece = depth + lat_count // 2
    sibling_part = swap(half_block(1 - core))
    context_sibling = swap(context)
    blocks = [jnp.concatenate([half_block(core), sibling_part], axis=0)]
    for j in range(1, chips):
        low = j & -j
        blocks.append(across(blocks[j ^ low], low))
    w_all = lax.all_gather(w_out, "ctx", axis=1, tiled=True)

    sources = [chip ^ j for j in range(chips)]
    starts = [
        (source * CORES + who) * depth for source in sources for who in (core, 1 - core)
    ]

    def starts_of(first, last):
        return jnp.stack(starts[first * CORES : last * CORES]).astype(jnp.int32)

    acc = project(starts_of(0, 1), context, context_sibling, blocks[:1], None, depth, piece)
    acc = project(
        starts_of(1, chips - 1), context, context_sibling, blocks[1:-1], acc, depth, piece
    )
    offset_groups = jnp.stack(
        [
            jnp.concatenate(
                [
                    lax.dynamic_slice_in_dim(offsets, (source * CORES + who) * lat_count, lat_count)
                    for who in (core, 1 - core)
                ]
            )
            for source in sources
        ]
    )
    firsts = jnp.stack([me * rows, (me + 1 - 2 * core) * rows]).astype(jnp.int32)
    messages = attend(
        starts_of(chips - 1, chips), firsts, context, context_sibling, blocks, acc, offset_groups,
        heads, depth, piece,
    )
    arrived = [messages[0]] + [across(messages[j], j) for j in range(1, chips)]
    gain = lax.dynamic_slice_in_dim(head_gain, core * half, half).reshape(1, half)
    normed_own, normed_other = combine(arrived, gain, heads, lat_count)
    normed_sibling = swap(normed_other)
    mine_dp = lax.axis_index("dp")
    terms = output_terms(
        jnp.stack([mine_dp, core]).astype(jnp.int32), normed_own, normed_sibling, w_all, n_dp
    )
    total = terms[0].astype(jnp.float32)
    for i in range(1, n_dp):
        total += lax.ppermute(terms[i], "dp", [(d, d ^ i) for d in range(n_dp)]).astype(jnp.float32)
    return total.astype(jnp.bfloat16)


def solution(mesh):
    n_dp, n_ctx = mesh.shape["dp"], mesh.shape["ctx"]
    placed = (
        P("ctx", None),
        P("ctx", "dp"),
        P("ctx", "dp"),
        P("ctx", "dp"),
        P(),
        P("dp"),
        P("dp", "ctx"),
    )

    def body(*args):
        return on_device(n_dp, n_ctx, *args)

    return jax.shard_map(
        body, mesh=mesh, in_specs=placed, out_specs=P("ctx", "dp"), check_vma=False
    )
```

```python
import functools
import math

import jax
import jax.numpy as jnp
from jax import lax
from jax.experimental import pallas as pl
from jax.experimental.pallas import tpu as pltpu
from jax.sharding import PartitionSpec as P

DH = 128
NEGATIVE = -1e30
CORES = 2
STATS = 16
VMEM = pl.BlockSpec(memory_space=pltpu.VMEM)
SMEM = pl.BlockSpec(memory_space=pltpu.SMEM)
ANY = pl.BlockSpec(memory_space=pl.ANY)
PARAMS = pltpu.CompilerParams(vmem_limit_bytes=40 * 2**20)


def three_parts(value):
    high = value.astype(jnp.bfloat16).astype(jnp.float32)
    rest = value - high
    middle = rest.astype(jnp.bfloat16).astype(jnp.float32)
    low = (rest - middle).astype(jnp.bfloat16).astype(jnp.float32)
    return [high, middle, low]


def start_slices(starts_ref, contexts, buffer, sems, count, depth):
    copies = []
    for b in range(count):
        first = pl.multiple_of(starts_ref[b], DH)
        for which in range(CORES):
            slot = b * CORES + which
            copies.append(
                pltpu.make_async_copy(
                    contexts[which].at[:, pl.ds(first, depth)], buffer.at[slot], sems.at[slot]
                )
            )
    for copy in copies:
        copy.start()
    return copies


def add_products(copies, buffer, blocks, acc_ref, rows, depth, fresh):
    for b, block in enumerate(blocks):
        for which in range(CORES):
            slot = b * CORES + which
            copies[slot].wait()
            product = jnp.dot(buffer[slot], block[:depth, :], preferred_element_type=jnp.float32)
            place = slice(which * rows, (which + 1) * rows)
            if fresh and b == 0:
                acc_ref[place, :] = product
            else:
                acc_ref[place, :] += product


def project_kernel(count, has_acc, depth, *refs):
    starts_ref, own_ref, sibling_ref = refs[:3]
    blocks = refs[3 : 3 + count]
    acc_in = refs[3 + count] if has_acc else None
    acc_ref, buffer, sems = refs[-3:]
    copies = start_slices(starts_ref, (own_ref, sibling_ref), buffer, sems, count, depth)
    if has_acc:
        acc_ref[...] = acc_in[...]
    add_products(copies, buffer, blocks, acc_ref, own_ref.shape[0], depth, not has_acc)


def project(starts, own, sibling, blocks, acc, depth):
    count = len(blocks)
    rows = own.shape[0]
    width = blocks[0].shape[1]
    operands = [starts, own, sibling, *blocks] + ([acc] if acc is not None else [])
    return pl.pallas_call(
        functools.partial(project_kernel, count, acc is not None, depth),
        out_shape=jax.ShapeDtypeStruct((CORES * rows, width), jnp.float32),
        in_specs=[SMEM, ANY, ANY] + [VMEM] * (len(operands) - 3),
        out_specs=VMEM,
        scratch_shapes=[
            pltpu.VMEM((count * CORES, rows, depth), own.dtype),
            pltpu.SemaphoreType.DMA((count * CORES,)),
        ],
        compiler_params=PARAMS,
        cost_estimate=pl.CostEstimate(
            flops=2 * count * CORES * rows * depth * width,
            bytes_accessed=2 * count * CORES * rows * depth,
            transcendentals=0,
        ),
    )(*operands)


def attend_kernel(count, heads, depth, groups, slots, *refs):
    starts_ref, firsts_ref, slots_ref, places_ref, own_ref, sibling_ref = refs[:6]
    blocks = refs[6 : 6 + count]
    acc_in, offsets_ref = refs[6 + count : 8 + count]
    messages = refs[8 + count : 8 + count + slots]
    acc_ref, query_ref, group_ref, buffer, sems = refs[8 + count + slots :]
    rows = own_ref.shape[0]
    half = heads * DH
    lines = blocks[0].shape[0] - depth
    copies = start_slices(starts_ref, (own_ref, sibling_ref), buffer, sems, CORES, depth)
    acc_ref[...] = acc_in[...]
    for b, block in enumerate(blocks):
        query_ref[places_ref[b], :lines, :] = block[depth:, :half]
        query_ref[places_ref[b], lines:, :] = block[depth:, half:]
    add_products(copies, buffer, blocks[-CORES:], acc_ref, rows, depth, False)
    score_scale = 1.0 / math.sqrt(DH)
    line = lax.broadcasted_iota(jnp.int32, (CORES * rows, 1), 0)
    positions = jnp.where(line < rows, firsts_ref[0] + line, firsts_ref[1] + line - rows)
    for h in range(heads):
        keys = acc_ref[:, h * DH : (h + 1) * DH].astype(jnp.bfloat16)
        values = acc_ref[:, half + h * DH : half + (h + 1) * DH].T.astype(jnp.bfloat16)
        for g, members in enumerate(groups):
            query = jnp.concatenate(
                [query_ref[c, :, h * DH : (h + 1) * DH] for c in members], axis=0
            )
            scores = lax.dot_general(
                keys, query, (((1,), (1,)), ((), ())), preferred_element_type=jnp.float32
            ) * score_scale
            live = positions <= offsets_ref[g : g + 1, :]
            masked = jnp.where(live, scores, NEGATIVE)
            peak = jnp.max(masked, axis=0, keepdims=True)
            weights = jnp.where(live, jnp.exp(masked - peak), 0.0).astype(jnp.bfloat16)
            total = jnp.sum(weights.astype(jnp.float32), axis=0, keepdims=True)
            numerator = jnp.dot(values, weights, preferred_element_type=jnp.float32)
            stats = three_parts(peak) + three_parts(total)
            stats.append(jnp.zeros((STATS - len(stats), peak.shape[1]), jnp.float32))
            base = h * (DH + STATS)
            group_ref[g, base : base + DH, :] = numerator.astype(jnp.bfloat16)
            group_ref[g, base + DH : base + DH + STATS, :] = jnp.concatenate(
                stats, axis=0
            ).astype(jnp.bfloat16)
    for m in range(slots):
        messages[m][...] = group_ref[slots_ref[m]]


def attend(starts, firsts, slot_groups, places, own, sibling, blocks, acc, offsets, groups, heads, depth):
    count, slots = len(blocks), slot_groups.shape[0]
    rows, width = own.shape[0], blocks[0].shape[1]
    lat_count = 2 * (blocks[0].shape[0] - depth)
    group = lat_count * len(groups[0])
    length = heads * (DH + STATS)
    group_offsets = jnp.stack(
        [
            jnp.concatenate([offsets[c * lat_count : (c + 1) * lat_count] for c in members])
            for members in groups
        ]
    )
    return pl.pallas_call(
        functools.partial(attend_kernel, count, heads, depth, groups, slots),
        out_shape=[jax.ShapeDtypeStruct((length, group), jnp.bfloat16)] * slots,
        in_specs=[SMEM] * 4 + [ANY, ANY] + [VMEM] * (count + 2),
        out_specs=[VMEM] * slots,
        scratch_shapes=[
            pltpu.VMEM((CORES * rows, width), jnp.float32),
            pltpu.VMEM((count, lat_count, heads * DH), jnp.bfloat16),
            pltpu.VMEM((len(groups), length, group), jnp.bfloat16),
            pltpu.VMEM((CORES * CORES, rows, depth), own.dtype),
            pltpu.SemaphoreType.DMA((CORES * CORES,)),
        ],
        compiler_params=PARAMS,
        cost_estimate=pl.CostEstimate(
            flops=8 * CORES * rows * group * len(groups) * heads * DH,
            bytes_accessed=2 * CORES * CORES * rows * depth,
            transcendentals=CORES * rows * group * len(groups) * heads,
        ),
    )(starts, firsts, slot_groups, places, own, sibling, *blocks, acc, group_offsets)


def normed_head(messages, base):
    peaks, totals = [], []
    for message in messages:
        stats = message[base + DH : base + DH + STATS, :].astype(jnp.float32)
        peaks.append(stats[0:1] + stats[1:2] + stats[2:3])
        totals.append(stats[3:4] + stats[4:5] + stats[5:6])
    top = functools.reduce(jnp.maximum, peaks)
    total, numerator = 0.0, 0.0
    for message, peak, part in zip(messages, peaks, totals):
        scale = jnp.exp(peak - top)
        total += part * scale
        numerator += message[base : base + DH, :].astype(jnp.float32) * scale
    attended = numerator / total
    mean_square = jnp.mean(attended * attended, axis=0, keepdims=True)
    return (attended * lax.rsqrt(mean_square + 1e-05)).T


def combine_kernel(heads, lanes, core_ref, *refs):
    messages, gain_ref, out_ref = refs[:-2], refs[-2], refs[-1]
    half = heads * DH
    for lane in range(lanes):
        who = core_ref[0] if lane == 0 else 1 - core_ref[0]
        for h in range(heads):
            normed = normed_head(messages[lane::lanes], h * (DH + STATS))
            place = pl.ds(pl.multiple_of(who * half, DH) + h * DH, DH)
            normed = normed * gain_ref[:, place].astype(jnp.float32)
            if lanes == 1:
                place = slice(h * DH, (h + 1) * DH)
            out_ref[:, place] = normed.astype(jnp.bfloat16)


def combine(core, messages, gain, heads, lanes):
    return pl.pallas_call(
        functools.partial(combine_kernel, heads, lanes),
        out_shape=jax.ShapeDtypeStruct((messages[0].shape[1], lanes * heads * DH), jnp.bfloat16),
        in_specs=[SMEM] + [VMEM] * (len(messages) + 1),
        out_specs=VMEM,
        compiler_params=PARAMS,
    )(core, *messages, gain)


def pack_kernel(core_ref, key_ref, value_ref, query_ref, own_ref, other_ref):
    depth, half = key_ref.shape[0], key_ref.shape[1] // CORES
    lines = query_ref.shape[0] // 2
    for out_ref, who in ((own_ref, core_ref[0]), (other_ref, 1 - core_ref[0])):
        place = pl.ds(pl.multiple_of(who * half, DH), half)
        out_ref[:depth, :half] = key_ref[:, place]
        out_ref[:depth, half:] = value_ref[:, place]
        out_ref[depth:, :half] = query_ref[:lines, place]
        out_ref[depth:, half:] = query_ref[lines:, place]


def pack(core, w_key, w_value, queries):
    depth, panel = w_key.shape
    out = jax.ShapeDtypeStruct((depth + queries.shape[0] // 2, panel), w_key.dtype)
    return pl.pallas_call(
        pack_kernel,
        out_shape=[out, out],
        in_specs=[SMEM, VMEM, VMEM, VMEM],
        out_specs=[VMEM, VMEM],
        compiler_params=PARAMS,
    )(core, w_key, w_value, queries)


def finish_kernel(n_dp, core_ref, *refs):
    normed, own_w, sibling_w = refs[:n_dp], refs[n_dp : 2 * n_dp], refs[2 * n_dp : 3 * n_dp]
    own_ref, other_ref = refs[3 * n_dp :]
    rows, width = own_ref.shape[0], own_w[0].shape[1]
    for weights, who in ((own_w, core_ref[0]), (sibling_w, 1 - core_ref[0])):
        total = jnp.dot(normed[0][...], weights[0][...], preferred_element_type=jnp.float32)
        for i in range(1, n_dp):
            total += jnp.dot(normed[i][...], weights[i][...], preferred_element_type=jnp.float32)
        total = total.astype(jnp.bfloat16)
        place = pl.ds(pl.multiple_of(who * width, DH), width)
        own_ref[:, place] = total[:rows]
        other_ref[:, place] = total[rows:]


def finish(core, normed, own_w, sibling_w):
    rows, width = normed[0].shape[0] // 2, own_w[0].shape[1]
    out = jax.ShapeDtypeStruct((rows, CORES * width), jnp.bfloat16)
    return pl.pallas_call(
        functools.partial(finish_kernel, len(normed)),
        out_shape=[out, out],
        in_specs=[SMEM] + [VMEM] * (3 * len(normed)),
        out_specs=[VMEM, VMEM],
        compiler_params=PARAMS,
    )(core, *normed, *own_w, *sibling_w)


def output_kernel(n_dp, wide, place_ref, own_ref, sibling_ref, w_ref, *refs):
    terms, (buffer, sems) = refs[:n_dp], refs[n_dp:]
    half = own_ref.shape[1]
    copies = []
    for i in range(n_dp):
        first = pl.multiple_of((place_ref[0] ^ i) * wide, DH)
        copies.append(
            pltpu.make_async_copy(w_ref.at[:, pl.ds(first, wide)], buffer.at[i], sems.at[i])
        )
        copies[-1].start()
    mine = pl.multiple_of(place_ref[1] * half, DH)
    other = pl.multiple_of((1 - place_ref[1]) * half, DH)
    for i in range(n_dp):
        copies[i].wait()
        total = jnp.dot(own_ref[...], buffer[i, pl.ds(mine, half), :], preferred_element_type=jnp.float32)
        total += jnp.dot(
            sibling_ref[...], buffer[i, pl.ds(other, half), :], preferred_element_type=jnp.float32
        )
        terms[i][...] = total.astype(jnp.bfloat16)


def output_terms(place, own, sibling, w_all, n_dp):
    wide = w_all.shape[1] // n_dp
    term = jax.ShapeDtypeStruct((own.shape[0], wide), jnp.bfloat16)
    return pl.pallas_call(
        functools.partial(output_kernel, n_dp, wide),
        out_shape=[term] * n_dp,
        in_specs=[SMEM, VMEM, VMEM, ANY],
        out_specs=[VMEM] * n_dp,
        scratch_shapes=[
            pltpu.VMEM((n_dp, w_all.shape[0], wide), w_all.dtype),
            pltpu.SemaphoreType.DMA((n_dp,)),
        ],
        compiler_params=PARAMS,
    )(place, own, sibling, w_all)


def on_device(n_dp, n_ctx, context, w_key, w_value, queries, offsets, head_gain, w_out):
    chips = n_ctx // CORES
    rows = context.shape[0]
    depth, panel = w_key.shape
    heads = panel // CORES // DH
    lat_count = queries.shape[0]
    me, mine_dp = lax.axis_index("ctx"), lax.axis_index("dp")
    chip, core = me // CORES, lax.rem(me, CORES)
    core_only = core.reshape(1)

    def across(array, bits):
        return lax.ppermute(array, "ctx", [(i, i ^ bits) for i in range(n_ctx)])

    def over_dp(array, bits):
        return lax.ppermute(array, "dp", [(d, d ^ bits) for d in range(n_dp)])

    own_part, other_part = pack(core_only, w_key, w_value, queries)
    pairs = [None] * chips
    for j in sorted(range(1, chips), key=lambda j: (j.bit_count(), -j)):
        low = j & -j
        if j == low:
            pairs[j] = (across(own_part, CORES * j), across(other_part, CORES * j + 1))
        else:
            pairs[j] = tuple(across(part, CORES * low) for part in pairs[j ^ low])
    pairs[0] = (own_part, across(other_part, 1))
    context_sibling = across(context, 1)

    places = jnp.stack(
        [(chip ^ j) * CORES + who for j in range(chips) for who in (core, 1 - core)]
    ).astype(jnp.int32)
    starts = places * depth
    blocks = [part for pair in pairs for part in pair]
    last = CORES * (chips - 1)
    acc = project(starts[:CORES], context, context_sibling, blocks[:CORES], None, depth)
    acc = project(starts[CORES:last], context, context_sibling, blocks[CORES:last], acc, depth)
    firsts = jnp.stack([me * rows, (me ^ 1) * rows]).astype(jnp.int32)
    gain = head_gain.reshape(1, panel)

    def messages_to(groups, slot_groups):
        return attend(
            starts[last:], firsts, slot_groups.astype(jnp.int32), places, context, context_sibling,
            blocks, acc, offsets, groups, heads, depth,
        )

    if chips == 4 and n_dp == chips:
        first, count = CORES, 2 * CORES
        middle = list(range(first, first + count))
        groups = tuple((c, c ^ CORES) for c in middle)
        slot_groups = jnp.clip((me ^ jnp.arange(n_ctx)) - first, 0, count - 1)
        messages = messages_to(groups, slot_groups)

        between = [(c, c ^ (3 * CORES)) for c in middle]
        ready, _ = lax.optimization_barrier((w_out, pairs[2]))
        outer = lax.ppermute(w_out, "ctx", [(c ^ CORES, c) for c in middle])
        shards = [w_out, outer, lax.ppermute(outer, "ctx", between), lax.ppermute(ready, "ctx", between)]
        own_w = []
        for i in range(n_dp):
            wanted = chip ^ mine_dp ^ i
            part = shards[0]
            for j in range(1, chips):
                part = jnp.where(wanted == j, shards[j], part)
            own_w.append(over_dp(part, i) if i else part)
        sibling_w = [across(part, 1) for part in own_w]

        arrived = [messages[0]] + [
            lax.ppermute(messages[m], "ctx", [(c ^ m, c) for c in middle]) for m in range(1, n_ctx)
        ]
        normed = combine(core_only, arrived, gain, heads, CORES)
        normed = [normed] + [over_dp(normed, i) for i in range(1, n_dp)]
        own_rows, outer_rows = finish(core_only, normed, own_w, sibling_w)
        outer_rows = lax.ppermute(outer_rows, "ctx", [(c, c ^ CORES) for c in middle])
        return jnp.where((chip == 1) | (chip == 2), own_rows, outer_rows)

    groups = tuple((CORES * z, CORES * z + 1) for z in range(chips))
    messages = messages_to(groups, chip ^ jnp.arange(chips))
    arrived = [messages[0]] + [across(messages[j], CORES * j) for j in range(1, chips)]
    normed = combine(core_only, arrived, gain, heads, 1)
    normed_own = lax.dynamic_slice_in_dim(normed, core * lat_count, lat_count)
    normed_other = lax.dynamic_slice_in_dim(normed, (1 - core) * lat_count, lat_count)
    w_all = lax.all_gather(w_out, "ctx", axis=1, tiled=True)
    terms = output_terms(
        jnp.stack([mine_dp, core]).astype(jnp.int32), normed_own, across(normed_other, 1), w_all, n_dp
    )
    total = terms[0].astype(jnp.float32)
    for i in range(1, n_dp):
        total += over_dp(terms[i], i).astype(jnp.float32)
    return total.astype(jnp.bfloat16)


def solution(mesh):
    n_dp, n_ctx = mesh.shape["dp"], mesh.shape["ctx"]
    placed = (
        P("ctx", None),
        P("ctx", "dp"),
        P("ctx", "dp"),
        P("ctx", "dp"),
        P(),
        P("dp"),
        P("dp", "ctx"),
    )

    def body(*args):
        return on_device(n_dp, n_ctx, *args)

    return jax.shard_map(
        body, mesh=mesh, in_specs=placed, out_specs=P("ctx", "dp"), check_vma=False
    )
```

```python
import functools
import math

import jax
import jax.numpy as jnp
from jax import lax
from jax.experimental import pallas as pl
from jax.experimental.pallas import tpu as pltpu
from jax.sharding import PartitionSpec as P

DH = 128
NEGATIVE = -1e30
CORES = 2
STATS = 16
VMEM = pl.BlockSpec(memory_space=pltpu.VMEM)
SMEM = pl.BlockSpec(memory_space=pltpu.SMEM)
ANY = pl.BlockSpec(memory_space=pl.ANY)
PARAMS = pltpu.CompilerParams(vmem_limit_bytes=40 * 2**20)
WIDE = pltpu.CompilerParams(vmem_limit_bytes=60 * 2**20)


def three_parts(value):
    high = value.astype(jnp.bfloat16).astype(jnp.float32)
    rest = value - high
    middle = rest.astype(jnp.bfloat16).astype(jnp.float32)
    low = (rest - middle).astype(jnp.bfloat16).astype(jnp.float32)
    return [high, middle, low]


def start_slices(starts_ref, skip, contexts, buffer, sems, count, depth):
    copies = []
    for b in range(count):
        first = pl.multiple_of(starts_ref[skip + b], DH)
        for which in range(CORES):
            slot = b * CORES + which
            copies.append(
                pltpu.make_async_copy(
                    contexts[which].at[:, pl.ds(first, depth)], buffer.at[slot],
                    sems.at[skip * CORES + slot],
                )
            )
    for copy in copies:
        copy.start()
    return copies


def add_products(copies, buffer, blocks, acc_ref, rows, depth, fresh):
    for b, block in enumerate(blocks):
        for which in range(CORES):
            slot = b * CORES + which
            if copies is not None:
                copies[slot].wait()
            product = jnp.dot(buffer[slot], block[:depth, :], preferred_element_type=jnp.float32)
            place = slice(which * rows, (which + 1) * rows)
            if fresh and b == 0:
                acc_ref[place, :] = product
            else:
                acc_ref[place, :] += product


def project_kernel(count, extra, has_acc, depth, *refs):
    starts_ref, own_ref, sibling_ref = refs[:3]
    blocks = refs[3 : 3 + count]
    acc_in = refs[3 + count] if has_acc else None
    acc_ref, later_ref, buffer, sems = refs[-4:]
    contexts = (own_ref, sibling_ref)
    copies = start_slices(starts_ref, 0, contexts, buffer, sems, count, depth)
    later = start_slices(starts_ref, count, contexts, later_ref, sems, extra, depth)
    if has_acc:
        acc_ref[...] = acc_in[...]
    add_products(copies, buffer, blocks, acc_ref, own_ref.shape[0], depth, not has_acc)
    for copy in later:
        copy.wait()


def project(starts, own, sibling, blocks, acc, depth):
    count, extra = len(blocks), starts.shape[0] - len(blocks)
    rows = own.shape[0]
    width = blocks[0].shape[1]
    operands = [starts, own, sibling, *blocks] + ([acc] if acc is not None else [])
    return pl.pallas_call(
        functools.partial(project_kernel, count, extra, acc is not None, depth),
        out_shape=[
            jax.ShapeDtypeStruct((CORES * rows, width), jnp.float32),
            jax.ShapeDtypeStruct((max(extra, 1) * CORES, rows if extra else 16, depth), own.dtype),
        ],
        in_specs=[SMEM, ANY, ANY] + [VMEM] * (len(operands) - 3),
        out_specs=[VMEM, VMEM],
        scratch_shapes=[
            pltpu.VMEM((count * CORES, rows, depth), own.dtype),
            pltpu.SemaphoreType.DMA(((count + extra) * CORES,)),
        ],
        compiler_params=PARAMS,
        cost_estimate=pl.CostEstimate(
            flops=2 * count * CORES * rows * depth * width,
            bytes_accessed=2 * count * CORES * rows * depth,
            transcendentals=0,
        ),
    )(*operands)


def attend_kernel(count, heads, depth, groups, slots, *refs):
    firsts_ref, slots_ref, places_ref, slices_ref = refs[:4]
    blocks = refs[4 : 4 + count]
    acc_in, offsets_ref = refs[4 + count : 6 + count]
    messages = refs[6 + count : 6 + count + slots]
    acc_ref, query_ref, group_ref = refs[6 + count + slots :]
    rows = slices_ref.shape[1]
    half = heads * DH
    lines = blocks[0].shape[0] - depth
    acc_ref[...] = acc_in[...]
    for b, block in enumerate(blocks):
        query_ref[places_ref[b], :lines, :] = block[depth:, :half]
        query_ref[places_ref[b], lines:, :] = block[depth:, half:]
    add_products(None, slices_ref, blocks[-CORES:], acc_ref, rows, depth, False)
    score_scale = 1.0 / math.sqrt(DH)
    line = lax.broadcasted_iota(jnp.int32, (CORES * rows, 1), 0)
    positions = jnp.where(line < rows, firsts_ref[0] + line, firsts_ref[1] + line - rows)
    for h in range(heads):
        keys = acc_ref[:, h * DH : (h + 1) * DH].astype(jnp.bfloat16)
        values = acc_ref[:, half + h * DH : half + (h + 1) * DH].T.astype(jnp.bfloat16)
        for g, members in enumerate(groups):
            query = jnp.concatenate(
                [query_ref[c, :, h * DH : (h + 1) * DH] for c in members], axis=0
            )
            scores = lax.dot_general(
                keys, query, (((1,), (1,)), ((), ())), preferred_element_type=jnp.float32
            ) * score_scale
            live = positions <= offsets_ref[g : g + 1, :]
            masked = jnp.where(live, scores, NEGATIVE)
            peak = jnp.max(masked, axis=0, keepdims=True)
            weights = jnp.where(live, jnp.exp(masked - peak), 0.0).astype(jnp.bfloat16)
            total = jnp.sum(weights.astype(jnp.float32), axis=0, keepdims=True)
            numerator = jnp.dot(values, weights, preferred_element_type=jnp.float32)
            stats = three_parts(peak) + three_parts(total)
            stats.append(jnp.zeros((STATS - len(stats), peak.shape[1]), jnp.float32))
            base = h * (DH + STATS)
            group_ref[g, base : base + DH, :] = numerator.astype(jnp.bfloat16)
            group_ref[g, base + DH : base + DH + STATS, :] = jnp.concatenate(
                stats, axis=0
            ).astype(jnp.bfloat16)
    for m in range(slots):
        messages[m][...] = group_ref[slots_ref[m]]


def attend(firsts, slot_groups, places, slices, blocks, acc, offsets, groups, heads, depth):
    count, slots = len(blocks), slot_groups.shape[0]
    rows, width = slices.shape[1], blocks[0].shape[1]
    lat_count = 2 * (blocks[0].shape[0] - depth)
    group = lat_count * len(groups[0])
    length = heads * (DH + STATS)
    group_offsets = jnp.stack(
        [
            jnp.concatenate([offsets[c * lat_count : (c + 1) * lat_count] for c in members])
            for members in groups
        ]
    )
    return pl.pallas_call(
        functools.partial(attend_kernel, count, heads, depth, groups, slots),
        out_shape=[jax.ShapeDtypeStruct((length, group), jnp.bfloat16)] * slots,
        in_specs=[SMEM] * 3 + [VMEM] * (count + 3),
        out_specs=[VMEM] * slots,
        scratch_shapes=[
            pltpu.VMEM((CORES * rows, width), jnp.float32),
            pltpu.VMEM((count, lat_count, heads * DH), jnp.bfloat16),
            pltpu.VMEM((len(groups), length, group), jnp.bfloat16),
        ],
        compiler_params=PARAMS,
        cost_estimate=pl.CostEstimate(
            flops=8 * CORES * rows * group * len(groups) * heads * DH,
            bytes_accessed=2 * CORES * CORES * rows * depth,
            transcendentals=CORES * rows * group * len(groups) * heads,
        ),
    )(firsts, slot_groups, places, slices, *blocks, acc, group_offsets)


def normed_head(messages, base):
    peaks, totals = [], []
    for message in messages:
        stats = message[base + DH : base + DH + STATS, :].astype(jnp.float32)
        peaks.append(stats[0:1] + stats[1:2] + stats[2:3])
        totals.append(stats[3:4] + stats[4:5] + stats[5:6])
    top = functools.reduce(jnp.maximum, peaks)
    total, numerator = 0.0, 0.0
    for message, peak, part in zip(messages, peaks, totals):
        scale = jnp.exp(peak - top)
        total += part * scale
        numerator += message[base : base + DH, :].astype(jnp.float32) * scale
    attended = numerator / total
    mean_square = jnp.mean(attended * attended, axis=0, keepdims=True)
    return (attended * lax.rsqrt(mean_square + 1e-05)).T


def combine_kernel(heads, core_ref, *refs):
    messages, gain_ref, out_ref = refs[:-2], refs[-2], refs[-1]
    half = out_ref.shape[1]
    for h in range(heads):
        place = pl.ds(pl.multiple_of(core_ref[0] * half, DH) + h * DH, DH)
        normed = normed_head(messages, h * (DH + STATS))
        normed = normed * gain_ref[:, place].astype(jnp.float32)
        out_ref[:, h * DH : (h + 1) * DH] = normed.astype(jnp.bfloat16)


def combine(core, messages, gain, heads):
    return pl.pallas_call(
        functools.partial(combine_kernel, heads),
        out_shape=jax.ShapeDtypeStruct((messages[0].shape[1], heads * DH), jnp.bfloat16),
        in_specs=[SMEM] + [VMEM] * (len(messages) + 1),
        out_specs=VMEM,
        compiler_params=PARAMS,
    )(core, *messages, gain)


def pack_kernel(core_ref, key_ref, value_ref, query_ref, own_ref, other_ref, sems):
    depth, half = key_ref.shape[0], key_ref.shape[1] // CORES
    lines = query_ref.shape[0] // 2
    copies = []
    for out_ref, who in ((own_ref, core_ref[0]), (other_ref, 1 - core_ref[0])):
        place = pl.ds(pl.multiple_of(who * half, DH), half)
        for source, target in (
            (key_ref.at[:, place], out_ref.at[pl.ds(0, depth), pl.ds(0, half)]),
            (value_ref.at[:, place], out_ref.at[pl.ds(0, depth), pl.ds(half, half)]),
            (query_ref.at[pl.ds(0, lines), place], out_ref.at[pl.ds(depth, lines), pl.ds(0, half)]),
            (query_ref.at[pl.ds(lines, lines), place], out_ref.at[pl.ds(depth, lines), pl.ds(half, half)]),
        ):
            copies.append(pltpu.make_async_copy(source, target, sems.at[len(copies)]))
            copies[-1].start()
    for copy in copies:
        copy.wait()


def pack(core, w_key, w_value, queries):
    depth, panel = w_key.shape
    out = jax.ShapeDtypeStruct((depth + queries.shape[0] // 2, panel), w_key.dtype)
    return pl.pallas_call(
        pack_kernel,
        out_shape=[out, out],
        in_specs=[SMEM, ANY, ANY, ANY],
        out_specs=[VMEM, VMEM],
        scratch_shapes=[pltpu.SemaphoreType.DMA((8,))],
        compiler_params=WIDE,
    )(core, w_key, w_value, queries)


def output_kernel(place_ref, own_ref, sibling_ref, *refs):
    chips = (len(refs) - 1) // 2
    weights, terms, result = refs[:chips], refs[chips:-1], refs[-1]
    half = own_ref.shape[1]
    mine = pl.ds(pl.multiple_of(place_ref[1] * half, DH), half)
    other = pl.ds(pl.multiple_of((1 - place_ref[1]) * half, DH), half)
    own, sibling = own_ref[...], sibling_ref[...]
    for j, w_ref in enumerate(weights):
        total = jnp.dot(own, w_ref[mine, :], preferred_element_type=jnp.float32)
        total += jnp.dot(sibling, w_ref[other, :], preferred_element_type=jnp.float32)
        result[j] = total.astype(jnp.bfloat16)
    for i, term in enumerate(terms):
        term[...] = result[place_ref[0] ^ i]


def output_terms(place, own, sibling, weights):
    chips, shape = len(weights), (own.shape[0], weights[0].shape[1])
    return pl.pallas_call(
        output_kernel,
        out_shape=[jax.ShapeDtypeStruct(shape, jnp.bfloat16)] * chips,
        in_specs=[SMEM] + [VMEM] * (2 + chips),
        out_specs=[VMEM] * chips,
        scratch_shapes=[pltpu.VMEM((chips, *shape), jnp.bfloat16)],
        compiler_params=PARAMS,
    )(place, own, sibling, *weights)


def add_kernel(core_ref, *refs):
    terms, (own_ref, other_ref) = refs[:-2], refs[-2:]
    count = own_ref.shape[0]
    for out_ref, who in ((own_ref, core_ref[0]), (other_ref, 1 - core_ref[0])):
        lines = pl.ds(pl.multiple_of(who * count, count), count)
        total = terms[0][lines, :].astype(jnp.float32)
        for term in terms[1:]:
            total += term[lines, :].astype(jnp.float32)
        out_ref[...] = total.astype(jnp.bfloat16)


def add_terms(core, terms):
    rows, width = terms[0].shape
    out = jax.ShapeDtypeStruct((rows // CORES, width), jnp.bfloat16)
    return pl.pallas_call(
        add_kernel,
        out_shape=[out, out],
        in_specs=[SMEM] + [VMEM] * len(terms),
        out_specs=[VMEM, VMEM],
        compiler_params=PARAMS,
    )(core, *terms)


def on_device(n_dp, n_ctx, context, w_key, w_value, queries, offsets, head_gain, w_out):
    chips = n_ctx // CORES
    rows = context.shape[0]
    depth, panel = w_key.shape
    heads = panel // CORES // DH
    lat_count = queries.shape[0]
    me, mine_dp = lax.axis_index("ctx"), lax.axis_index("dp")
    chip, core = me // CORES, lax.rem(me, CORES)
    core_only = core.reshape(1)

    def across(array, bits):
        return lax.ppermute(array, "ctx", [(i, i ^ bits) for i in range(n_ctx)])

    def over_dp(array, bits):
        return lax.ppermute(array, "dp", [(d, d ^ bits) for d in range(n_dp)])

    def after(array, *others):
        return lax.optimization_barrier((array, others))[0]

    near_first = sorted(range(1, chips), key=lambda j: (j.bit_count(), -j))
    own_part, other_part = pack(core_only, w_key, w_value, queries)
    pairs = [None] * chips
    for j in near_first:
        low = j & -j
        if j == low:
            pairs[j] = (across(own_part, CORES * j), across(other_part, CORES * j + 1))
        else:
            pairs[j] = tuple(across(part, CORES * low) for part in pairs[j ^ low])
    context_sibling = across(context, 1)
    pairs[0] = (own_part, across(after(other_part, pairs[1], pairs[chips // 2]), 1))

    places = jnp.stack(
        [(chip ^ j) * CORES + who for j in range(chips) for who in (core, 1 - core)]
    ).astype(jnp.int32)
    starts = places * depth
    blocks = [part for pair in pairs for part in pair]
    last = CORES * (chips - 1)
    acc, _ = project(starts[:CORES], context, context_sibling, blocks[:CORES], None, depth)
    acc, slices = project(
        starts[CORES:], context, context_sibling, blocks[CORES:last], acc, depth
    )
    firsts = jnp.stack([me * rows, (me ^ 1) * rows]).astype(jnp.int32)
    groups = tuple((CORES * z, CORES * z + 1) for z in range(chips))
    slot_groups = (chip ^ jnp.arange(chips)).astype(jnp.int32)
    messages = attend(
        firsts, slot_groups, places, slices, blocks, acc, offsets, groups, heads, depth
    )
    arrived = [messages[0]] + [across(messages[j], CORES * j) for j in range(1, chips)]
    normed = combine(core_only, arrived, head_gain.reshape(1, panel), heads)

    shards = [after(w_out, *pairs[-1], acc)] + [None] * (chips - 1)
    for j in near_first:
        low = j & -j
        shard = shards[j ^ low]
        shards[j] = across(shard if j == low else after(shard, normed), CORES * low)
    terms = output_terms(
        jnp.stack([mine_dp ^ chip, core]).astype(jnp.int32), normed, across(normed, 1), shards
    )
    terms = [terms[0]] + [over_dp(terms[i], i) for i in range(1, n_dp)]
    mine, other = add_terms(core_only, terms)
    theirs = across(other, 1)
    return jnp.where(
        core == 0, jnp.concatenate([mine, theirs], axis=1), jnp.concatenate([theirs, mine], axis=1)
    )


def solution(mesh):
    n_dp, n_ctx = mesh.shape["dp"], mesh.shape["ctx"]
    placed = (
        P("ctx", None),
        P("ctx", "dp"),
        P("ctx", "dp"),
        P("ctx", "dp"),
        P(),
        P("dp"),
        P("dp", "ctx"),
    )

    def body(*args):
        return on_device(n_dp, n_ctx, *args)

    return jax.shard_map(
        body, mesh=mesh, in_specs=placed, out_specs=P("ctx", "dp"), check_vma=False
    )
```

```python
import functools
import math

import jax
import jax.numpy as jnp
from jax import lax
from jax.experimental import pallas as pl
from jax.experimental.pallas import tpu as pltpu
from jax.sharding import PartitionSpec as P

DH = 128
NEGATIVE = -1e30
CORES = 2
STATS = 16
VMEM = pl.BlockSpec(memory_space=pltpu.VMEM)
SMEM = pl.BlockSpec(memory_space=pltpu.SMEM)
ANY = pl.BlockSpec(memory_space=pl.ANY)
PARAMS = pltpu.CompilerParams(vmem_limit_bytes=40 * 2**20)
WIDE = pltpu.CompilerParams(vmem_limit_bytes=60 * 2**20)


def three_parts(value):
    high = value.astype(jnp.bfloat16).astype(jnp.float32)
    rest = value - high
    middle = rest.astype(jnp.bfloat16).astype(jnp.float32)
    low = (rest - middle).astype(jnp.bfloat16).astype(jnp.float32)
    return [high, middle, low]


def start_slices(starts_ref, skip, contexts, buffer, sems, count, depth):
    copies = []
    for b in range(count):
        first = pl.multiple_of(starts_ref[skip + b], DH)
        for which in range(CORES):
            slot = b * CORES + which
            copies.append(
                pltpu.make_async_copy(
                    contexts[which].at[:, pl.ds(first, depth)], buffer.at[slot],
                    sems.at[skip * CORES + slot],
                )
            )
    for copy in copies:
        copy.start()
    return copies


def add_products(copies, buffer, blocks, acc_ref, rows, depth, fresh):
    for b, block in enumerate(blocks):
        for which in range(CORES):
            slot = b * CORES + which
            if copies is not None:
                copies[slot].wait()
            product = jnp.dot(buffer[slot], block[:depth, :], preferred_element_type=jnp.float32)
            place = slice(which * rows, (which + 1) * rows)
            if fresh and b == 0:
                acc_ref[place, :] = product
            else:
                acc_ref[place, :] += product


def project_kernel(count, extra, has_acc, depth, *refs):
    starts_ref, own_ref, sibling_ref = refs[:3]
    blocks = refs[3 : 3 + count]
    acc_in = refs[3 + count] if has_acc else None
    acc_ref, later_ref, buffer, sems = refs[-4:]
    contexts = (own_ref, sibling_ref)
    copies = start_slices(starts_ref, 0, contexts, buffer, sems, count, depth)
    later = start_slices(starts_ref, count, contexts, later_ref, sems, extra, depth)
    if has_acc:
        acc_ref[...] = acc_in[...]
    add_products(copies, buffer, blocks, acc_ref, own_ref.shape[0], depth, not has_acc)
    for copy in later:
        copy.wait()


def project(starts, own, sibling, blocks, acc, depth):
    count, extra = len(blocks), starts.shape[0] - len(blocks)
    rows = own.shape[0]
    width = blocks[0].shape[1]
    operands = [starts, own, sibling, *blocks] + ([acc] if acc is not None else [])
    return pl.pallas_call(
        functools.partial(project_kernel, count, extra, acc is not None, depth),
        out_shape=[
            jax.ShapeDtypeStruct((CORES * rows, width), jnp.float32),
            jax.ShapeDtypeStruct((max(extra, 1) * CORES, rows if extra else 16, depth), own.dtype),
        ],
        in_specs=[SMEM, ANY, ANY] + [VMEM] * (len(operands) - 3),
        out_specs=[VMEM, VMEM],
        scratch_shapes=[
            pltpu.VMEM((count * CORES, rows, depth), own.dtype),
            pltpu.SemaphoreType.DMA(((count + extra) * CORES,)),
        ],
        compiler_params=PARAMS,
        cost_estimate=pl.CostEstimate(
            flops=2 * count * CORES * rows * depth * width,
            bytes_accessed=2 * count * CORES * rows * depth,
            transcendentals=0,
        ),
    )(*operands)


def attend_kernel(count, heads, depth, groups, slots, *refs):
    firsts_ref, slots_ref, places_ref, slices_ref = refs[:4]
    blocks = refs[4 : 4 + count]
    acc_in, offsets_ref = refs[4 + count : 6 + count]
    messages = refs[6 + count : 6 + count + slots]
    acc_ref, query_ref, group_ref = refs[6 + count + slots :]
    rows = slices_ref.shape[1]
    half = heads * DH
    lines = blocks[0].shape[0] - depth
    acc_ref[...] = acc_in[...]
    for b, block in enumerate(blocks):
        query_ref[places_ref[b], :lines, :] = block[depth:, :half]
        query_ref[places_ref[b], lines:, :] = block[depth:, half:]
    add_products(None, slices_ref, blocks[-CORES:], acc_ref, rows, depth, False)
    score_scale = 1.0 / math.sqrt(DH)
    line = lax.broadcasted_iota(jnp.int32, (CORES * rows, 1), 0)
    positions = jnp.where(line < rows, firsts_ref[0] + line, firsts_ref[1] + line - rows)
    for h in range(heads):
        keys = acc_ref[:, h * DH : (h + 1) * DH].astype(jnp.bfloat16)
        values = acc_ref[:, half + h * DH : half + (h + 1) * DH].T.astype(jnp.bfloat16)
        for g, members in enumerate(groups):
            query = jnp.concatenate(
                [query_ref[c, :, h * DH : (h + 1) * DH] for c in members], axis=0
            )
            scores = lax.dot_general(
                keys, query, (((1,), (1,)), ((), ())), preferred_element_type=jnp.float32
            ) * score_scale
            live = positions <= offsets_ref[g : g + 1, :]
            masked = jnp.where(live, scores, NEGATIVE)
            peak = jnp.max(masked, axis=0, keepdims=True)
            weights = jnp.where(live, jnp.exp(masked - peak), 0.0).astype(jnp.bfloat16)
            total = jnp.sum(weights.astype(jnp.float32), axis=0, keepdims=True)
            numerator = jnp.dot(values, weights, preferred_element_type=jnp.float32)
            stats = three_parts(peak) + three_parts(total)
            stats.append(jnp.zeros((STATS - len(stats), peak.shape[1]), jnp.float32))
            base = h * (DH + STATS)
            group_ref[g, base : base + DH, :] = numerator.astype(jnp.bfloat16)
            group_ref[g, base + DH : base + DH + STATS, :] = jnp.concatenate(
                stats, axis=0
            ).astype(jnp.bfloat16)
    for m in range(slots):
        messages[m][...] = group_ref[slots_ref[m]]


def attend(firsts, slot_groups, places, slices, blocks, acc, offsets, groups, heads, depth):
    count, slots = len(blocks), slot_groups.shape[0]
    rows, width = slices.shape[1], blocks[0].shape[1]
    lat_count = 2 * (blocks[0].shape[0] - depth)
    group = lat_count * len(groups[0])
    length = heads * (DH + STATS)
    group_offsets = jnp.stack(
        [
            jnp.concatenate([offsets[c * lat_count : (c + 1) * lat_count] for c in members])
            for members in groups
        ]
    )
    return pl.pallas_call(
        functools.partial(attend_kernel, count, heads, depth, groups, slots),
        out_shape=[jax.ShapeDtypeStruct((length, group), jnp.bfloat16)] * slots,
        in_specs=[SMEM] * 3 + [VMEM] * (count + 3),
        out_specs=[VMEM] * slots,
        scratch_shapes=[
            pltpu.VMEM((CORES * rows, width), jnp.float32),
            pltpu.VMEM((count, lat_count, heads * DH), jnp.bfloat16),
            pltpu.VMEM((len(groups), length, group), jnp.bfloat16),
        ],
        compiler_params=PARAMS,
        cost_estimate=pl.CostEstimate(
            flops=8 * CORES * rows * group * len(groups) * heads * DH,
            bytes_accessed=2 * CORES * CORES * rows * depth,
            transcendentals=CORES * rows * group * len(groups) * heads,
        ),
    )(firsts, slot_groups, places, slices, *blocks, acc, group_offsets)


def normed_head(messages, base):
    peaks, totals = [], []
    for message in messages:
        stats = message[base + DH : base + DH + STATS, :].astype(jnp.float32)
        peaks.append(stats[0:1] + stats[1:2] + stats[2:3])
        totals.append(stats[3:4] + stats[4:5] + stats[5:6])
    top = functools.reduce(jnp.maximum, peaks)
    total, numerator = 0.0, 0.0
    for message, peak, part in zip(messages, peaks, totals):
        scale = jnp.exp(peak - top)
        total += part * scale
        numerator += message[base : base + DH, :].astype(jnp.float32) * scale
    attended = numerator / total
    mean_square = jnp.mean(attended * attended, axis=0, keepdims=True)
    return (attended * lax.rsqrt(mean_square + 1e-05)).T


def combine_kernel(heads, core_ref, *refs):
    messages, gain_ref, out_ref = refs[:-2], refs[-2], refs[-1]
    half = out_ref.shape[1]
    for h in range(heads):
        place = pl.ds(pl.multiple_of(core_ref[0] * half, DH) + h * DH, DH)
        normed = normed_head(messages, h * (DH + STATS))
        normed = normed * gain_ref[:, place].astype(jnp.float32)
        out_ref[:, h * DH : (h + 1) * DH] = normed.astype(jnp.bfloat16)


def combine(core, messages, gain, heads):
    return pl.pallas_call(
        functools.partial(combine_kernel, heads),
        out_shape=jax.ShapeDtypeStruct((messages[0].shape[1], heads * DH), jnp.bfloat16),
        in_specs=[SMEM] + [VMEM] * (len(messages) + 1),
        out_specs=VMEM,
        compiler_params=PARAMS,
    )(core, *messages, gain)


def pack_kernel(core_ref, key_ref, value_ref, query_ref, own_ref, other_ref, sems):
    depth, half = key_ref.shape[0], key_ref.shape[1] // CORES
    lines = query_ref.shape[0] // 2
    copies = []
    for out_ref, who in ((own_ref, core_ref[0]), (other_ref, 1 - core_ref[0])):
        place = pl.ds(pl.multiple_of(who * half, DH), half)
        for source, target in (
            (key_ref.at[:, place], out_ref.at[pl.ds(0, depth), pl.ds(0, half)]),
            (value_ref.at[:, place], out_ref.at[pl.ds(0, depth), pl.ds(half, half)]),
            (query_ref.at[pl.ds(0, lines), place], out_ref.at[pl.ds(depth, lines), pl.ds(0, half)]),
            (query_ref.at[pl.ds(lines, lines), place], out_ref.at[pl.ds(depth, lines), pl.ds(half, half)]),
        ):
            copies.append(pltpu.make_async_copy(source, target, sems.at[len(copies)]))
            copies[-1].start()
    for copy in copies:
        copy.wait()


def pack(core, w_key, w_value, queries):
    depth, panel = w_key.shape
    out = jax.ShapeDtypeStruct((depth + queries.shape[0] // 2, panel), w_key.dtype)
    return pl.pallas_call(
        pack_kernel,
        out_shape=[out, out],
        in_specs=[SMEM, ANY, ANY, ANY],
        out_specs=[ANY, ANY],
        scratch_shapes=[pltpu.SemaphoreType.DMA((8,))],
        compiler_params=WIDE,
    )(core, w_key, w_value, queries)


def output_kernel(place_ref, own_ref, sibling_ref, *refs):
    chips = (len(refs) - 1) // 2
    weights, terms, result = refs[:chips], refs[chips:-1], refs[-1]
    half = own_ref.shape[1]
    mine = pl.ds(pl.multiple_of(place_ref[1] * half, DH), half)
    other = pl.ds(pl.multiple_of((1 - place_ref[1]) * half, DH), half)
    own, sibling = own_ref[...], sibling_ref[...]
    for j, w_ref in enumerate(weights):
        total = jnp.dot(own, w_ref[mine, :], preferred_element_type=jnp.float32)
        total += jnp.dot(sibling, w_ref[other, :], preferred_element_type=jnp.float32)
        result[j] = total.astype(jnp.bfloat16)
    for i, term in enumerate(terms):
        term[...] = result[place_ref[0] ^ i]


def output_terms(place, own, sibling, weights):
    chips, shape = len(weights), (own.shape[0], weights[0].shape[1])
    return pl.pallas_call(
        output_kernel,
        out_shape=[jax.ShapeDtypeStruct(shape, jnp.bfloat16)] * chips,
        in_specs=[SMEM] + [VMEM] * (2 + chips),
        out_specs=[VMEM] * chips,
        scratch_shapes=[pltpu.VMEM((chips, *shape), jnp.bfloat16)],
        compiler_params=PARAMS,
    )(place, own, sibling, *weights)


def add_kernel(core_ref, *refs):
    terms, (own_ref, other_ref) = refs[:-2], refs[-2:]
    count = own_ref.shape[0]
    for out_ref, who in ((own_ref, core_ref[0]), (other_ref, 1 - core_ref[0])):
        lines = pl.ds(pl.multiple_of(who * count, count), count)
        total = terms[0][lines, :].astype(jnp.float32)
        for term in terms[1:]:
            total += term[lines, :].astype(jnp.float32)
        out_ref[...] = total.astype(jnp.bfloat16)


def add_terms(core, terms):
    rows, width = terms[0].shape
    out = jax.ShapeDtypeStruct((rows // CORES, width), jnp.bfloat16)
    return pl.pallas_call(
        add_kernel,
        out_shape=[out, out],
        in_specs=[SMEM] + [VMEM] * len(terms),
        out_specs=[VMEM, VMEM],
        compiler_params=PARAMS,
    )(core, *terms)


def on_device(n_dp, n_ctx, context, w_key, w_value, queries, offsets, head_gain, w_out):
    chips = n_ctx // CORES
    rows = context.shape[0]
    depth, panel = w_key.shape
    heads = panel // CORES // DH
    lat_count = queries.shape[0]
    me, mine_dp = lax.axis_index("ctx"), lax.axis_index("dp")
    chip, core = me // CORES, lax.rem(me, CORES)
    core_only = core.reshape(1)

    def across(array, bits):
        return lax.ppermute(array, "ctx", [(i, i ^ bits) for i in range(n_ctx)])

    def over_dp(array, bits):
        return lax.ppermute(array, "dp", [(d, d ^ bits) for d in range(n_dp)])

    def after(array, *others):
        return lax.optimization_barrier((array, others))[0]

    near_first = sorted(range(1, chips), key=lambda j: (j.bit_count(), -j))
    own_part, other_part = pack(core_only, w_key, w_value, queries)
    pairs = [None] * chips
    for j in near_first:
        low = j & -j
        if j == low:
            pairs[j] = (across(own_part, CORES * j), across(other_part, CORES * j + 1))
        else:
            pairs[j] = tuple(across(part, CORES * low) for part in pairs[j ^ low])
    context_sibling = across(after(context, own_part), 1)
    pairs[0] = (own_part, across(after(other_part, pairs[1], pairs[chips // 2]), 1))

    places = jnp.stack(
        [(chip ^ j) * CORES + who for j in range(chips) for who in (core, 1 - core)]
    ).astype(jnp.int32)
    starts = places * depth
    blocks = [part for pair in pairs for part in pair]
    last = CORES * (chips - 1)
    first_acc, _ = project(starts[:CORES], context, context_sibling, blocks[:CORES], None, depth)
    acc, slices = project(
        starts[CORES:], context, context_sibling, blocks[CORES:last], first_acc, depth
    )
    firsts = jnp.stack([me * rows, (me ^ 1) * rows]).astype(jnp.int32)
    groups = tuple((CORES * z, CORES * z + 1) for z in range(chips))
    slot_groups = (chip ^ jnp.arange(chips)).astype(jnp.int32)
    messages = attend(
        firsts, slot_groups, places, slices, blocks, acc, offsets, groups, heads, depth
    )
    arrived = [messages[0]] + [across(messages[j], CORES * j) for j in range(1, chips)]
    shards = [after(w_out, acc, *pairs[-1])] + [None] * (chips - 1)
    for j in near_first:
        low = j & -j
        shard = shards[j ^ low]
        shards[j] = across(shard if j == low else after(shard, *arrived[1:]), CORES * low)
    normed = combine(core_only, arrived, head_gain.reshape(1, panel), heads)

    terms = output_terms(
        jnp.stack([mine_dp ^ chip, core]).astype(jnp.int32), normed, across(normed, 1), shards
    )
    terms = [terms[0]] + [over_dp(terms[i], i) for i in range(1, n_dp)]
    mine, other = add_terms(core_only, terms)
    theirs = across(other, 1)
    return jnp.where(
        core == 0, jnp.concatenate([mine, theirs], axis=1), jnp.concatenate([theirs, mine], axis=1)
    )


def solution(mesh):
    n_dp, n_ctx = mesh.shape["dp"], mesh.shape["ctx"]
    placed = (
        P("ctx", None),
        P("ctx", "dp"),
        P("ctx", "dp"),
        P("ctx", "dp"),
        P(),
        P("dp"),
        P("dp", "ctx"),
    )

    def body(*args):
        return on_device(n_dp, n_ctx, *args)

    return jax.shard_map(
        body, mesh=mesh, in_specs=placed, out_specs=P("ctx", "dp"), check_vma=False
    )
```

```python
import functools
import math

import jax
import jax.numpy as jnp
from jax import lax
from jax.experimental import pallas as pl
from jax.experimental.pallas import tpu as pltpu
from jax.sharding import PartitionSpec as P

DH = 128
NEGATIVE = -1e30
CORES = 2
STATS = 16
VMEM = pl.BlockSpec(memory_space=pltpu.VMEM)
SMEM = pl.BlockSpec(memory_space=pltpu.SMEM)
ANY = pl.BlockSpec(memory_space=pl.ANY)
PARAMS = pltpu.CompilerParams(vmem_limit_bytes=40 * 2**20)
WIDE = pltpu.CompilerParams(vmem_limit_bytes=60 * 2**20)


def three_parts(value):
    high = value.astype(jnp.bfloat16).astype(jnp.float32)
    rest = value - high
    middle = rest.astype(jnp.bfloat16).astype(jnp.float32)
    low = (rest - middle).astype(jnp.bfloat16).astype(jnp.float32)
    return [high, middle, low]


def start_slices(starts_ref, skip, contexts, buffer, sems, count, depth):
    copies = []
    for b in range(count):
        first = pl.multiple_of(starts_ref[skip + b], DH)
        for which in range(CORES):
            slot = b * CORES + which
            copies.append(
                pltpu.make_async_copy(
                    contexts[which].at[:, pl.ds(first, depth)], buffer.at[slot],
                    sems.at[skip * CORES + slot],
                )
            )
    for copy in copies:
        copy.start()
    return copies


def add_products(copies, buffer, blocks, acc_ref, rows, depth, fresh):
    for b, block in enumerate(blocks):
        for which in range(CORES):
            slot = b * CORES + which
            if copies is not None:
                copies[slot].wait()
            product = jnp.dot(buffer[slot], block[:depth, :], preferred_element_type=jnp.float32)
            place = slice(which * rows, (which + 1) * rows)
            if fresh and b == 0:
                acc_ref[place, :] = product
            else:
                acc_ref[place, :] += product


def project_kernel(count, extra, has_acc, depth, *refs):
    starts_ref, own_ref, sibling_ref = refs[:3]
    blocks = refs[3 : 3 + count]
    acc_in = refs[3 + count] if has_acc else None
    acc_ref, later_ref, buffer, sems = refs[-4:]
    contexts = (own_ref, sibling_ref)
    copies = start_slices(starts_ref, 0, contexts, buffer, sems, count, depth)
    later = start_slices(starts_ref, count, contexts, later_ref, sems, extra, depth)
    if has_acc:
        acc_ref[...] = acc_in[...]
    add_products(copies, buffer, blocks, acc_ref, own_ref.shape[0], depth, not has_acc)
    for copy in later:
        copy.wait()


def project(starts, own, sibling, blocks, acc, depth):
    count, extra = len(blocks), starts.shape[0] - len(blocks)
    rows = own.shape[0]
    width = blocks[0].shape[1]
    operands = [starts, own, sibling, *blocks] + ([acc] if acc is not None else [])
    return pl.pallas_call(
        functools.partial(project_kernel, count, extra, acc is not None, depth),
        out_shape=[
            jax.ShapeDtypeStruct((CORES * rows, width), jnp.float32),
            jax.ShapeDtypeStruct((max(extra, 1) * CORES, rows if extra else 16, depth), own.dtype),
        ],
        in_specs=[SMEM, ANY, ANY] + [VMEM] * (len(operands) - 3),
        out_specs=[VMEM, VMEM],
        scratch_shapes=[
            pltpu.VMEM((count * CORES, rows, depth), own.dtype),
            pltpu.SemaphoreType.DMA(((count + extra) * CORES,)),
        ],
        compiler_params=PARAMS,
        cost_estimate=pl.CostEstimate(
            flops=2 * count * CORES * rows * depth * width,
            bytes_accessed=2 * count * CORES * rows * depth,
            transcendentals=0,
        ),
    )(*operands)


def attend_kernel(count, heads, depth, groups, slots, *refs):
    firsts_ref, slots_ref, places_ref, slices_ref = refs[:4]
    blocks = refs[4 : 4 + count]
    acc_in, offsets_ref = refs[4 + count : 6 + count]
    messages = refs[6 + count : 6 + count + slots]
    acc_ref, query_ref, group_ref = refs[6 + count + slots :]
    rows = slices_ref.shape[1]
    half = heads * DH
    lines = blocks[0].shape[0] - depth
    acc_ref[...] = acc_in[...]
    for b, block in enumerate(blocks):
        query_ref[places_ref[b], :lines, :] = block[depth:, :half]
        query_ref[places_ref[b], lines:, :] = block[depth:, half:]
    add_products(None, slices_ref, blocks[-CORES:], acc_ref, rows, depth, False)
    score_scale = 1.0 / math.sqrt(DH)
    line = lax.broadcasted_iota(jnp.int32, (CORES * rows, 1), 0)
    positions = jnp.where(line < rows, firsts_ref[0] + line, firsts_ref[1] + line - rows)
    for h in range(heads):
        keys = acc_ref[:, h * DH : (h + 1) * DH].astype(jnp.bfloat16)
        values = acc_ref[:, half + h * DH : half + (h + 1) * DH].T.astype(jnp.bfloat16)
        for g, members in enumerate(groups):
            query = jnp.concatenate(
                [query_ref[c, :, h * DH : (h + 1) * DH] for c in members], axis=0
            )
            scores = lax.dot_general(
                keys, query, (((1,), (1,)), ((), ())), preferred_element_type=jnp.float32
            ) * score_scale
            live = positions <= offsets_ref[g : g + 1, :]
            masked = jnp.where(live, scores, NEGATIVE)
            peak = jnp.max(masked, axis=0, keepdims=True)
            weights = jnp.where(live, jnp.exp(masked - peak), 0.0).astype(jnp.bfloat16)
            total = jnp.sum(weights.astype(jnp.float32), axis=0, keepdims=True)
            numerator = jnp.dot(values, weights, preferred_element_type=jnp.float32)
            stats = three_parts(peak) + three_parts(total)
            stats.append(jnp.zeros((STATS - len(stats), peak.shape[1]), jnp.float32))
            base = h * (DH + STATS)
            group_ref[g, base : base + DH, :] = numerator.astype(jnp.bfloat16)
            group_ref[g, base + DH : base + DH + STATS, :] = jnp.concatenate(
                stats, axis=0
            ).astype(jnp.bfloat16)
    for m in range(slots):
        messages[m][...] = group_ref[slots_ref[m]]


def attend(firsts, slot_groups, places, slices, blocks, acc, offsets, groups, heads, depth):
    count, slots = len(blocks), slot_groups.shape[0]
    rows, width = slices.shape[1], blocks[0].shape[1]
    lat_count = 2 * (blocks[0].shape[0] - depth)
    group = lat_count * len(groups[0])
    length = heads * (DH + STATS)
    group_offsets = jnp.stack(
        [
            jnp.concatenate([offsets[c * lat_count : (c + 1) * lat_count] for c in members])
            for members in groups
        ]
    )
    return pl.pallas_call(
        functools.partial(attend_kernel, count, heads, depth, groups, slots),
        out_shape=[jax.ShapeDtypeStruct((length, group), jnp.bfloat16)] * slots,
        in_specs=[SMEM] * 3 + [VMEM] * (count + 3),
        out_specs=[VMEM] * slots,
        scratch_shapes=[
            pltpu.VMEM((CORES * rows, width), jnp.float32),
            pltpu.VMEM((count, lat_count, heads * DH), jnp.bfloat16),
            pltpu.VMEM((len(groups), length, group), jnp.bfloat16),
        ],
        compiler_params=PARAMS,
        cost_estimate=pl.CostEstimate(
            flops=8 * CORES * rows * group * len(groups) * heads * DH,
            bytes_accessed=2 * CORES * CORES * rows * depth,
            transcendentals=CORES * rows * group * len(groups) * heads,
        ),
    )(firsts, slot_groups, places, slices, *blocks, acc, group_offsets)


def normed_head(messages, base):
    peaks, totals = [], []
    for message in messages:
        stats = message[base + DH : base + DH + STATS, :].astype(jnp.float32)
        peaks.append(stats[0:1] + stats[1:2] + stats[2:3])
        totals.append(stats[3:4] + stats[4:5] + stats[5:6])
    top = functools.reduce(jnp.maximum, peaks)
    total, numerator = 0.0, 0.0
    for message, peak, part in zip(messages, peaks, totals):
        scale = jnp.exp(peak - top)
        total += part * scale
        numerator += message[base : base + DH, :].astype(jnp.float32) * scale
    attended = numerator / total
    mean_square = jnp.mean(attended * attended, axis=0, keepdims=True)
    return (attended * lax.rsqrt(mean_square + 1e-05)).T


def combine_kernel(heads, core_ref, *refs):
    messages, gain_ref, out_ref = refs[:-2], refs[-2], refs[-1]
    half = out_ref.shape[1]
    for h in range(heads):
        place = pl.ds(pl.multiple_of(core_ref[0] * half, DH) + h * DH, DH)
        normed = normed_head(messages, h * (DH + STATS))
        normed = normed * gain_ref[:, place].astype(jnp.float32)
        out_ref[:, h * DH : (h + 1) * DH] = normed.astype(jnp.bfloat16)


def combine(core, messages, gain, heads):
    return pl.pallas_call(
        functools.partial(combine_kernel, heads),
        out_shape=jax.ShapeDtypeStruct((messages[0].shape[1], heads * DH), jnp.bfloat16),
        in_specs=[SMEM] + [VMEM] * (len(messages) + 1),
        out_specs=VMEM,
        compiler_params=PARAMS,
    )(core, *messages, gain)


def pack_kernel(core_ref, key_ref, value_ref, query_ref, own_ref, other_ref, sems):
    depth, half = key_ref.shape[0], key_ref.shape[1] // CORES
    lines = query_ref.shape[0] // 2
    copies = []
    for out_ref, who in ((own_ref, core_ref[0]), (other_ref, 1 - core_ref[0])):
        place = pl.ds(pl.multiple_of(who * half, DH), half)
        for source, target in (
            (key_ref.at[:, place], out_ref.at[pl.ds(0, depth), pl.ds(0, half)]),
            (value_ref.at[:, place], out_ref.at[pl.ds(0, depth), pl.ds(half, half)]),
            (query_ref.at[pl.ds(0, lines), place], out_ref.at[pl.ds(depth, lines), pl.ds(0, half)]),
            (query_ref.at[pl.ds(lines, lines), place], out_ref.at[pl.ds(depth, lines), pl.ds(half, half)]),
        ):
            copies.append(pltpu.make_async_copy(source, target, sems.at[len(copies)]))
            copies[-1].start()
    for copy in copies:
        copy.wait()


def pack(core, w_key, w_value, queries):
    depth, panel = w_key.shape
    out = jax.ShapeDtypeStruct((depth + queries.shape[0] // 2, panel), w_key.dtype)
    return pl.pallas_call(
        pack_kernel,
        out_shape=[out, out],
        in_specs=[SMEM, ANY, ANY, ANY],
        out_specs=[VMEM, VMEM],
        scratch_shapes=[pltpu.SemaphoreType.DMA((8,))],
        compiler_params=WIDE,
    )(core, w_key, w_value, queries)


def output_kernel(place_ref, own_ref, sibling_ref, *refs):
    chips = (len(refs) - 1) // 2
    weights, terms, result = refs[:chips], refs[chips:-1], refs[-1]
    half = own_ref.shape[1]
    mine = pl.ds(pl.multiple_of(place_ref[1] * half, DH), half)
    other = pl.ds(pl.multiple_of((1 - place_ref[1]) * half, DH), half)
    own, sibling = own_ref[...], sibling_ref[...]
    for j, w_ref in enumerate(weights):
        total = jnp.dot(own, w_ref[mine, :], preferred_element_type=jnp.float32)
        total += jnp.dot(sibling, w_ref[other, :], preferred_element_type=jnp.float32)
        result[j] = total.astype(jnp.bfloat16)
    for i, term in enumerate(terms):
        term[...] = result[place_ref[0] ^ i]


def output_terms(place, own, sibling, weights):
    chips, shape = len(weights), (own.shape[0], weights[0].shape[1])
    return pl.pallas_call(
        output_kernel,
        out_shape=[jax.ShapeDtypeStruct(shape, jnp.bfloat16)] * chips,
        in_specs=[SMEM] + [VMEM] * (2 + chips),
        out_specs=[VMEM] * chips,
        scratch_shapes=[pltpu.VMEM((chips, *shape), jnp.bfloat16)],
        compiler_params=PARAMS,
    )(place, own, sibling, *weights)


def finish_kernel(core_ref, own_ref, sibling_ref, *refs):
    outs = refs[-2 * CORES - 1 : -1]
    weights, total_ref = refs[: -2 * CORES - 1], refs[-1]
    core = core_ref[0]
    half = own_ref.shape[1] // len(weights)
    count = outs[0].shape[0]
    for i, w_ref in enumerate(weights):
        for rows_ref, who in ((own_ref, core), (sibling_ref, 1 - core)):
            product = jnp.dot(
                rows_ref[:, i * half : (i + 1) * half],
                w_ref[pl.ds(pl.multiple_of(who * half, DH), half), :],
                preferred_element_type=jnp.float32,
            )
            if i == 0 and rows_ref is own_ref:
                total_ref[...] = product
            else:
                total_ref[...] += product
    for o, out_ref in enumerate(outs):
        block = (o // CORES) * CORES + (core if o % CORES == 0 else 1 - core)
        lines = pl.ds(pl.multiple_of(block * count, count), count)
        out_ref[...] = total_ref[lines, :].astype(jnp.bfloat16)


def finish(core, own, sibling, weights):
    rows, width = own.shape[0], weights[0].shape[1]
    out = jax.ShapeDtypeStruct((rows // (2 * CORES), width), jnp.bfloat16)
    return pl.pallas_call(
        finish_kernel,
        out_shape=[out] * (2 * CORES),
        in_specs=[SMEM] + [VMEM] * (2 + len(weights)),
        out_specs=[VMEM] * (2 * CORES),
        scratch_shapes=[pltpu.VMEM((rows, width), jnp.float32)],
        compiler_params=PARAMS,
    )(core, own, sibling, *weights)


def add_kernel(core_ref, *refs):
    terms, (own_ref, other_ref) = refs[:-2], refs[-2:]
    count = own_ref.shape[0]
    for out_ref, who in ((own_ref, core_ref[0]), (other_ref, 1 - core_ref[0])):
        lines = pl.ds(pl.multiple_of(who * count, count), count)
        total = terms[0][lines, :].astype(jnp.float32)
        for term in terms[1:]:
            total += term[lines, :].astype(jnp.float32)
        out_ref[...] = total.astype(jnp.bfloat16)


def add_terms(core, terms):
    rows, width = terms[0].shape
    out = jax.ShapeDtypeStruct((rows // CORES, width), jnp.bfloat16)
    return pl.pallas_call(
        add_kernel,
        out_shape=[out, out],
        in_specs=[SMEM] + [VMEM] * len(terms),
        out_specs=[VMEM, VMEM],
        compiler_params=PARAMS,
    )(core, *terms)


def on_device(n_dp, n_ctx, context, w_key, w_value, queries, offsets, head_gain, w_out):
    chips = n_ctx // CORES
    rows = context.shape[0]
    depth, panel = w_key.shape
    heads = panel // CORES // DH
    lat_count = queries.shape[0]
    me, mine_dp = lax.axis_index("ctx"), lax.axis_index("dp")
    chip, core = me // CORES, lax.rem(me, CORES)
    core_only = core.reshape(1)

    def across(array, bits):
        return lax.ppermute(array, "ctx", [(i, i ^ bits) for i in range(n_ctx)])

    def over_dp(array, bits):
        return lax.ppermute(array, "dp", [(d, d ^ bits) for d in range(n_dp)])

    def after(array, *others):
        return lax.optimization_barrier((array, others))[0]

    near_first = sorted(range(1, chips), key=lambda j: (j.bit_count(), -j))
    own_part, other_part = pack(core_only, w_key, w_value, queries)
    pairs = [None] * chips
    for j in near_first:
        low = j & -j
        if j == low:
            pairs[j] = (across(own_part, CORES * j), across(other_part, CORES * j + 1))
        else:
            pairs[j] = tuple(
                across(after(part, near), CORES * low) for part, near in zip(pairs[j ^ low], pairs[1])
            )
    in_middle = chips == 4 and n_dp == chips
    middle = [CORES + c for c in range(2 * CORES)]

    def to_middle(array, bits):
        return lax.ppermute(array, "ctx", [(c ^ bits, c) for c in middle])

    outer = to_middle(after(w_out, own_part), CORES) if in_middle else w_out
    context_sibling = across(after(context, outer, *pairs[1], *pairs[chips // 2]), 1)
    pairs[0] = (own_part, across(after(other_part, outer, *pairs[1], *pairs[chips // 2]), 1))

    places = jnp.stack(
        [(chip ^ j) * CORES + who for j in range(chips) for who in (core, 1 - core)]
    ).astype(jnp.int32)
    starts = places * depth
    blocks = [part for pair in pairs for part in pair]
    last = CORES * (chips - 1)
    first_acc, _ = project(starts[:CORES], context, context_sibling, blocks[:CORES], None, depth)
    acc, slices = project(
        starts[CORES:], context, context_sibling, blocks[CORES:last], first_acc, depth
    )
    firsts = jnp.stack([me * rows, (me ^ 1) * rows]).astype(jnp.int32)
    gain = head_gain.reshape(1, panel)

    def messages_to(groups, slot_groups):
        return attend(
            firsts, slot_groups.astype(jnp.int32), places, slices, blocks, acc, offsets, groups,
            heads, depth,
        )

    if in_middle:
        both = after(jnp.concatenate([outer, w_out], axis=0), *pairs[1], *pairs[2])
        shards = [w_out, outer, *jnp.split(after(to_middle(both, 3 * CORES), acc), 2)]
        line = tuple(range(n_ctx))
        groups = (line[2:4] + line[0:2], line[4:6] + line[6:8])
        messages = messages_to(groups, jnp.clip((chip ^ jnp.arange(chips)) - 1, 0, 1))
        arrived = [messages[0]] + [to_middle(messages[j], CORES * j) for j in range(1, chips)]
        picked = []
        for i in range(n_dp):
            wanted = chip ^ mine_dp ^ i
            shard = shards[0]
            for j in range(1, chips):
                shard = jnp.where(wanted == j, shards[j], shard)
            picked.append(shard)
        weights = [picked[0]] + [over_dp(picked[i], i) for i in range(1, n_dp)]

        normed = combine(core_only, arrived, after(gain, *weights[1:3]), heads)
        normed = [normed] + [over_dp(normed, i) for i in range(1, n_dp)]
        normed = jnp.concatenate(normed, axis=1)
        mine, sibling, outer_mine, outer_sibling = finish(
            core_only, normed, across(normed, 1), weights
        )
        is_middle = (chip == 1) | (chip == 2)
        theirs = to_middle(sibling, 1)
        outer_mine = lax.ppermute(outer_mine, "ctx", [(c, c ^ CORES) for c in middle])
        outer_theirs = lax.ppermute(outer_sibling, "ctx", [(c, c ^ CORES ^ 1) for c in middle])
        mine = jnp.where(is_middle, mine, outer_mine)
        theirs = jnp.where(is_middle, theirs, outer_theirs)
        return jnp.where(
            core == 0, jnp.concatenate([mine, theirs], axis=1), jnp.concatenate([theirs, mine], axis=1)
        )

    groups = tuple((CORES * z, CORES * z + 1) for z in range(chips))
    messages = messages_to(groups, chip ^ jnp.arange(chips))
    arrived = [messages[0]] + [across(messages[j], CORES * j) for j in range(1, chips)]
    shards = [after(w_out, acc, *pairs[-1])] + [None] * (chips - 1)
    for j in near_first:
        low = j & -j
        shard = shards[j ^ low]
        shards[j] = across(shard if j == low else after(shard, *arrived[1:]), CORES * low)
    normed = combine(core_only, arrived, gain, heads)

    terms = output_terms(
        jnp.stack([mine_dp ^ chip, core]).astype(jnp.int32), normed, across(normed, 1), shards
    )
    terms = [terms[0]] + [over_dp(terms[i], i) for i in range(1, n_dp)]
    mine, other = add_terms(core_only, terms)
    theirs = across(other, 1)
    return jnp.where(
        core == 0, jnp.concatenate([mine, theirs], axis=1), jnp.concatenate([theirs, mine], axis=1)
    )


def solution(mesh):
    n_dp, n_ctx = mesh.shape["dp"], mesh.shape["ctx"]
    placed = (
        P("ctx", None),
        P("ctx", "dp"),
        P("ctx", "dp"),
        P("ctx", "dp"),
        P(),
        P("dp"),
        P("dp", "ctx"),
    )

    def body(*args):
        return on_device(n_dp, n_ctx, *args)

    return jax.shard_map(
        body, mesh=mesh, in_specs=placed, out_specs=P("ctx", "dp"), check_vma=False
    )
```

```python
import functools
import math

import jax
import jax.numpy as jnp
from jax import lax
from jax.experimental import pallas as pl
from jax.experimental.pallas import tpu as pltpu
from jax.sharding import PartitionSpec as P

DH = 128
NEGATIVE = -1e30
CORES = 2
STATS = 16
VMEM = pl.BlockSpec(memory_space=pltpu.VMEM)
SMEM = pl.BlockSpec(memory_space=pltpu.SMEM)
ANY = pl.BlockSpec(memory_space=pl.ANY)
PARAMS = pltpu.CompilerParams(vmem_limit_bytes=40 * 2**20)
WIDE = pltpu.CompilerParams(vmem_limit_bytes=60 * 2**20)


def three_parts(value):
    high = value.astype(jnp.bfloat16).astype(jnp.float32)
    rest = value - high
    middle = rest.astype(jnp.bfloat16).astype(jnp.float32)
    low = (rest - middle).astype(jnp.bfloat16).astype(jnp.float32)
    return [high, middle, low]


def start_slices(starts_ref, skip, contexts, buffer, sems, count, depth):
    copies = []
    for b in range(count):
        first = pl.multiple_of(starts_ref[skip + b], DH)
        for which in range(CORES):
            slot = b * CORES + which
            copies.append(
                pltpu.make_async_copy(
                    contexts[which].at[:, pl.ds(first, depth)], buffer.at[slot],
                    sems.at[skip * CORES + slot],
                )
            )
    for copy in copies:
        copy.start()
    return copies


def add_products(copies, buffer, blocks, acc_ref, rows, depth, fresh):
    for b, block in enumerate(blocks):
        for which in range(CORES):
            slot = b * CORES + which
            if copies is not None:
                copies[slot].wait()
            product = jnp.dot(buffer[slot], block[:depth, :], preferred_element_type=jnp.float32)
            place = slice(which * rows, (which + 1) * rows)
            if fresh and b == 0:
                acc_ref[place, :] = product
            else:
                acc_ref[place, :] += product


def project_kernel(count, extra, has_acc, depth, *refs):
    starts_ref, own_ref, sibling_ref = refs[:3]
    blocks = refs[3 : 3 + count]
    acc_in = refs[3 + count] if has_acc else None
    acc_ref, later_ref, buffer, sems = refs[-4:]
    contexts = (own_ref, sibling_ref)
    copies = start_slices(starts_ref, 0, contexts, buffer, sems, count, depth)
    later = start_slices(starts_ref, count, contexts, later_ref, sems, extra, depth)
    if has_acc:
        acc_ref[...] = acc_in[...]
    add_products(copies, buffer, blocks, acc_ref, own_ref.shape[0], depth, not has_acc)
    for copy in later:
        copy.wait()


def project(starts, own, sibling, blocks, acc, depth):
    count, extra = len(blocks), starts.shape[0] - len(blocks)
    rows = own.shape[0]
    width = blocks[0].shape[1]
    operands = [starts, own, sibling, *blocks] + ([acc] if acc is not None else [])
    return pl.pallas_call(
        functools.partial(project_kernel, count, extra, acc is not None, depth),
        out_shape=[
            jax.ShapeDtypeStruct((CORES * rows, width), jnp.float32),
            jax.ShapeDtypeStruct((max(extra, 1) * CORES, rows if extra else 16, depth), own.dtype),
        ],
        in_specs=[SMEM, ANY, ANY] + [VMEM] * (len(operands) - 3),
        out_specs=[VMEM, VMEM],
        scratch_shapes=[
            pltpu.VMEM((count * CORES, rows, depth), own.dtype),
            pltpu.SemaphoreType.DMA(((count + extra) * CORES,)),
        ],
        compiler_params=PARAMS,
        cost_estimate=pl.CostEstimate(
            flops=2 * count * CORES * rows * depth * width,
            bytes_accessed=2 * count * CORES * rows * depth,
            transcendentals=0,
        ),
    )(*operands)


def attend_kernel(count, heads, depth, groups, slots, *refs):
    firsts_ref, slots_ref, places_ref, slices_ref = refs[:4]
    blocks = refs[4 : 4 + count]
    acc_in, offsets_ref = refs[4 + count : 6 + count]
    messages = refs[6 + count : 6 + count + slots]
    acc_ref, query_ref, group_ref = refs[6 + count + slots :]
    rows = slices_ref.shape[1]
    half = heads * DH
    lines = blocks[0].shape[0] - depth
    acc_ref[...] = acc_in[...]
    for b, block in enumerate(blocks):
        query_ref[places_ref[b], :lines, :] = block[depth:, :half]
        query_ref[places_ref[b], lines:, :] = block[depth:, half:]
    add_products(None, slices_ref, blocks[-CORES:], acc_ref, rows, depth, False)
    score_scale = 1.0 / math.sqrt(DH)
    line = lax.broadcasted_iota(jnp.int32, (CORES * rows, 1), 0)
    positions = jnp.where(line < rows, firsts_ref[0] + line, firsts_ref[1] + line - rows)
    for h in range(heads):
        keys = acc_ref[:, h * DH : (h + 1) * DH].astype(jnp.bfloat16)
        values = acc_ref[:, half + h * DH : half + (h + 1) * DH].T.astype(jnp.bfloat16)
        for g, members in enumerate(groups):
            query = jnp.concatenate(
                [query_ref[c, :, h * DH : (h + 1) * DH] for c in members], axis=0
            )
            scores = lax.dot_general(
                keys, query, (((1,), (1,)), ((), ())), preferred_element_type=jnp.float32
            ) * score_scale
            live = positions <= offsets_ref[g : g + 1, :]
            masked = jnp.where(live, scores, NEGATIVE)
            peak = jnp.max(masked, axis=0, keepdims=True)
            weights = jnp.where(live, jnp.exp(masked - peak), 0.0).astype(jnp.bfloat16)
            total = jnp.sum(weights.astype(jnp.float32), axis=0, keepdims=True)
            numerator = jnp.dot(values, weights, preferred_element_type=jnp.float32)
            stats = three_parts(peak) + three_parts(total)
            stats.append(jnp.zeros((STATS - len(stats), peak.shape[1]), jnp.float32))
            base = h * (DH + STATS)
            group_ref[g, base : base + DH, :] = numerator.astype(jnp.bfloat16)
            group_ref[g, base + DH : base + DH + STATS, :] = jnp.concatenate(
                stats, axis=0
            ).astype(jnp.bfloat16)
    for m in range(slots):
        messages[m][...] = group_ref[slots_ref[m]]


def attend(firsts, slot_groups, places, slices, blocks, acc, offsets, groups, heads, depth):
    count, slots = len(blocks), slot_groups.shape[0]
    rows, width = slices.shape[1], blocks[0].shape[1]
    lat_count = 2 * (blocks[0].shape[0] - depth)
    group = lat_count * len(groups[0])
    length = heads * (DH + STATS)
    group_offsets = jnp.stack(
        [
            jnp.concatenate([offsets[c * lat_count : (c + 1) * lat_count] for c in members])
            for members in groups
        ]
    )
    return pl.pallas_call(
        functools.partial(attend_kernel, count, heads, depth, groups, slots),
        out_shape=[jax.ShapeDtypeStruct((length, group), jnp.bfloat16)] * slots,
        in_specs=[SMEM] * 3 + [VMEM] * (count + 3),
        out_specs=[VMEM] * slots,
        scratch_shapes=[
            pltpu.VMEM((CORES * rows, width), jnp.float32),
            pltpu.VMEM((count, lat_count, heads * DH), jnp.bfloat16),
            pltpu.VMEM((len(groups), length, group), jnp.bfloat16),
        ],
        compiler_params=PARAMS,
        cost_estimate=pl.CostEstimate(
            flops=8 * CORES * rows * group * len(groups) * heads * DH,
            bytes_accessed=2 * CORES * CORES * rows * depth,
            transcendentals=CORES * rows * group * len(groups) * heads,
        ),
    )(firsts, slot_groups, places, slices, *blocks, acc, group_offsets)


def normed_head(messages, base):
    peaks, totals = [], []
    for message in messages:
        stats = message[base + DH : base + DH + STATS, :].astype(jnp.float32)
        peaks.append(stats[0:1] + stats[1:2] + stats[2:3])
        totals.append(stats[3:4] + stats[4:5] + stats[5:6])
    top = functools.reduce(jnp.maximum, peaks)
    total, numerator = 0.0, 0.0
    for message, peak, part in zip(messages, peaks, totals):
        scale = jnp.exp(peak - top)
        total += part * scale
        numerator += message[base : base + DH, :].astype(jnp.float32) * scale
    attended = numerator / total
    mean_square = jnp.mean(attended * attended, axis=0, keepdims=True)
    return (attended * lax.rsqrt(mean_square + 1e-05)).T


def combine_kernel(heads, core_ref, *refs):
    messages, gain_ref, out_ref = refs[:-2], refs[-2], refs[-1]
    half = out_ref.shape[1]
    for h in range(heads):
        place = pl.ds(pl.multiple_of(core_ref[0] * half, DH) + h * DH, DH)
        normed = normed_head(messages, h * (DH + STATS))
        normed = normed * gain_ref[:, place].astype(jnp.float32)
        out_ref[:, h * DH : (h + 1) * DH] = normed.astype(jnp.bfloat16)


def combine(core, messages, gain, heads):
    return pl.pallas_call(
        functools.partial(combine_kernel, heads),
        out_shape=jax.ShapeDtypeStruct((messages[0].shape[1], heads * DH), jnp.bfloat16),
        in_specs=[SMEM] + [VMEM] * (len(messages) + 1),
        out_specs=VMEM,
        compiler_params=PARAMS,
    )(core, *messages, gain)


def pack_kernel(core_ref, key_ref, value_ref, query_ref, own_ref, other_ref, sems):
    depth, half = key_ref.shape[0], key_ref.shape[1] // CORES
    lines = query_ref.shape[0] // 2
    copies = []
    for out_ref, who in ((own_ref, core_ref[0]), (other_ref, 1 - core_ref[0])):
        place = pl.ds(pl.multiple_of(who * half, DH), half)
        for source, target in (
            (key_ref.at[:, place], out_ref.at[pl.ds(0, depth), pl.ds(0, half)]),
            (value_ref.at[:, place], out_ref.at[pl.ds(0, depth), pl.ds(half, half)]),
            (query_ref.at[pl.ds(0, lines), place], out_ref.at[pl.ds(depth, lines), pl.ds(0, half)]),
            (query_ref.at[pl.ds(lines, lines), place], out_ref.at[pl.ds(depth, lines), pl.ds(half, half)]),
        ):
            copies.append(pltpu.make_async_copy(source, target, sems.at[len(copies)]))
            copies[-1].start()
    for copy in copies:
        copy.wait()


def pack(core, w_key, w_value, queries):
    depth, panel = w_key.shape
    out = jax.ShapeDtypeStruct((depth + queries.shape[0] // 2, panel), w_key.dtype)
    return pl.pallas_call(
        pack_kernel,
        out_shape=[out, out],
        in_specs=[SMEM, ANY, ANY, ANY],
        out_specs=[VMEM, VMEM],
        scratch_shapes=[pltpu.SemaphoreType.DMA((8,))],
        compiler_params=WIDE,
    )(core, w_key, w_value, queries)


def output_kernel(place_ref, own_ref, sibling_ref, *refs):
    chips = (len(refs) - 1) // 2
    weights, terms, result = refs[:chips], refs[chips:-1], refs[-1]
    half = own_ref.shape[1]
    mine = pl.ds(pl.multiple_of(place_ref[1] * half, DH), half)
    other = pl.ds(pl.multiple_of((1 - place_ref[1]) * half, DH), half)
    own, sibling = own_ref[...], sibling_ref[...]
    for j, w_ref in enumerate(weights):
        total = jnp.dot(own, w_ref[mine, :], preferred_element_type=jnp.float32)
        total += jnp.dot(sibling, w_ref[other, :], preferred_element_type=jnp.float32)
        result[j] = total.astype(jnp.bfloat16)
    for i, term in enumerate(terms):
        term[...] = result[place_ref[0] ^ i]


def output_terms(place, own, sibling, weights):
    chips, shape = len(weights), (own.shape[0], weights[0].shape[1])
    return pl.pallas_call(
        output_kernel,
        out_shape=[jax.ShapeDtypeStruct(shape, jnp.bfloat16)] * chips,
        in_specs=[SMEM] + [VMEM] * (2 + chips),
        out_specs=[VMEM] * chips,
        scratch_shapes=[pltpu.VMEM((chips, *shape), jnp.bfloat16)],
        compiler_params=PARAMS,
    )(place, own, sibling, *weights)


def finish_kernel(core_ref, own_ref, sibling_ref, *refs):
    outs = refs[-2 * CORES - 1 : -1]
    weights, total_ref = refs[: -2 * CORES - 1], refs[-1]
    core = core_ref[0]
    half = own_ref.shape[1] // len(weights)
    count = outs[0].shape[0]
    for i, w_ref in enumerate(weights):
        for rows_ref, who in ((own_ref, core), (sibling_ref, 1 - core)):
            product = jnp.dot(
                rows_ref[:, i * half : (i + 1) * half],
                w_ref[pl.ds(pl.multiple_of(who * half, DH), half), :],
                preferred_element_type=jnp.float32,
            )
            if i == 0 and rows_ref is own_ref:
                total_ref[...] = product
            else:
                total_ref[...] += product
    for o, out_ref in enumerate(outs):
        block = (o // CORES) * CORES + (core if o % CORES == 0 else 1 - core)
        lines = pl.ds(pl.multiple_of(block * count, count), count)
        out_ref[...] = total_ref[lines, :].astype(jnp.bfloat16)


def finish(core, own, sibling, weights):
    rows, width = own.shape[0], weights[0].shape[1]
    out = jax.ShapeDtypeStruct((rows // (2 * CORES), width), jnp.bfloat16)
    return pl.pallas_call(
        finish_kernel,
        out_shape=[out] * (2 * CORES),
        in_specs=[SMEM] + [VMEM] * (2 + len(weights)),
        out_specs=[VMEM] * (2 * CORES),
        scratch_shapes=[pltpu.VMEM((rows, width), jnp.float32)],
        compiler_params=PARAMS,
    )(core, own, sibling, *weights)


def add_kernel(core_ref, *refs):
    terms, (own_ref, other_ref) = refs[:-2], refs[-2:]
    count = own_ref.shape[0]
    for out_ref, who in ((own_ref, core_ref[0]), (other_ref, 1 - core_ref[0])):
        lines = pl.ds(pl.multiple_of(who * count, count), count)
        total = terms[0][lines, :].astype(jnp.float32)
        for term in terms[1:]:
            total += term[lines, :].astype(jnp.float32)
        out_ref[...] = total.astype(jnp.bfloat16)


def add_terms(core, terms):
    rows, width = terms[0].shape
    out = jax.ShapeDtypeStruct((rows // CORES, width), jnp.bfloat16)
    return pl.pallas_call(
        add_kernel,
        out_shape=[out, out],
        in_specs=[SMEM] + [VMEM] * len(terms),
        out_specs=[VMEM, VMEM],
        compiler_params=PARAMS,
    )(core, *terms)


def on_device(n_dp, n_ctx, context, w_key, w_value, queries, offsets, head_gain, w_out):
    chips = n_ctx // CORES
    rows = context.shape[0]
    depth, panel = w_key.shape
    heads = panel // CORES // DH
    lat_count = queries.shape[0]
    me, mine_dp = lax.axis_index("ctx"), lax.axis_index("dp")
    chip, core = me // CORES, lax.rem(me, CORES)
    core_only = core.reshape(1)

    def across(array, bits):
        return lax.ppermute(array, "ctx", [(i, i ^ bits) for i in range(n_ctx)])

    def over_dp(array, bits):
        return lax.ppermute(array, "dp", [(d, d ^ bits) for d in range(n_dp)])

    def after(array, *others):
        return lax.optimization_barrier((array, others))[0]

    near_first = sorted(range(1, chips), key=lambda j: (j.bit_count(), -j))
    own_part, other_part = pack(core_only, w_key, w_value, queries)
    pairs = [None] * chips
    for j in near_first:
        low = j & -j
        if j == low:
            pairs[j] = (across(own_part, CORES * j), across(other_part, CORES * j + 1))
        else:
            pairs[j] = tuple(
                across(after(part, near), CORES * low) for part, near in zip(pairs[j ^ low], pairs[1])
            )
    in_middle = chips == 4 and n_dp == chips
    middle = [CORES + c for c in range(2 * CORES)]

    def to_middle(array, bits):
        return lax.ppermute(array, "ctx", [(c ^ bits, c) for c in middle])

    context_sibling = across(after(context, own_part), 1)
    pairs[0] = (own_part, across(after(other_part, context_sibling), 1))
    outer = to_middle(after(w_out, context_sibling, pairs[1][0], pairs[2][0]), CORES) if in_middle else w_out

    places = jnp.stack(
        [(chip ^ j) * CORES + who for j in range(chips) for who in (core, 1 - core)]
    ).astype(jnp.int32)
    starts = places * depth
    blocks = [part for pair in pairs for part in pair]
    last = CORES * (chips - 1)
    first_acc, _ = project(starts[:CORES], context, context_sibling, blocks[:CORES], None, depth)
    acc, slices = project(
        starts[CORES:], context, context_sibling, blocks[CORES:last], first_acc, depth
    )
    firsts = jnp.stack([me * rows, (me ^ 1) * rows]).astype(jnp.int32)
    gain = head_gain.reshape(1, panel)

    def messages_to(groups, slot_groups):
        return attend(
            firsts, slot_groups.astype(jnp.int32), places, slices, blocks, acc, offsets, groups,
            heads, depth,
        )

    if in_middle:
        both = after(jnp.concatenate([outer, w_out], axis=0), *pairs[1], *pairs[2])
        shards = [w_out, outer, *jnp.split(after(to_middle(both, 3 * CORES), acc), 2)]
        line = tuple(range(n_ctx))
        groups = (line[2:4] + line[0:2], line[4:6] + line[6:8])
        messages = messages_to(groups, jnp.clip((chip ^ jnp.arange(chips)) - 1, 0, 1))
        arrived = [messages[0]] + [to_middle(messages[j], CORES * j) for j in range(1, chips)]
        picked = []
        for i in range(n_dp):
            wanted = chip ^ mine_dp ^ i
            shard = shards[0]
            for j in range(1, chips):
                shard = jnp.where(wanted == j, shards[j], shard)
            picked.append(shard)
        weights = [picked[0]] + [over_dp(picked[i], i) for i in range(1, n_dp)]

        normed = combine(core_only, arrived, after(gain, *weights[1:]), heads)
        normed = [normed] + [over_dp(normed, i) for i in range(1, n_dp)]
        normed = jnp.concatenate(normed, axis=1)
        mine, sibling, outer_mine, outer_sibling = finish(
            core_only, normed, across(normed, 1), weights
        )
        is_middle = (chip == 1) | (chip == 2)
        theirs = to_middle(sibling, 1)
        outer_mine = lax.ppermute(outer_mine, "ctx", [(c, c ^ CORES) for c in middle])
        outer_theirs = lax.ppermute(outer_sibling, "ctx", [(c, c ^ CORES ^ 1) for c in middle])
        mine = jnp.where(is_middle, mine, outer_mine)
        theirs = jnp.where(is_middle, theirs, outer_theirs)
        return jnp.where(
            core == 0, jnp.concatenate([mine, theirs], axis=1), jnp.concatenate([theirs, mine], axis=1)
        )

    groups = tuple((CORES * z, CORES * z + 1) for z in range(chips))
    messages = messages_to(groups, chip ^ jnp.arange(chips))
    arrived = [messages[0]] + [across(messages[j], CORES * j) for j in range(1, chips)]
    shards = [after(w_out, acc, *pairs[-1])] + [None] * (chips - 1)
    for j in near_first:
        low = j & -j
        shard = shards[j ^ low]
        shards[j] = across(shard if j == low else after(shard, *arrived[1:]), CORES * low)
    normed = combine(core_only, arrived, gain, heads)

    terms = output_terms(
        jnp.stack([mine_dp ^ chip, core]).astype(jnp.int32), normed, across(normed, 1), shards
    )
    terms = [terms[0]] + [over_dp(terms[i], i) for i in range(1, n_dp)]
    mine, other = add_terms(core_only, terms)
    theirs = across(other, 1)
    return jnp.where(
        core == 0, jnp.concatenate([mine, theirs], axis=1), jnp.concatenate([theirs, mine], axis=1)
    )


def solution(mesh):
    n_dp, n_ctx = mesh.shape["dp"], mesh.shape["ctx"]
    placed = (
        P("ctx", None),
        P("ctx", "dp"),
        P("ctx", "dp"),
        P("ctx", "dp"),
        P(),
        P("dp"),
        P("dp", "ctx"),
    )

    def body(*args):
        return on_device(n_dp, n_ctx, *args)

    return jax.shard_map(
        body, mesh=mesh, in_specs=placed, out_specs=P("ctx", "dp"), check_vma=False
    )
```

```python
import functools
import math

import jax
import jax.numpy as jnp
from jax import lax
from jax.experimental import pallas as pl
from jax.experimental.pallas import tpu as pltpu
from jax.sharding import PartitionSpec as P

DH = 128
NEGATIVE = -1e30
CORES = 2
STATS = 16
VMEM = pl.BlockSpec(memory_space=pltpu.VMEM)
SMEM = pl.BlockSpec(memory_space=pltpu.SMEM)
ANY = pl.BlockSpec(memory_space=pl.ANY)
PARAMS = pltpu.CompilerParams(vmem_limit_bytes=40 * 2**20)
WIDE = pltpu.CompilerParams(vmem_limit_bytes=60 * 2**20)


def three_parts(value):
    high = value.astype(jnp.bfloat16).astype(jnp.float32)
    rest = value - high
    middle = rest.astype(jnp.bfloat16).astype(jnp.float32)
    low = (rest - middle).astype(jnp.bfloat16).astype(jnp.float32)
    return [high, middle, low]


def start_slices(starts_ref, skip, contexts, buffer, sems, count, depth):
    copies = []
    for b in range(count):
        first = pl.multiple_of(starts_ref[skip + b], DH)
        for which in range(CORES):
            slot = b * CORES + which
            copies.append(
                pltpu.make_async_copy(
                    contexts[which].at[:, pl.ds(first, depth)], buffer.at[slot],
                    sems.at[skip * CORES + slot],
                )
            )
    for copy in copies:
        copy.start()
    return copies


def add_products(copies, buffer, blocks, acc_ref, rows, depth, fresh):
    for b, block in enumerate(blocks):
        for which in range(CORES):
            slot = b * CORES + which
            if copies is not None:
                copies[slot].wait()
            product = jnp.dot(buffer[slot], block[:depth, :], preferred_element_type=jnp.float32)
            place = slice(which * rows, (which + 1) * rows)
            if fresh and b == 0:
                acc_ref[place, :] = product
            else:
                acc_ref[place, :] += product


def project_kernel(count, extra, has_acc, depth, *refs):
    starts_ref, own_ref, sibling_ref = refs[:3]
    blocks = refs[3 : 3 + count]
    acc_in = refs[3 + count] if has_acc else None
    acc_ref, later_ref, buffer, sems = refs[-4:]
    contexts = (own_ref, sibling_ref)
    copies = start_slices(starts_ref, 0, contexts, buffer, sems, count, depth)
    later = start_slices(starts_ref, count, contexts, later_ref, sems, extra, depth)
    if has_acc:
        acc_ref[...] = acc_in[...]
    add_products(copies, buffer, blocks, acc_ref, own_ref.shape[0], depth, not has_acc)
    for copy in later:
        copy.wait()


def project(starts, own, sibling, blocks, acc, depth):
    count, extra = len(blocks), starts.shape[0] - len(blocks)
    rows = own.shape[0]
    width = blocks[0].shape[1]
    operands = [starts, own, sibling, *blocks] + ([acc] if acc is not None else [])
    return pl.pallas_call(
        functools.partial(project_kernel, count, extra, acc is not None, depth),
        out_shape=[
            jax.ShapeDtypeStruct((CORES * rows, width), jnp.float32),
            jax.ShapeDtypeStruct((max(extra, 1) * CORES, rows if extra else 16, depth), own.dtype),
        ],
        in_specs=[SMEM, ANY, ANY] + [VMEM] * (len(operands) - 3),
        out_specs=[VMEM, VMEM],
        scratch_shapes=[
            pltpu.VMEM((count * CORES, rows, depth), own.dtype),
            pltpu.SemaphoreType.DMA(((count + extra) * CORES,)),
        ],
        compiler_params=PARAMS,
        cost_estimate=pl.CostEstimate(
            flops=2 * count * CORES * rows * depth * width,
            bytes_accessed=2 * count * CORES * rows * depth,
            transcendentals=0,
        ),
    )(*operands)


def attend_kernel(count, heads, depth, groups, slots, *refs):
    firsts_ref, slots_ref, places_ref, slices_ref = refs[:4]
    blocks = refs[4 : 4 + count]
    acc_in, offsets_ref = refs[4 + count : 6 + count]
    messages = refs[6 + count : 6 + count + slots]
    acc_ref, query_ref, group_ref = refs[6 + count + slots :]
    rows = slices_ref.shape[1]
    half = heads * DH
    lines = blocks[0].shape[0] - depth
    acc_ref[...] = acc_in[...]
    for b, block in enumerate(blocks):
        query_ref[places_ref[b], :lines, :] = block[depth:, :half]
        query_ref[places_ref[b], lines:, :] = block[depth:, half:]
    add_products(None, slices_ref, blocks[-CORES:], acc_ref, rows, depth, False)
    score_scale = 1.0 / math.sqrt(DH)
    line = lax.broadcasted_iota(jnp.int32, (CORES * rows, 1), 0)
    positions = jnp.where(line < rows, firsts_ref[0] + line, firsts_ref[1] + line - rows)
    for h in range(heads):
        keys = acc_ref[:, h * DH : (h + 1) * DH].astype(jnp.bfloat16)
        values = acc_ref[:, half + h * DH : half + (h + 1) * DH].T.astype(jnp.bfloat16)
        for g, members in enumerate(groups):
            query = jnp.concatenate(
                [query_ref[c, :, h * DH : (h + 1) * DH] for c in members], axis=0
            )
            scores = lax.dot_general(
                keys, query, (((1,), (1,)), ((), ())), preferred_element_type=jnp.float32
            ) * score_scale
            live = positions <= offsets_ref[g : g + 1, :]
            masked = jnp.where(live, scores, NEGATIVE)
            peak = jnp.max(masked, axis=0, keepdims=True)
            weights = jnp.where(live, jnp.exp(masked - peak), 0.0).astype(jnp.bfloat16)
            total = jnp.sum(weights.astype(jnp.float32), axis=0, keepdims=True)
            numerator = jnp.dot(values, weights, preferred_element_type=jnp.float32)
            stats = three_parts(peak) + three_parts(total)
            stats.append(jnp.zeros((STATS - len(stats), peak.shape[1]), jnp.float32))
            base = h * (DH + STATS)
            group_ref[g, base : base + DH, :] = numerator.astype(jnp.bfloat16)
            group_ref[g, base + DH : base + DH + STATS, :] = jnp.concatenate(
                stats, axis=0
            ).astype(jnp.bfloat16)
    for m in range(slots):
        messages[m][...] = group_ref[slots_ref[m]]


def attend(firsts, slot_groups, places, slices, blocks, acc, offsets, groups, heads, depth):
    count, slots = len(blocks), slot_groups.shape[0]
    rows, width = slices.shape[1], blocks[0].shape[1]
    lat_count = 2 * (blocks[0].shape[0] - depth)
    group = lat_count * len(groups[0])
    length = heads * (DH + STATS)
    group_offsets = jnp.stack(
        [
            jnp.concatenate([offsets[c * lat_count : (c + 1) * lat_count] for c in members])
            for members in groups
        ]
    )
    return pl.pallas_call(
        functools.partial(attend_kernel, count, heads, depth, groups, slots),
        out_shape=[jax.ShapeDtypeStruct((length, group), jnp.bfloat16)] * slots,
        in_specs=[SMEM] * 3 + [VMEM] * (count + 3),
        out_specs=[VMEM] * slots,
        scratch_shapes=[
            pltpu.VMEM((CORES * rows, width), jnp.float32),
            pltpu.VMEM((count, lat_count, heads * DH), jnp.bfloat16),
            pltpu.VMEM((len(groups), length, group), jnp.bfloat16),
        ],
        compiler_params=PARAMS,
        cost_estimate=pl.CostEstimate(
            flops=8 * CORES * rows * group * len(groups) * heads * DH,
            bytes_accessed=2 * CORES * CORES * rows * depth,
            transcendentals=CORES * rows * group * len(groups) * heads,
        ),
    )(firsts, slot_groups, places, slices, *blocks, acc, group_offsets)


def normed_head(messages, base):
    peaks, totals = [], []
    for message in messages:
        stats = message[base + DH : base + DH + STATS, :].astype(jnp.float32)
        peaks.append(stats[0:1] + stats[1:2] + stats[2:3])
        totals.append(stats[3:4] + stats[4:5] + stats[5:6])
    top = functools.reduce(jnp.maximum, peaks)
    total, numerator = 0.0, 0.0
    for message, peak, part in zip(messages, peaks, totals):
        scale = jnp.exp(peak - top)
        total += part * scale
        numerator += message[base : base + DH, :].astype(jnp.float32) * scale
    attended = numerator / total
    mean_square = jnp.mean(attended * attended, axis=0, keepdims=True)
    return (attended * lax.rsqrt(mean_square + 1e-05)).T


def combine_kernel(heads, core_ref, *refs):
    messages, gain_ref, out_ref = refs[:-2], refs[-2], refs[-1]
    half = out_ref.shape[1]
    for h in range(heads):
        place = pl.ds(pl.multiple_of(core_ref[0] * half, DH) + h * DH, DH)
        normed = normed_head(messages, h * (DH + STATS))
        normed = normed * gain_ref[:, place].astype(jnp.float32)
        out_ref[:, h * DH : (h + 1) * DH] = normed.astype(jnp.bfloat16)


def combine(core, messages, gain, heads):
    return pl.pallas_call(
        functools.partial(combine_kernel, heads),
        out_shape=jax.ShapeDtypeStruct((messages[0].shape[1], heads * DH), jnp.bfloat16),
        in_specs=[SMEM] + [VMEM] * (len(messages) + 1),
        out_specs=VMEM,
        compiler_params=PARAMS,
    )(core, *messages, gain)


def pack_kernel(core_ref, key_ref, value_ref, query_ref, own_ref, other_ref, sems):
    depth, half = key_ref.shape[0], key_ref.shape[1] // CORES
    lines = query_ref.shape[0] // 2
    copies = []
    for out_ref, who in ((own_ref, core_ref[0]), (other_ref, 1 - core_ref[0])):
        place = pl.ds(pl.multiple_of(who * half, DH), half)
        for source, target in (
            (key_ref.at[:, place], out_ref.at[pl.ds(0, depth), pl.ds(0, half)]),
            (value_ref.at[:, place], out_ref.at[pl.ds(0, depth), pl.ds(half, half)]),
            (query_ref.at[pl.ds(0, lines), place], out_ref.at[pl.ds(depth, lines), pl.ds(0, half)]),
            (query_ref.at[pl.ds(lines, lines), place], out_ref.at[pl.ds(depth, lines), pl.ds(half, half)]),
        ):
            copies.append(pltpu.make_async_copy(source, target, sems.at[len(copies)]))
            copies[-1].start()
    for copy in copies:
        copy.wait()


def pack(core, w_key, w_value, queries):
    depth, panel = w_key.shape
    out = jax.ShapeDtypeStruct((depth + queries.shape[0] // 2, panel), w_key.dtype)
    return pl.pallas_call(
        pack_kernel,
        out_shape=[out, out],
        in_specs=[SMEM, ANY, ANY, ANY],
        out_specs=[VMEM, VMEM],
        scratch_shapes=[pltpu.SemaphoreType.DMA((8,))],
        compiler_params=WIDE,
    )(core, w_key, w_value, queries)


def output_kernel(place_ref, own_ref, sibling_ref, *refs):
    chips = (len(refs) - 1) // 2
    weights, terms, result = refs[:chips], refs[chips:-1], refs[-1]
    half = own_ref.shape[1]
    mine = pl.ds(pl.multiple_of(place_ref[1] * half, DH), half)
    other = pl.ds(pl.multiple_of((1 - place_ref[1]) * half, DH), half)
    own, sibling = own_ref[...], sibling_ref[...]
    for j, w_ref in enumerate(weights):
        total = jnp.dot(own, w_ref[mine, :], preferred_element_type=jnp.float32)
        total += jnp.dot(sibling, w_ref[other, :], preferred_element_type=jnp.float32)
        result[j] = total.astype(jnp.bfloat16)
    for i, term in enumerate(terms):
        term[...] = result[place_ref[0] ^ i]


def output_terms(place, own, sibling, weights):
    chips, shape = len(weights), (own.shape[0], weights[0].shape[1])
    return pl.pallas_call(
        output_kernel,
        out_shape=[jax.ShapeDtypeStruct(shape, jnp.bfloat16)] * chips,
        in_specs=[SMEM] + [VMEM] * (2 + chips),
        out_specs=[VMEM] * chips,
        scratch_shapes=[pltpu.VMEM((chips, *shape), jnp.bfloat16)],
        compiler_params=PARAMS,
    )(place, own, sibling, *weights)


def add_kernel(core_ref, *refs):
    terms, (own_ref, other_ref) = refs[:-2], refs[-2:]
    count = own_ref.shape[0]
    for out_ref, who in ((own_ref, core_ref[0]), (other_ref, 1 - core_ref[0])):
        lines = pl.ds(pl.multiple_of(who * count, count), count)
        total = terms[0][lines, :].astype(jnp.float32)
        for term in terms[1:]:
            total += term[lines, :].astype(jnp.float32)
        out_ref[...] = total.astype(jnp.bfloat16)


def add_terms(core, terms):
    rows, width = terms[0].shape
    out = jax.ShapeDtypeStruct((rows // CORES, width), jnp.bfloat16)
    return pl.pallas_call(
        add_kernel,
        out_shape=[out, out],
        in_specs=[SMEM] + [VMEM] * len(terms),
        out_specs=[VMEM, VMEM],
        compiler_params=PARAMS,
    )(core, *terms)


def on_device(n_dp, n_ctx, context, w_key, w_value, queries, offsets, head_gain, w_out):
    chips = n_ctx // CORES
    rows = context.shape[0]
    depth, panel = w_key.shape
    heads = panel // CORES // DH
    lat_count = queries.shape[0]
    me, mine_dp = lax.axis_index("ctx"), lax.axis_index("dp")
    chip, core = me // CORES, lax.rem(me, CORES)
    core_only = core.reshape(1)

    def across(array, bits):
        return lax.ppermute(array, "ctx", [(i, i ^ bits) for i in range(n_ctx)])

    def over_dp(array, bits):
        return lax.ppermute(array, "dp", [(d, d ^ bits) for d in range(n_dp)])

    def after(array, *others):
        return lax.optimization_barrier((array, others))[0]

    near_first = sorted(range(1, chips), key=lambda j: (j.bit_count(), -j))
    own_part, other_part = pack(core_only, w_key, w_value, queries)
    pairs = [None] * chips
    for j in near_first:
        low = j & -j
        if j == low:
            pairs[j] = (across(own_part, CORES * j), across(other_part, CORES * j + 1))
        else:
            pairs[j] = tuple(across(part, CORES * low) for part in pairs[j ^ low])
    context_sibling = across(after(context, own_part), 1)
    pairs[0] = (own_part, across(after(other_part, pairs[1], pairs[chips // 2]), 1))

    places = jnp.stack(
        [(chip ^ j) * CORES + who for j in range(chips) for who in (core, 1 - core)]
    ).astype(jnp.int32)
    starts = places * depth
    blocks = [part for pair in pairs for part in pair]
    last = CORES * (chips - 1)
    first_acc, _ = project(starts[:CORES], context, context_sibling, blocks[:CORES], None, depth)
    acc, slices = project(
        starts[CORES:], context, context_sibling, blocks[CORES:last], first_acc, depth
    )
    firsts = jnp.stack([me * rows, (me ^ 1) * rows]).astype(jnp.int32)
    groups = tuple((CORES * z, CORES * z + 1) for z in range(chips))
    slot_groups = (chip ^ jnp.arange(chips)).astype(jnp.int32)
    messages = attend(
        firsts, slot_groups, places, slices, blocks, acc, offsets, groups, heads, depth
    )
    arrived = [messages[0]] + [across(messages[j], CORES * j) for j in range(1, chips)]
    shards = [after(w_out, acc, *pairs[-1])] + [None] * (chips - 1)
    for j in near_first:
        low = j & -j
        shard = shards[j ^ low]
        shards[j] = across(shard if j == low else after(shard, shards[1], *arrived[1:]), CORES * low)
    normed = combine(core_only, arrived, head_gain.reshape(1, panel), heads)

    terms = output_terms(
        jnp.stack([mine_dp ^ chip, core]).astype(jnp.int32), normed, across(normed, 1), shards
    )
    terms = [terms[0]] + [over_dp(terms[i], i) for i in range(1, n_dp)]
    mine, other = add_terms(core_only, terms)
    theirs = across(other, 1)
    return jnp.where(
        core == 0, jnp.concatenate([mine, theirs], axis=1), jnp.concatenate([theirs, mine], axis=1)
    )


def solution(mesh):
    n_dp, n_ctx = mesh.shape["dp"], mesh.shape["ctx"]
    placed = (
        P("ctx", None),
        P("ctx", "dp"),
        P("ctx", "dp"),
        P("ctx", "dp"),
        P(),
        P("dp"),
        P("dp", "ctx"),
    )

    def body(*args):
        return on_device(n_dp, n_ctx, *args)

    return jax.shard_map(
        body, mesh=mesh, in_specs=placed, out_specs=P("ctx", "dp"), check_vma=False
    )
```

```python
import functools
import math

import jax
import jax.numpy as jnp
from jax import lax
from jax.experimental import pallas as pl
from jax.experimental.pallas import tpu as pltpu
from jax.sharding import PartitionSpec as P

DH = 128
NEGATIVE = -1e30
CORES = 2
STATS = 16
VMEM = pl.BlockSpec(memory_space=pltpu.VMEM)
SMEM = pl.BlockSpec(memory_space=pltpu.SMEM)
ANY = pl.BlockSpec(memory_space=pl.ANY)
PARAMS = pltpu.CompilerParams(vmem_limit_bytes=40 * 2**20)
WIDE = pltpu.CompilerParams(vmem_limit_bytes=60 * 2**20)


def three_parts(value):
    high = value.astype(jnp.bfloat16).astype(jnp.float32)
    rest = value - high
    middle = rest.astype(jnp.bfloat16).astype(jnp.float32)
    low = (rest - middle).astype(jnp.bfloat16).astype(jnp.float32)
    return [high, middle, low]


def start_slices(starts_ref, skip, contexts, buffer, sems, count, depth):
    copies = []
    for b in range(count):
        first = pl.multiple_of(starts_ref[skip + b], DH)
        for which in range(CORES):
            slot = b * CORES + which
            copies.append(
                pltpu.make_async_copy(
                    contexts[which].at[:, pl.ds(first, depth)], buffer.at[slot],
                    sems.at[skip * CORES + slot],
                )
            )
    for copy in copies:
        copy.start()
    return copies


def add_products(copies, buffer, blocks, acc_ref, rows, depth, fresh):
    for b, block in enumerate(blocks):
        for which in range(CORES):
            slot = b * CORES + which
            if copies is not None:
                copies[slot].wait()
            product = jnp.dot(buffer[slot], block[:depth, :], preferred_element_type=jnp.float32)
            place = slice(which * rows, (which + 1) * rows)
            if fresh and b == 0:
                acc_ref[place, :] = product
            else:
                acc_ref[place, :] += product


def project_kernel(count, extra, has_acc, depth, *refs):
    starts_ref, own_ref, sibling_ref = refs[:3]
    blocks = refs[3 : 3 + count]
    acc_in = refs[3 + count] if has_acc else None
    acc_ref, later_ref, buffer, sems = refs[-4:]
    contexts = (own_ref, sibling_ref)
    copies = start_slices(starts_ref, 0, contexts, buffer, sems, count, depth)
    later = start_slices(starts_ref, count, contexts, later_ref, sems, extra, depth)
    if has_acc:
        acc_ref[...] = acc_in[...]
    add_products(copies, buffer, blocks, acc_ref, own_ref.shape[0], depth, not has_acc)
    for copy in later:
        copy.wait()


def project(starts, own, sibling, blocks, acc, depth):
    count, extra = len(blocks), starts.shape[0] - len(blocks)
    rows = own.shape[0]
    width = blocks[0].shape[1]
    operands = [starts, own, sibling, *blocks] + ([acc] if acc is not None else [])
    return pl.pallas_call(
        functools.partial(project_kernel, count, extra, acc is not None, depth),
        out_shape=[
            jax.ShapeDtypeStruct((CORES * rows, width), jnp.float32),
            jax.ShapeDtypeStruct((max(extra, 1) * CORES, rows if extra else 16, depth), own.dtype),
        ],
        in_specs=[SMEM, ANY, ANY] + [VMEM] * (len(operands) - 3),
        out_specs=[VMEM, VMEM],
        scratch_shapes=[
            pltpu.VMEM((count * CORES, rows, depth), own.dtype),
            pltpu.SemaphoreType.DMA(((count + extra) * CORES,)),
        ],
        compiler_params=PARAMS,
        cost_estimate=pl.CostEstimate(
            flops=2 * count * CORES * rows * depth * width,
            bytes_accessed=2 * count * CORES * rows * depth,
            transcendentals=0,
        ),
    )(*operands)


def attend_kernel(count, heads, depth, groups, slots, *refs):
    firsts_ref, slots_ref, places_ref, slices_ref = refs[:4]
    blocks = refs[4 : 4 + count]
    acc_in, offsets_ref = refs[4 + count : 6 + count]
    messages = refs[6 + count : 6 + count + slots]
    acc_ref, query_ref, group_ref = refs[6 + count + slots :]
    rows = slices_ref.shape[1]
    half = heads * DH
    lines = blocks[0].shape[0] - depth
    acc_ref[...] = acc_in[...]
    for b, block in enumerate(blocks):
        query_ref[places_ref[b], :lines, :] = block[depth:, :half]
        query_ref[places_ref[b], lines:, :] = block[depth:, half:]
    add_products(None, slices_ref, blocks[-CORES:], acc_ref, rows, depth, False)
    score_scale = 1.0 / math.sqrt(DH)
    line = lax.broadcasted_iota(jnp.int32, (CORES * rows, 1), 0)
    positions = jnp.where(line < rows, firsts_ref[0] + line, firsts_ref[1] + line - rows)
    for h in range(heads):
        keys = acc_ref[:, h * DH : (h + 1) * DH].astype(jnp.bfloat16)
        values = acc_ref[:, half + h * DH : half + (h + 1) * DH].T.astype(jnp.bfloat16)
        for g, members in enumerate(groups):
            query = jnp.concatenate(
                [query_ref[c, :, h * DH : (h + 1) * DH] for c in members], axis=0
            )
            scores = lax.dot_general(
                keys, query, (((1,), (1,)), ((), ())), preferred_element_type=jnp.float32
            ) * score_scale
            live = positions <= offsets_ref[g : g + 1, :]
            masked = jnp.where(live, scores, NEGATIVE)
            peak = jnp.max(masked, axis=0, keepdims=True)
            weights = jnp.where(live, jnp.exp(masked - peak), 0.0).astype(jnp.bfloat16)
            total = jnp.sum(weights.astype(jnp.float32), axis=0, keepdims=True)
            numerator = jnp.dot(values, weights, preferred_element_type=jnp.float32)
            stats = three_parts(peak) + three_parts(total)
            stats.append(jnp.zeros((STATS - len(stats), peak.shape[1]), jnp.float32))
            base = h * (DH + STATS)
            group_ref[g, base : base + DH, :] = numerator.astype(jnp.bfloat16)
            group_ref[g, base + DH : base + DH + STATS, :] = jnp.concatenate(
                stats, axis=0
            ).astype(jnp.bfloat16)
    for m in range(slots):
        messages[m][...] = group_ref[slots_ref[m]]


def attend(firsts, slot_groups, places, slices, blocks, acc, offsets, groups, heads, depth):
    count, slots = len(blocks), slot_groups.shape[0]
    rows, width = slices.shape[1], blocks[0].shape[1]
    lat_count = 2 * (blocks[0].shape[0] - depth)
    group = lat_count * len(groups[0])
    length = heads * (DH + STATS)
    group_offsets = jnp.stack(
        [
            jnp.concatenate([offsets[c * lat_count : (c + 1) * lat_count] for c in members])
            for members in groups
        ]
    )
    return pl.pallas_call(
        functools.partial(attend_kernel, count, heads, depth, groups, slots),
        out_shape=[jax.ShapeDtypeStruct((length, group), jnp.bfloat16)] * slots,
        in_specs=[SMEM] * 3 + [VMEM] * (count + 3),
        out_specs=[VMEM] * slots,
        scratch_shapes=[
            pltpu.VMEM((CORES * rows, width), jnp.float32),
            pltpu.VMEM((count, lat_count, heads * DH), jnp.bfloat16),
            pltpu.VMEM((len(groups), length, group), jnp.bfloat16),
        ],
        compiler_params=PARAMS,
        cost_estimate=pl.CostEstimate(
            flops=8 * CORES * rows * group * len(groups) * heads * DH,
            bytes_accessed=2 * CORES * CORES * rows * depth,
            transcendentals=CORES * rows * group * len(groups) * heads,
        ),
    )(firsts, slot_groups, places, slices, *blocks, acc, group_offsets)


def normed_head(messages, base):
    peaks, totals = [], []
    for message in messages:
        stats = message[base + DH : base + DH + STATS, :].astype(jnp.float32)
        peaks.append(stats[0:1] + stats[1:2] + stats[2:3])
        totals.append(stats[3:4] + stats[4:5] + stats[5:6])
    top = functools.reduce(jnp.maximum, peaks)
    total, numerator = 0.0, 0.0
    for message, peak, part in zip(messages, peaks, totals):
        scale = jnp.exp(peak - top)
        total += part * scale
        numerator += message[base : base + DH, :].astype(jnp.float32) * scale
    attended = numerator / total
    mean_square = jnp.mean(attended * attended, axis=0, keepdims=True)
    return (attended * lax.rsqrt(mean_square + 1e-05)).T


def combine_kernel(heads, core_ref, *refs):
    messages, gain_ref, out_ref = refs[:-2], refs[-2], refs[-1]
    half = out_ref.shape[1]
    for h in range(heads):
        place = pl.ds(pl.multiple_of(core_ref[0] * half, DH) + h * DH, DH)
        normed = normed_head(messages, h * (DH + STATS))
        normed = normed * gain_ref[:, place].astype(jnp.float32)
        out_ref[:, h * DH : (h + 1) * DH] = normed.astype(jnp.bfloat16)


def combine(core, messages, gain, heads):
    return pl.pallas_call(
        functools.partial(combine_kernel, heads),
        out_shape=jax.ShapeDtypeStruct((messages[0].shape[1], heads * DH), jnp.bfloat16),
        in_specs=[SMEM] + [VMEM] * (len(messages) + 1),
        out_specs=VMEM,
        compiler_params=PARAMS,
    )(core, *messages, gain)


def pack_kernel(core_ref, key_ref, value_ref, query_ref, own_ref, other_ref, sems):
    depth, half = key_ref.shape[0], key_ref.shape[1] // CORES
    lines = query_ref.shape[0] // 2
    copies = []
    for out_ref, who in ((own_ref, core_ref[0]), (other_ref, 1 - core_ref[0])):
        place = pl.ds(pl.multiple_of(who * half, DH), half)
        for source, target in (
            (key_ref.at[:, place], out_ref.at[pl.ds(0, depth), pl.ds(0, half)]),
            (value_ref.at[:, place], out_ref.at[pl.ds(0, depth), pl.ds(half, half)]),
            (query_ref.at[pl.ds(0, lines), place], out_ref.at[pl.ds(depth, lines), pl.ds(0, half)]),
            (query_ref.at[pl.ds(lines, lines), place], out_ref.at[pl.ds(depth, lines), pl.ds(half, half)]),
        ):
            copies.append(pltpu.make_async_copy(source, target, sems.at[len(copies)]))
            copies[-1].start()
    for copy in copies:
        copy.wait()


def pack(core, w_key, w_value, queries):
    depth, panel = w_key.shape
    out = jax.ShapeDtypeStruct((depth + queries.shape[0] // 2, panel), w_key.dtype)
    return pl.pallas_call(
        pack_kernel,
        out_shape=[out, out],
        in_specs=[SMEM, ANY, ANY, ANY],
        out_specs=[VMEM, VMEM],
        scratch_shapes=[pltpu.SemaphoreType.DMA((8,))],
        compiler_params=WIDE,
    )(core, w_key, w_value, queries)


def output_kernel(place_ref, own_ref, sibling_ref, *refs):
    chips = (len(refs) - 1) // 2
    weights, terms, result = refs[:chips], refs[chips:-1], refs[-1]
    half = own_ref.shape[1]
    mine = pl.ds(pl.multiple_of(place_ref[1] * half, DH), half)
    other = pl.ds(pl.multiple_of((1 - place_ref[1]) * half, DH), half)
    own, sibling = own_ref[...], sibling_ref[...]
    for j, w_ref in enumerate(weights):
        total = jnp.dot(own, w_ref[mine, :], preferred_element_type=jnp.float32)
        total += jnp.dot(sibling, w_ref[other, :], preferred_element_type=jnp.float32)
        result[j] = total.astype(jnp.bfloat16)
    for i, term in enumerate(terms):
        term[...] = result[place_ref[0] ^ i]


def output_terms(place, own, sibling, weights):
    chips, shape = len(weights), (own.shape[0], weights[0].shape[1])
    return pl.pallas_call(
        output_kernel,
        out_shape=[jax.ShapeDtypeStruct(shape, jnp.bfloat16)] * chips,
        in_specs=[SMEM] + [VMEM] * (2 + chips),
        out_specs=[VMEM] * chips,
        scratch_shapes=[pltpu.VMEM((chips, *shape), jnp.bfloat16)],
        compiler_params=PARAMS,
    )(place, own, sibling, *weights)


def add_kernel(core_ref, *refs):
    terms, (own_ref, other_ref) = refs[:-2], refs[-2:]
    count = own_ref.shape[0]
    for out_ref, who in ((own_ref, core_ref[0]), (other_ref, 1 - core_ref[0])):
        lines = pl.ds(pl.multiple_of(who * count, count), count)
        total = terms[0][lines, :].astype(jnp.float32)
        for term in terms[1:]:
            total += term[lines, :].astype(jnp.float32)
        out_ref[...] = total.astype(jnp.bfloat16)


def add_terms(core, terms):
    rows, width = terms[0].shape
    out = jax.ShapeDtypeStruct((rows // CORES, width), jnp.bfloat16)
    return pl.pallas_call(
        add_kernel,
        out_shape=[out, out],
        in_specs=[SMEM] + [VMEM] * len(terms),
        out_specs=[VMEM, VMEM],
        compiler_params=PARAMS,
    )(core, *terms)


def on_device(n_dp, n_ctx, context, w_key, w_value, queries, offsets, head_gain, w_out):
    chips = n_ctx // CORES
    rows = context.shape[0]
    depth, panel = w_key.shape
    heads = panel // CORES // DH
    lat_count = queries.shape[0]
    me, mine_dp = lax.axis_index("ctx"), lax.axis_index("dp")
    chip, core = me // CORES, lax.rem(me, CORES)
    core_only = core.reshape(1)

    def across(array, bits):
        return lax.ppermute(array, "ctx", [(i, i ^ bits) for i in range(n_ctx)])

    def over_dp(array, bits):
        return lax.ppermute(array, "dp", [(d, d ^ bits) for d in range(n_dp)])

    def after(array, *others):
        return lax.optimization_barrier((array, others))[0]

    near_first = sorted(range(1, chips), key=lambda j: (j.bit_count(), -j))
    own_part, other_part = pack(core_only, w_key, w_value, queries)
    pairs = [None] * chips
    for j in near_first:
        low = j & -j
        if j == low:
            pairs[j] = (across(own_part, CORES * j), across(other_part, CORES * j + 1))
        else:
            pairs[j] = tuple(
                across(after(part, near), CORES * low) for part, near in zip(pairs[j ^ low], pairs[1])
            )
    context_sibling = across(after(context, own_part), 1)
    pairs[0] = (own_part, across(after(other_part, context_sibling), 1))

    places = jnp.stack(
        [(chip ^ j) * CORES + who for j in range(chips) for who in (core, 1 - core)]
    ).astype(jnp.int32)
    starts = places * depth
    blocks = [part for pair in pairs for part in pair]
    last = CORES * (chips - 1)
    first_acc, _ = project(starts[:CORES], context, context_sibling, blocks[:CORES], None, depth)
    acc, slices = project(
        starts[CORES:], context, context_sibling, blocks[CORES:last], first_acc, depth
    )
    firsts = jnp.stack([me * rows, (me ^ 1) * rows]).astype(jnp.int32)
    groups = tuple((CORES * z, CORES * z + 1) for z in range(chips))
    slot_groups = (chip ^ jnp.arange(chips)).astype(jnp.int32)
    messages = attend(
        firsts, slot_groups, places, slices, blocks, acc, offsets, groups, heads, depth
    )
    arrived = [messages[0]] + [across(messages[j], CORES * j) for j in range(1, chips)]
    shards = [after(w_out, acc, *pairs[-1])] + [None] * (chips - 1)
    for j in near_first:
        low = j & -j
        shard = shards[j ^ low]
        shards[j] = across(shard if j == low else after(shard, shards[1], *arrived[1:]), CORES * low)
    normed = combine(core_only, arrived, head_gain.reshape(1, panel), heads)

    terms = output_terms(
        jnp.stack([mine_dp ^ chip, core]).astype(jnp.int32), normed, across(normed, 1), shards
    )
    terms = [terms[0]] + [over_dp(terms[i], i) for i in range(1, n_dp)]
    mine, other = add_terms(core_only, terms)
    theirs = across(other, 1)
    return jnp.where(
        core == 0, jnp.concatenate([mine, theirs], axis=1), jnp.concatenate([theirs, mine], axis=1)
    )


def solution(mesh):
    n_dp, n_ctx = mesh.shape["dp"], mesh.shape["ctx"]
    placed = (
        P("ctx", None),
        P("ctx", "dp"),
        P("ctx", "dp"),
        P("ctx", "dp"),
        P(),
        P("dp"),
        P("dp", "ctx"),
    )

    def body(*args):
        return on_device(n_dp, n_ctx, *args)

    return jax.shard_map(
        body, mesh=mesh, in_specs=placed, out_specs=P("ctx", "dp"), check_vma=False
    )
```

```python
import functools
import math

import jax
import jax.numpy as jnp
from jax import lax
from jax.experimental import pallas as pl
from jax.experimental.pallas import tpu as pltpu
from jax.sharding import PartitionSpec as P

DH = 128
NEGATIVE = -1e30
CORES = 2
STATS = 16
VMEM = pl.BlockSpec(memory_space=pltpu.VMEM)
SMEM = pl.BlockSpec(memory_space=pltpu.SMEM)
ANY = pl.BlockSpec(memory_space=pl.ANY)
PARAMS = pltpu.CompilerParams(vmem_limit_bytes=40 * 2**20)
WIDE = pltpu.CompilerParams(vmem_limit_bytes=60 * 2**20)


def three_parts(value):
    high = value.astype(jnp.bfloat16).astype(jnp.float32)
    rest = value - high
    middle = rest.astype(jnp.bfloat16).astype(jnp.float32)
    low = (rest - middle).astype(jnp.bfloat16).astype(jnp.float32)
    return [high, middle, low]


def start_slices(starts_ref, skip, contexts, buffer, sems, count, depth):
    copies = []
    for b in range(count):
        first = pl.multiple_of(starts_ref[skip + b], DH)
        for which in range(CORES):
            slot = b * CORES + which
            copies.append(
                pltpu.make_async_copy(
                    contexts[which].at[:, pl.ds(first, depth)], buffer.at[slot],
                    sems.at[skip * CORES + slot],
                )
            )
    for copy in copies:
        copy.start()
    return copies


def add_products(copies, buffer, blocks, acc_ref, rows, depth, fresh):
    for b, block in enumerate(blocks):
        for which in range(CORES):
            slot = b * CORES + which
            if copies is not None:
                copies[slot].wait()
            product = jnp.dot(buffer[slot], block[:depth, :], preferred_element_type=jnp.float32)
            place = slice(which * rows, (which + 1) * rows)
            if fresh and b == 0:
                acc_ref[place, :] = product
            else:
                acc_ref[place, :] += product


def project_kernel(count, extra, has_acc, depth, *refs):
    starts_ref, own_ref, sibling_ref = refs[:3]
    blocks = refs[3 : 3 + count]
    acc_in = refs[3 + count] if has_acc else None
    acc_ref, later_ref, buffer, sems = refs[-4:]
    contexts = (own_ref, sibling_ref)
    copies = start_slices(starts_ref, 0, contexts, buffer, sems, count, depth)
    later = start_slices(starts_ref, count, contexts, later_ref, sems, extra, depth)
    if has_acc:
        acc_ref[...] = acc_in[...]
    add_products(copies, buffer, blocks, acc_ref, own_ref.shape[0], depth, not has_acc)
    for copy in later:
        copy.wait()


def project(starts, own, sibling, blocks, acc, depth):
    count, extra = len(blocks), starts.shape[0] - len(blocks)
    rows = own.shape[0]
    width = blocks[0].shape[1]
    operands = [starts, own, sibling, *blocks] + ([acc] if acc is not None else [])
    return pl.pallas_call(
        functools.partial(project_kernel, count, extra, acc is not None, depth),
        out_shape=[
            jax.ShapeDtypeStruct((CORES * rows, width), jnp.float32),
            jax.ShapeDtypeStruct((max(extra, 1) * CORES, rows if extra else 16, depth), own.dtype),
        ],
        in_specs=[SMEM, ANY, ANY] + [VMEM] * (len(operands) - 3),
        out_specs=[VMEM, VMEM],
        scratch_shapes=[
            pltpu.VMEM((count * CORES, rows, depth), own.dtype),
            pltpu.SemaphoreType.DMA(((count + extra) * CORES,)),
        ],
        compiler_params=PARAMS,
        cost_estimate=pl.CostEstimate(
            flops=2 * count * CORES * rows * depth * width,
            bytes_accessed=2 * count * CORES * rows * depth,
            transcendentals=0,
        ),
    )(*operands)


def attend_kernel(count, heads, depth, groups, slots, *refs):
    firsts_ref, slots_ref, places_ref, slices_ref = refs[:4]
    blocks = refs[4 : 4 + count]
    acc_in, offsets_ref = refs[4 + count : 6 + count]
    messages = refs[6 + count : 6 + count + slots]
    acc_ref, query_ref, group_ref = refs[6 + count + slots :]
    rows = slices_ref.shape[1]
    half = heads * DH
    lines = blocks[0].shape[0] - depth
    acc_ref[...] = acc_in[...]
    for b, block in enumerate(blocks):
        query_ref[places_ref[b], :lines, :] = block[depth:, :half]
        query_ref[places_ref[b], lines:, :] = block[depth:, half:]
    add_products(None, slices_ref, blocks[-CORES:], acc_ref, rows, depth, False)
    score_scale = 1.0 / math.sqrt(DH)
    line = lax.broadcasted_iota(jnp.int32, (CORES * rows, 1), 0)
    positions = jnp.where(line < rows, firsts_ref[0] + line, firsts_ref[1] + line - rows)
    for h in range(heads):
        keys = acc_ref[:, h * DH : (h + 1) * DH].astype(jnp.bfloat16)
        values = acc_ref[:, half + h * DH : half + (h + 1) * DH].T.astype(jnp.bfloat16)
        for g, members in enumerate(groups):
            query = jnp.concatenate(
                [query_ref[c, :, h * DH : (h + 1) * DH] for c in members], axis=0
            )
            scores = lax.dot_general(
                keys, query, (((1,), (1,)), ((), ())), preferred_element_type=jnp.float32
            ) * score_scale
            live = positions <= offsets_ref[g : g + 1, :]
            masked = jnp.where(live, scores, NEGATIVE)
            peak = jnp.max(masked, axis=0, keepdims=True)
            weights = jnp.where(live, jnp.exp(masked - peak), 0.0).astype(jnp.bfloat16)
            total = jnp.sum(weights.astype(jnp.float32), axis=0, keepdims=True)
            numerator = jnp.dot(values, weights, preferred_element_type=jnp.float32)
            stats = three_parts(peak) + three_parts(total)
            stats.append(jnp.zeros((STATS - len(stats), peak.shape[1]), jnp.float32))
            base = h * (DH + STATS)
            group_ref[g, base : base + DH, :] = numerator.astype(jnp.bfloat16)
            group_ref[g, base + DH : base + DH + STATS, :] = jnp.concatenate(
                stats, axis=0
            ).astype(jnp.bfloat16)
    for m in range(slots):
        messages[m][...] = group_ref[slots_ref[m]]


def attend(firsts, slot_groups, places, slices, blocks, acc, offsets, groups, heads, depth):
    count, slots = len(blocks), slot_groups.shape[0]
    rows, width = slices.shape[1], blocks[0].shape[1]
    lat_count = 2 * (blocks[0].shape[0] - depth)
    group = lat_count * len(groups[0])
    length = heads * (DH + STATS)
    group_offsets = jnp.stack(
        [
            jnp.concatenate([offsets[c * lat_count : (c + 1) * lat_count] for c in members])
            for members in groups
        ]
    )
    return pl.pallas_call(
        functools.partial(attend_kernel, count, heads, depth, groups, slots),
        out_shape=[jax.ShapeDtypeStruct((length, group), jnp.bfloat16)] * slots,
        in_specs=[SMEM] * 3 + [VMEM] * (count + 3),
        out_specs=[VMEM] * slots,
        scratch_shapes=[
            pltpu.VMEM((CORES * rows, width), jnp.float32),
            pltpu.VMEM((count, lat_count, heads * DH), jnp.bfloat16),
            pltpu.VMEM((len(groups), length, group), jnp.bfloat16),
        ],
        compiler_params=PARAMS,
        cost_estimate=pl.CostEstimate(
            flops=8 * CORES * rows * group * len(groups) * heads * DH,
            bytes_accessed=2 * CORES * CORES * rows * depth,
            transcendentals=CORES * rows * group * len(groups) * heads,
        ),
    )(firsts, slot_groups, places, slices, *blocks, acc, group_offsets)


def normed_head(messages, base):
    peaks, totals = [], []
    for message in messages:
        stats = message[base + DH : base + DH + STATS, :].astype(jnp.float32)
        peaks.append(stats[0:1] + stats[1:2] + stats[2:3])
        totals.append(stats[3:4] + stats[4:5] + stats[5:6])
    top = functools.reduce(jnp.maximum, peaks)
    total, numerator = 0.0, 0.0
    for message, peak, part in zip(messages, peaks, totals):
        scale = jnp.exp(peak - top)
        total += part * scale
        numerator += message[base : base + DH, :].astype(jnp.float32) * scale
    attended = numerator / total
    mean_square = jnp.mean(attended * attended, axis=0, keepdims=True)
    return (attended * lax.rsqrt(mean_square + 1e-05)).T


def combine_kernel(heads, core_ref, *refs):
    messages, gain_ref, out_ref = refs[:-2], refs[-2], refs[-1]
    half = out_ref.shape[1]
    for h in range(heads):
        place = pl.ds(pl.multiple_of(core_ref[0] * half, DH) + h * DH, DH)
        normed = normed_head(messages, h * (DH + STATS))
        normed = normed * gain_ref[:, place].astype(jnp.float32)
        out_ref[:, h * DH : (h + 1) * DH] = normed.astype(jnp.bfloat16)


def combine(core, messages, gain, heads):
    return pl.pallas_call(
        functools.partial(combine_kernel, heads),
        out_shape=jax.ShapeDtypeStruct((messages[0].shape[1], heads * DH), jnp.bfloat16),
        in_specs=[SMEM] + [VMEM] * (len(messages) + 1),
        out_specs=VMEM,
        compiler_params=PARAMS,
    )(core, *messages, gain)


def pack_kernel(core_ref, key_ref, value_ref, query_ref, own_ref, other_ref, sems):
    depth, half = key_ref.shape[0], key_ref.shape[1] // CORES
    lines = query_ref.shape[0] // 2
    copies = []
    for out_ref, who in ((own_ref, core_ref[0]), (other_ref, 1 - core_ref[0])):
        place = pl.ds(pl.multiple_of(who * half, DH), half)
        for source, target in (
            (key_ref.at[:, place], out_ref.at[pl.ds(0, depth), pl.ds(0, half)]),
            (value_ref.at[:, place], out_ref.at[pl.ds(0, depth), pl.ds(half, half)]),
            (query_ref.at[pl.ds(0, lines), place], out_ref.at[pl.ds(depth, lines), pl.ds(0, half)]),
            (query_ref.at[pl.ds(lines, lines), place], out_ref.at[pl.ds(depth, lines), pl.ds(half, half)]),
        ):
            copies.append(pltpu.make_async_copy(source, target, sems.at[len(copies)]))
            copies[-1].start()
    for copy in copies:
        copy.wait()


def pack(core, w_key, w_value, queries):
    depth, panel = w_key.shape
    out = jax.ShapeDtypeStruct((depth + queries.shape[0] // 2, panel), w_key.dtype)
    return pl.pallas_call(
        pack_kernel,
        out_shape=[out, out],
        in_specs=[SMEM, ANY, ANY, ANY],
        out_specs=[VMEM, VMEM],
        scratch_shapes=[pltpu.SemaphoreType.DMA((8,))],
        compiler_params=WIDE,
    )(core, w_key, w_value, queries)


def output_kernel(place_ref, own_ref, sibling_ref, *refs):
    chips = (len(refs) - 1) // 2
    weights, terms, result = refs[:chips], refs[chips:-1], refs[-1]
    half = own_ref.shape[1]
    mine = pl.ds(pl.multiple_of(place_ref[1] * half, DH), half)
    other = pl.ds(pl.multiple_of((1 - place_ref[1]) * half, DH), half)
    own, sibling = own_ref[...], sibling_ref[...]
    for j, w_ref in enumerate(weights):
        total = jnp.dot(own, w_ref[mine, :], preferred_element_type=jnp.float32)
        total += jnp.dot(sibling, w_ref[other, :], preferred_element_type=jnp.float32)
        result[j] = total.astype(jnp.bfloat16)
    for i, term in enumerate(terms):
        term[...] = result[place_ref[0] ^ i]


def output_terms(place, own, sibling, weights):
    chips, shape = len(weights), (own.shape[0], weights[0].shape[1])
    return pl.pallas_call(
        output_kernel,
        out_shape=[jax.ShapeDtypeStruct(shape, jnp.bfloat16)] * chips,
        in_specs=[SMEM] + [VMEM] * (2 + chips),
        out_specs=[VMEM] * chips,
        scratch_shapes=[pltpu.VMEM((chips, *shape), jnp.bfloat16)],
        compiler_params=PARAMS,
    )(place, own, sibling, *weights)


def add_kernel(core_ref, *refs):
    terms, (own_ref, other_ref) = refs[:-2], refs[-2:]
    count = own_ref.shape[0]
    for out_ref, who in ((own_ref, core_ref[0]), (other_ref, 1 - core_ref[0])):
        lines = pl.ds(pl.multiple_of(who * count, count), count)
        total = terms[0][lines, :].astype(jnp.float32)
        for term in terms[1:]:
            total += term[lines, :].astype(jnp.float32)
        out_ref[...] = total.astype(jnp.bfloat16)


def add_terms(core, terms):
    rows, width = terms[0].shape
    out = jax.ShapeDtypeStruct((rows // CORES, width), jnp.bfloat16)
    return pl.pallas_call(
        add_kernel,
        out_shape=[out, out],
        in_specs=[SMEM] + [VMEM] * len(terms),
        out_specs=[VMEM, VMEM],
        compiler_params=PARAMS,
    )(core, *terms)


def on_device(n_dp, n_ctx, context, w_key, w_value, queries, offsets, head_gain, w_out):
    chips = n_ctx // CORES
    rows = context.shape[0]
    depth, panel = w_key.shape
    heads = panel // CORES // DH
    lat_count = queries.shape[0]
    me, mine_dp = lax.axis_index("ctx"), lax.axis_index("dp")
    chip, core = me // CORES, lax.rem(me, CORES)
    core_only = core.reshape(1)

    def across(array, bits):
        return lax.ppermute(array, "ctx", [(i, i ^ bits) for i in range(n_ctx)])

    def over_dp(array, bits):
        return lax.ppermute(array, "dp", [(d, d ^ bits) for d in range(n_dp)])

    def after(array, *others):
        return lax.optimization_barrier((array, others))[0]

    near_first = sorted(range(1, chips), key=lambda j: (j.bit_count(), -j))
    own_part, other_part = pack(core_only, w_key, w_value, queries)
    pairs = [None] * chips
    for j in near_first:
        if j & (j - 1) == 0:
            pairs[j] = (across(own_part, CORES * j), across(other_part, CORES * j + 1))
    context_sibling = across(after(context, own_part), 1)
    pairs[0] = (own_part, across(after(other_part, context_sibling), 1))

    places = jnp.stack(
        [(chip ^ j) * CORES + who for j in range(chips) for who in (core, 1 - core)]
    ).astype(jnp.int32)
    starts = places * depth
    first_acc, _ = project(starts[:CORES], context, context_sibling, pairs[0], None, depth)
    for j in near_first:
        low = j & -j
        if j != low:
            held, near = pairs[j ^ low], pairs[1]
            pairs[j] = (
                across(after(held[0], near[0]), CORES * low),
                across(after(held[1], near[1], first_acc), CORES * low),
            )
    blocks = [part for pair in pairs for part in pair]
    last = CORES * (chips - 1)
    acc, slices = project(
        starts[CORES:], context, context_sibling, blocks[CORES:last], first_acc, depth
    )
    firsts = jnp.stack([me * rows, (me ^ 1) * rows]).astype(jnp.int32)
    groups = tuple((CORES * z, CORES * z + 1) for z in range(chips))
    slot_groups = (chip ^ jnp.arange(chips)).astype(jnp.int32)
    messages = attend(
        firsts, slot_groups, places, slices, blocks, acc, offsets, groups, heads, depth
    )
    arrived = [messages[0]] + [across(messages[j], CORES * j) for j in range(1, chips)]
    shards = [after(w_out, acc)] + [None] * (chips - 1)
    for j in near_first:
        low = j & -j
        shard = shards[j ^ low]
        shards[j] = across(shard if j == low else after(shard, shards[1], *arrived[1:]), CORES * low)
    normed = combine(core_only, arrived, head_gain.reshape(1, panel), heads)

    terms = output_terms(
        jnp.stack([mine_dp ^ chip, core]).astype(jnp.int32), normed, across(normed, 1), shards
    )
    terms = [terms[0]] + [over_dp(terms[i], i) for i in range(1, n_dp)]
    mine, other = add_terms(core_only, terms)
    theirs = across(other, 1)
    return jnp.where(
        core == 0, jnp.concatenate([mine, theirs], axis=1), jnp.concatenate([theirs, mine], axis=1)
    )


def solution(mesh):
    n_dp, n_ctx = mesh.shape["dp"], mesh.shape["ctx"]
    placed = (
        P("ctx", None),
        P("ctx", "dp"),
        P("ctx", "dp"),
        P("ctx", "dp"),
        P(),
        P("dp"),
        P("dp", "ctx"),
    )

    def body(*args):
        return on_device(n_dp, n_ctx, *args)

    return jax.shard_map(
        body, mesh=mesh, in_specs=placed, out_specs=P("ctx", "dp"), check_vma=False
    )
```

```python
import functools
import math

import jax
import jax.numpy as jnp
from jax import lax
from jax.experimental import pallas as pl
from jax.experimental.pallas import tpu as pltpu
from jax.sharding import PartitionSpec as P

DH = 128
NEGATIVE = -1e30
CORES = 2
STATS = 16
VMEM = pl.BlockSpec(memory_space=pltpu.VMEM)
SMEM = pl.BlockSpec(memory_space=pltpu.SMEM)
ANY = pl.BlockSpec(memory_space=pl.ANY)
PARAMS = pltpu.CompilerParams(vmem_limit_bytes=40 * 2**20)
WIDE = pltpu.CompilerParams(vmem_limit_bytes=60 * 2**20)


def three_parts(value):
    high = value.astype(jnp.bfloat16).astype(jnp.float32)
    rest = value - high
    middle = rest.astype(jnp.bfloat16).astype(jnp.float32)
    low = (rest - middle).astype(jnp.bfloat16).astype(jnp.float32)
    return [high, middle, low]


def start_slices(starts_ref, skip, contexts, buffer, sems, count, depth):
    copies = []
    for b in range(count):
        first = pl.multiple_of(starts_ref[skip + b], DH)
        for which in range(CORES):
            slot = b * CORES + which
            copies.append(
                pltpu.make_async_copy(
                    contexts[which].at[:, pl.ds(first, depth)], buffer.at[slot],
                    sems.at[skip * CORES + slot],
                )
            )
    for copy in copies:
        copy.start()
    return copies


def add_products(copies, buffer, blocks, acc_ref, rows, depth, fresh):
    for b, block in enumerate(blocks):
        for which in range(CORES):
            slot = b * CORES + which
            if copies is not None:
                copies[slot].wait()
            product = jnp.dot(buffer[slot], block[:depth, :], preferred_element_type=jnp.float32)
            place = slice(which * rows, (which + 1) * rows)
            if fresh and b == 0:
                acc_ref[place, :] = product
            else:
                acc_ref[place, :] += product


def project_kernel(count, extra, has_acc, depth, *refs):
    starts_ref, own_ref, sibling_ref = refs[:3]
    blocks = refs[3 : 3 + count]
    acc_in = refs[3 + count] if has_acc else None
    acc_ref, later_ref, buffer, sems = refs[-4:]
    contexts = (own_ref, sibling_ref)
    copies = start_slices(starts_ref, 0, contexts, buffer, sems, count, depth)
    later = start_slices(starts_ref, count, contexts, later_ref, sems, extra, depth)
    if has_acc:
        acc_ref[...] = acc_in[...]
    add_products(copies, buffer, blocks, acc_ref, own_ref.shape[0], depth, not has_acc)
    for copy in later:
        copy.wait()


def project(starts, own, sibling, blocks, acc, depth):
    count, extra = len(blocks), starts.shape[0] - len(blocks)
    rows = own.shape[0]
    width = blocks[0].shape[1]
    operands = [starts, own, sibling, *blocks] + ([acc] if acc is not None else [])
    return pl.pallas_call(
        functools.partial(project_kernel, count, extra, acc is not None, depth),
        out_shape=[
            jax.ShapeDtypeStruct((CORES * rows, width), jnp.float32),
            jax.ShapeDtypeStruct((max(extra, 1) * CORES, rows if extra else 16, depth), own.dtype),
        ],
        in_specs=[SMEM, ANY, ANY] + [VMEM] * (len(operands) - 3),
        out_specs=[VMEM, VMEM],
        scratch_shapes=[
            pltpu.VMEM((count * CORES, rows, depth), own.dtype),
            pltpu.SemaphoreType.DMA(((count + extra) * CORES,)),
        ],
        compiler_params=PARAMS,
        cost_estimate=pl.CostEstimate(
            flops=2 * count * CORES * rows * depth * width,
            bytes_accessed=2 * count * CORES * rows * depth,
            transcendentals=0,
        ),
    )(*operands)


def attend_kernel(count, heads, depth, groups, slots, *refs):
    firsts_ref, slots_ref, places_ref, slices_ref = refs[:4]
    blocks = refs[4 : 4 + count]
    acc_in, offsets_ref = refs[4 + count : 6 + count]
    messages = refs[6 + count : 6 + count + slots]
    acc_ref, query_ref, group_ref = refs[6 + count + slots :]
    rows = slices_ref.shape[1]
    half = heads * DH
    lines = blocks[0].shape[0] - depth
    acc_ref[...] = acc_in[...]
    for b, block in enumerate(blocks):
        query_ref[places_ref[b], :lines, :] = block[depth:, :half]
        query_ref[places_ref[b], lines:, :] = block[depth:, half:]
    add_products(None, slices_ref, blocks[-CORES:], acc_ref, rows, depth, False)
    score_scale = 1.0 / math.sqrt(DH)
    line = lax.broadcasted_iota(jnp.int32, (CORES * rows, 1), 0)
    positions = jnp.where(line < rows, firsts_ref[0] + line, firsts_ref[1] + line - rows)
    for h in range(heads):
        keys = acc_ref[:, h * DH : (h + 1) * DH].astype(jnp.bfloat16)
        values = acc_ref[:, half + h * DH : half + (h + 1) * DH].T.astype(jnp.bfloat16)
        for g, members in enumerate(groups):
            query = jnp.concatenate(
                [query_ref[c, :, h * DH : (h + 1) * DH] for c in members], axis=0
            )
            scores = lax.dot_general(
                keys, query, (((1,), (1,)), ((), ())), preferred_element_type=jnp.float32
            ) * score_scale
            live = positions <= offsets_ref[g : g + 1, :]
            masked = jnp.where(live, scores, NEGATIVE)
            peak = jnp.max(masked, axis=0, keepdims=True)
            weights = jnp.where(live, jnp.exp(masked - peak), 0.0).astype(jnp.bfloat16)
            total = jnp.sum(weights.astype(jnp.float32), axis=0, keepdims=True)
            numerator = jnp.dot(values, weights, preferred_element_type=jnp.float32)
            stats = three_parts(peak) + three_parts(total)
            stats.append(jnp.zeros((STATS - len(stats), peak.shape[1]), jnp.float32))
            base = h * (DH + STATS)
            group_ref[g, base : base + DH, :] = numerator.astype(jnp.bfloat16)
            group_ref[g, base + DH : base + DH + STATS, :] = jnp.concatenate(
                stats, axis=0
            ).astype(jnp.bfloat16)
    for m in range(slots):
        messages[m][...] = group_ref[slots_ref[m]]


def attend(firsts, slot_groups, places, slices, blocks, acc, offsets, groups, heads, depth):
    count, slots = len(blocks), slot_groups.shape[0]
    rows, width = slices.shape[1], blocks[0].shape[1]
    lat_count = 2 * (blocks[0].shape[0] - depth)
    group = lat_count * len(groups[0])
    length = heads * (DH + STATS)
    group_offsets = jnp.stack(
        [
            jnp.concatenate([offsets[c * lat_count : (c + 1) * lat_count] for c in members])
            for members in groups
        ]
    )
    return pl.pallas_call(
        functools.partial(attend_kernel, count, heads, depth, groups, slots),
        out_shape=[jax.ShapeDtypeStruct((length, group), jnp.bfloat16)] * slots,
        in_specs=[SMEM] * 3 + [VMEM] * (count + 3),
        out_specs=[VMEM] * slots,
        scratch_shapes=[
            pltpu.VMEM((CORES * rows, width), jnp.float32),
            pltpu.VMEM((count, lat_count, heads * DH), jnp.bfloat16),
            pltpu.VMEM((len(groups), length, group), jnp.bfloat16),
        ],
        compiler_params=PARAMS,
        cost_estimate=pl.CostEstimate(
            flops=8 * CORES * rows * group * len(groups) * heads * DH,
            bytes_accessed=2 * CORES * CORES * rows * depth,
            transcendentals=CORES * rows * group * len(groups) * heads,
        ),
    )(firsts, slot_groups, places, slices, *blocks, acc, group_offsets)


def normed_head(messages, base):
    peaks, totals = [], []
    for message in messages:
        stats = message[base + DH : base + DH + STATS, :].astype(jnp.float32)
        peaks.append(stats[0:1] + stats[1:2] + stats[2:3])
        totals.append(stats[3:4] + stats[4:5] + stats[5:6])
    top = functools.reduce(jnp.maximum, peaks)
    total, numerator = 0.0, 0.0
    for message, peak, part in zip(messages, peaks, totals):
        scale = jnp.exp(peak - top)
        total += part * scale
        numerator += message[base : base + DH, :].astype(jnp.float32) * scale
    attended = numerator / total
    mean_square = jnp.mean(attended * attended, axis=0, keepdims=True)
    return (attended * lax.rsqrt(mean_square + 1e-05)).T


def combine_kernel(heads, core_ref, *refs):
    messages, gain_ref, out_ref = refs[:-2], refs[-2], refs[-1]
    half = out_ref.shape[1]
    for h in range(heads):
        place = pl.ds(pl.multiple_of(core_ref[0] * half, DH) + h * DH, DH)
        normed = normed_head(messages, h * (DH + STATS))
        normed = normed * gain_ref[:, place].astype(jnp.float32)
        out_ref[:, h * DH : (h + 1) * DH] = normed.astype(jnp.bfloat16)


def combine(core, messages, gain, heads):
    return pl.pallas_call(
        functools.partial(combine_kernel, heads),
        out_shape=jax.ShapeDtypeStruct((messages[0].shape[1], heads * DH), jnp.bfloat16),
        in_specs=[SMEM] + [VMEM] * (len(messages) + 1),
        out_specs=VMEM,
        compiler_params=PARAMS,
    )(core, *messages, gain)


def pack_kernel(core_ref, key_ref, value_ref, query_ref, own_ref, other_ref, sems):
    depth, half = key_ref.shape[0], key_ref.shape[1] // CORES
    lines = query_ref.shape[0] // 2
    copies = []
    for out_ref, who in ((own_ref, core_ref[0]), (other_ref, 1 - core_ref[0])):
        place = pl.ds(pl.multiple_of(who * half, DH), half)
        for source, target in (
            (key_ref.at[:, place], out_ref.at[pl.ds(0, depth), pl.ds(0, half)]),
            (value_ref.at[:, place], out_ref.at[pl.ds(0, depth), pl.ds(half, half)]),
            (query_ref.at[pl.ds(0, lines), place], out_ref.at[pl.ds(depth, lines), pl.ds(0, half)]),
            (query_ref.at[pl.ds(lines, lines), place], out_ref.at[pl.ds(depth, lines), pl.ds(half, half)]),
        ):
            copies.append(pltpu.make_async_copy(source, target, sems.at[len(copies)]))
            copies[-1].start()
    for copy in copies:
        copy.wait()


def pack(core, w_key, w_value, queries):
    depth, panel = w_key.shape
    out = jax.ShapeDtypeStruct((depth + queries.shape[0] // 2, panel), w_key.dtype)
    return pl.pallas_call(
        pack_kernel,
        out_shape=[out, out],
        in_specs=[SMEM, ANY, ANY, ANY],
        out_specs=[VMEM, VMEM],
        scratch_shapes=[pltpu.SemaphoreType.DMA((8,))],
        compiler_params=WIDE,
    )(core, w_key, w_value, queries)


def output_kernel(place_ref, own_ref, sibling_ref, *refs):
    chips = (len(refs) - 1) // 2
    weights, terms, result = refs[:chips], refs[chips:-1], refs[-1]
    half = own_ref.shape[1]
    mine = pl.ds(pl.multiple_of(place_ref[1] * half, DH), half)
    other = pl.ds(pl.multiple_of((1 - place_ref[1]) * half, DH), half)
    own, sibling = own_ref[...], sibling_ref[...]
    for j, w_ref in enumerate(weights):
        total = jnp.dot(own, w_ref[mine, :], preferred_element_type=jnp.float32)
        total += jnp.dot(sibling, w_ref[other, :], preferred_element_type=jnp.float32)
        result[j] = total.astype(jnp.bfloat16)
    for i, term in enumerate(terms):
        term[...] = result[place_ref[0] ^ i]


def output_terms(place, own, sibling, weights):
    chips, shape = len(weights), (own.shape[0], weights[0].shape[1])
    return pl.pallas_call(
        output_kernel,
        out_shape=[jax.ShapeDtypeStruct(shape, jnp.bfloat16)] * chips,
        in_specs=[SMEM] + [VMEM] * (2 + chips),
        out_specs=[VMEM] * chips,
        scratch_shapes=[pltpu.VMEM((chips, *shape), jnp.bfloat16)],
        compiler_params=PARAMS,
    )(place, own, sibling, *weights)


def add_kernel(core_ref, *refs):
    terms, (own_ref, other_ref) = refs[:-2], refs[-2:]
    count = own_ref.shape[0]
    for out_ref, who in ((own_ref, core_ref[0]), (other_ref, 1 - core_ref[0])):
        lines = pl.ds(pl.multiple_of(who * count, count), count)
        total = terms[0][lines, :].astype(jnp.float32)
        for term in terms[1:]:
            total += term[lines, :].astype(jnp.float32)
        out_ref[...] = total.astype(jnp.bfloat16)


def add_terms(core, terms):
    rows, width = terms[0].shape
    out = jax.ShapeDtypeStruct((rows // CORES, width), jnp.bfloat16)
    return pl.pallas_call(
        add_kernel,
        out_shape=[out, out],
        in_specs=[SMEM] + [VMEM] * len(terms),
        out_specs=[VMEM, VMEM],
        compiler_params=PARAMS,
    )(core, *terms)


def on_device(n_dp, n_ctx, context, w_key, w_value, queries, offsets, head_gain, w_out):
    chips = n_ctx // CORES
    rows = context.shape[0]
    depth, panel = w_key.shape
    heads = panel // CORES // DH
    lat_count = queries.shape[0]
    me, mine_dp = lax.axis_index("ctx"), lax.axis_index("dp")
    chip, core = me // CORES, lax.rem(me, CORES)
    core_only = core.reshape(1)

    def across(array, bits):
        return lax.ppermute(array, "ctx", [(i, i ^ bits) for i in range(n_ctx)])

    def over_dp(array, bits):
        return lax.ppermute(array, "dp", [(d, d ^ bits) for d in range(n_dp)])

    def after(array, *others):
        return lax.optimization_barrier((array, others))[0]

    near_first = sorted(range(1, chips), key=lambda j: (j.bit_count(), -j))
    own_part, other_part = pack(core_only, w_key, w_value, queries)
    pairs = [None] * chips
    for j in near_first:
        if j & (j - 1) == 0:
            pairs[j] = (across(own_part, CORES * j), across(other_part, CORES * j + 1))
    context_sibling = across(after(context, own_part), 1)
    pairs[0] = (own_part, across(after(other_part, context_sibling), 1))

    places = jnp.stack(
        [(chip ^ j) * CORES + who for j in range(chips) for who in (core, 1 - core)]
    ).astype(jnp.int32)
    starts = places * depth
    first_acc, _ = project(starts[:CORES], context, context_sibling, pairs[0], None, depth)
    for j in near_first:
        low = j & -j
        if j != low:
            held, near = pairs[j ^ low], pairs[1]
            pairs[j] = (
                across(after(held[0], near[0]), CORES * low),
                across(after(held[1], near[1], first_acc), CORES * low),
            )
    blocks = [part for pair in pairs for part in pair]
    last = CORES * (chips - 1)
    acc, slices = project(
        starts[CORES:], context, context_sibling, blocks[CORES:last], first_acc, depth
    )
    firsts = jnp.stack([me * rows, (me ^ 1) * rows]).astype(jnp.int32)
    groups = tuple((CORES * z, CORES * z + 1) for z in range(chips))
    slot_groups = (chip ^ jnp.arange(chips)).astype(jnp.int32)
    messages = attend(
        firsts, slot_groups, places, slices, blocks, acc, offsets, groups, heads, depth
    )
    arrived = [messages[0]] + [across(messages[j], CORES * j) for j in range(1, chips)]
    shards = [after(w_out, acc)] + [None] * (chips - 1)
    for j in near_first:
        low = j & -j
        shard = shards[j ^ low]
        shards[j] = across(shard if j == low else after(shard, messages[0]), CORES * low)
    normed = combine(core_only, arrived, head_gain.reshape(1, panel), heads)

    terms = output_terms(
        jnp.stack([mine_dp ^ chip, core]).astype(jnp.int32), normed, across(normed, 1), shards
    )
    terms = [terms[0]] + [over_dp(terms[i], i) for i in range(1, n_dp)]
    mine, other = add_terms(core_only, terms)
    theirs = across(other, 1)
    return jnp.where(
        core == 0, jnp.concatenate([mine, theirs], axis=1), jnp.concatenate([theirs, mine], axis=1)
    )


def solution(mesh):
    n_dp, n_ctx = mesh.shape["dp"], mesh.shape["ctx"]
    placed = (
        P("ctx", None),
        P("ctx", "dp"),
        P("ctx", "dp"),
        P("ctx", "dp"),
        P(),
        P("dp"),
        P("dp", "ctx"),
    )

    def body(*args):
        return on_device(n_dp, n_ctx, *args)

    return jax.shard_map(
        body, mesh=mesh, in_specs=placed, out_specs=P("ctx", "dp"), check_vma=False
    )
```

```python
import functools
import math

import jax
import jax.numpy as jnp
from jax import lax
from jax.experimental import pallas as pl
from jax.experimental.pallas import tpu as pltpu
from jax.sharding import PartitionSpec as P

DH = 128
NEGATIVE = -1e30
CORES = 2
STATS = 16
VMEM = pl.BlockSpec(memory_space=pltpu.VMEM)
SMEM = pl.BlockSpec(memory_space=pltpu.SMEM)
ANY = pl.BlockSpec(memory_space=pl.ANY)
PARAMS = pltpu.CompilerParams(vmem_limit_bytes=40 * 2**20)
WIDE = pltpu.CompilerParams(vmem_limit_bytes=60 * 2**20)


def three_parts(value):
    high = value.astype(jnp.bfloat16).astype(jnp.float32)
    rest = value - high
    middle = rest.astype(jnp.bfloat16).astype(jnp.float32)
    low = (rest - middle).astype(jnp.bfloat16).astype(jnp.float32)
    return [high, middle, low]


def start_slices(starts_ref, skip, contexts, buffer, sems, count, depth):
    copies = []
    for b in range(count):
        first = pl.multiple_of(starts_ref[skip + b], DH)
        for which in range(CORES):
            slot = b * CORES + which
            copies.append(
                pltpu.make_async_copy(
                    contexts[which].at[:, pl.ds(first, depth)], buffer.at[slot],
                    sems.at[skip * CORES + slot],
                )
            )
    for copy in copies:
        copy.start()
    return copies


def add_products(copies, buffer, blocks, acc_ref, rows, depth, fresh):
    for b, block in enumerate(blocks):
        for which in range(CORES):
            slot = b * CORES + which
            if copies is not None:
                copies[slot].wait()
            product = jnp.dot(buffer[slot], block[:depth, :], preferred_element_type=jnp.float32)
            place = slice(which * rows, (which + 1) * rows)
            if fresh and b == 0:
                acc_ref[place, :] = product
            else:
                acc_ref[place, :] += product


def project_kernel(count, extra, has_acc, depth, *refs):
    starts_ref, own_ref, sibling_ref = refs[:3]
    blocks = refs[3 : 3 + count]
    acc_in = refs[3 + count] if has_acc else None
    acc_ref, later_ref, buffer, sems = refs[-4:]
    contexts = (own_ref, sibling_ref)
    copies = start_slices(starts_ref, 0, contexts, buffer, sems, count, depth)
    later = start_slices(starts_ref, count, contexts, later_ref, sems, extra, depth)
    if has_acc:
        acc_ref[...] = acc_in[...]
    add_products(copies, buffer, blocks, acc_ref, own_ref.shape[0], depth, not has_acc)
    for copy in later:
        copy.wait()


def project(starts, own, sibling, blocks, acc, depth):
    count, extra = len(blocks), starts.shape[0] - len(blocks)
    rows = own.shape[0]
    width = blocks[0].shape[1]
    operands = [starts, own, sibling, *blocks] + ([acc] if acc is not None else [])
    return pl.pallas_call(
        functools.partial(project_kernel, count, extra, acc is not None, depth),
        out_shape=[
            jax.ShapeDtypeStruct((CORES * rows, width), jnp.float32),
            jax.ShapeDtypeStruct((max(extra, 1) * CORES, rows if extra else 16, depth), own.dtype),
        ],
        in_specs=[SMEM, ANY, ANY] + [VMEM] * (len(operands) - 3),
        out_specs=[VMEM, VMEM],
        scratch_shapes=[
            pltpu.VMEM((count * CORES, rows, depth), own.dtype),
            pltpu.SemaphoreType.DMA(((count + extra) * CORES,)),
        ],
        compiler_params=PARAMS,
        cost_estimate=pl.CostEstimate(
            flops=2 * count * CORES * rows * depth * width,
            bytes_accessed=2 * count * CORES * rows * depth,
            transcendentals=0,
        ),
    )(*operands)


def attend_kernel(count, heads, depth, groups, slots, *refs):
    firsts_ref, slots_ref, places_ref, slices_ref = refs[:4]
    blocks = refs[4 : 4 + count]
    acc_in, offsets_ref = refs[4 + count : 6 + count]
    messages = refs[6 + count : 6 + count + slots]
    acc_ref, query_ref, group_ref = refs[6 + count + slots :]
    rows = slices_ref.shape[1]
    half = heads * DH
    lines = blocks[0].shape[0] - depth
    acc_ref[...] = acc_in[...]
    for b, block in enumerate(blocks):
        query_ref[places_ref[b], :lines, :] = block[depth:, :half]
        query_ref[places_ref[b], lines:, :] = block[depth:, half:]
    add_products(None, slices_ref, blocks[-CORES:], acc_ref, rows, depth, False)
    score_scale = 1.0 / math.sqrt(DH)
    line = lax.broadcasted_iota(jnp.int32, (CORES * rows, 1), 0)
    positions = jnp.where(line < rows, firsts_ref[0] + line, firsts_ref[1] + line - rows)
    for h in range(heads):
        keys = acc_ref[:, h * DH : (h + 1) * DH].astype(jnp.bfloat16)
        values = acc_ref[:, half + h * DH : half + (h + 1) * DH].T.astype(jnp.bfloat16)
        for g, members in enumerate(groups):
            query = jnp.concatenate(
                [query_ref[c, :, h * DH : (h + 1) * DH] for c in members], axis=0
            )
            scores = lax.dot_general(
                keys, query, (((1,), (1,)), ((), ())), preferred_element_type=jnp.float32
            ) * score_scale
            live = positions <= offsets_ref[g : g + 1, :]
            masked = jnp.where(live, scores, NEGATIVE)
            peak = jnp.max(masked, axis=0, keepdims=True)
            weights = jnp.where(live, jnp.exp(masked - peak), 0.0).astype(jnp.bfloat16)
            total = jnp.sum(weights.astype(jnp.float32), axis=0, keepdims=True)
            numerator = jnp.dot(values, weights, preferred_element_type=jnp.float32)
            stats = three_parts(peak) + three_parts(total)
            stats.append(jnp.zeros((STATS - len(stats), peak.shape[1]), jnp.float32))
            base = h * (DH + STATS)
            group_ref[g, base : base + DH, :] = numerator.astype(jnp.bfloat16)
            group_ref[g, base + DH : base + DH + STATS, :] = jnp.concatenate(
                stats, axis=0
            ).astype(jnp.bfloat16)
    for m in range(slots):
        messages[m][...] = group_ref[slots_ref[m]]


def attend(firsts, slot_groups, places, slices, blocks, acc, offsets, groups, heads, depth):
    count, slots = len(blocks), slot_groups.shape[0]
    rows, width = slices.shape[1], blocks[0].shape[1]
    lat_count = 2 * (blocks[0].shape[0] - depth)
    group = lat_count * len(groups[0])
    length = heads * (DH + STATS)
    group_offsets = jnp.stack(
        [
            jnp.concatenate([offsets[c * lat_count : (c + 1) * lat_count] for c in members])
            for members in groups
        ]
    )
    return pl.pallas_call(
        functools.partial(attend_kernel, count, heads, depth, groups, slots),
        out_shape=[jax.ShapeDtypeStruct((length, group), jnp.bfloat16)] * slots,
        in_specs=[SMEM] * 3 + [VMEM] * (count + 3),
        out_specs=[VMEM] * slots,
        scratch_shapes=[
            pltpu.VMEM((CORES * rows, width), jnp.float32),
            pltpu.VMEM((count, lat_count, heads * DH), jnp.bfloat16),
            pltpu.VMEM((len(groups), length, group), jnp.bfloat16),
        ],
        compiler_params=PARAMS,
        cost_estimate=pl.CostEstimate(
            flops=8 * CORES * rows * group * len(groups) * heads * DH,
            bytes_accessed=2 * CORES * CORES * rows * depth,
            transcendentals=CORES * rows * group * len(groups) * heads,
        ),
    )(firsts, slot_groups, places, slices, *blocks, acc, group_offsets)


def normed_head(messages, base):
    peaks, totals = [], []
    for message in messages:
        stats = message[base + DH : base + DH + STATS, :].astype(jnp.float32)
        peaks.append(stats[0:1] + stats[1:2] + stats[2:3])
        totals.append(stats[3:4] + stats[4:5] + stats[5:6])
    top = functools.reduce(jnp.maximum, peaks)
    total, numerator = 0.0, 0.0
    for message, peak, part in zip(messages, peaks, totals):
        scale = jnp.exp(peak - top)
        total += part * scale
        numerator += message[base : base + DH, :].astype(jnp.float32) * scale
    attended = numerator / total
    mean_square = jnp.mean(attended * attended, axis=0, keepdims=True)
    return (attended * lax.rsqrt(mean_square + 1e-05)).T


def combine_kernel(heads, core_ref, *refs):
    messages, gain_ref, out_ref = refs[:-2], refs[-2], refs[-1]
    half = out_ref.shape[1]
    for h in range(heads):
        place = pl.ds(pl.multiple_of(core_ref[0] * half, DH) + h * DH, DH)
        normed = normed_head(messages, h * (DH + STATS))
        normed = normed * gain_ref[:, place].astype(jnp.float32)
        out_ref[:, h * DH : (h + 1) * DH] = normed.astype(jnp.bfloat16)


def combine(core, messages, gain, heads):
    return pl.pallas_call(
        functools.partial(combine_kernel, heads),
        out_shape=jax.ShapeDtypeStruct((messages[0].shape[1], heads * DH), jnp.bfloat16),
        in_specs=[SMEM] + [VMEM] * (len(messages) + 1),
        out_specs=VMEM,
        compiler_params=PARAMS,
    )(core, *messages, gain)


def pack_kernel(core_ref, key_ref, value_ref, query_ref, own_ref, other_ref, sems):
    depth, half = key_ref.shape[0], key_ref.shape[1] // CORES
    lines = query_ref.shape[0] // 2
    copies = []
    for out_ref, who in ((own_ref, core_ref[0]), (other_ref, 1 - core_ref[0])):
        place = pl.ds(pl.multiple_of(who * half, DH), half)
        for source, target in (
            (key_ref.at[:, place], out_ref.at[pl.ds(0, depth), pl.ds(0, half)]),
            (value_ref.at[:, place], out_ref.at[pl.ds(0, depth), pl.ds(half, half)]),
            (query_ref.at[pl.ds(0, lines), place], out_ref.at[pl.ds(depth, lines), pl.ds(0, half)]),
            (query_ref.at[pl.ds(lines, lines), place], out_ref.at[pl.ds(depth, lines), pl.ds(half, half)]),
        ):
            copies.append(pltpu.make_async_copy(source, target, sems.at[len(copies)]))
            copies[-1].start()
    for copy in copies:
        copy.wait()


def pack(core, w_key, w_value, queries):
    depth, panel = w_key.shape
    out = jax.ShapeDtypeStruct((depth + queries.shape[0] // 2, panel), w_key.dtype)
    return pl.pallas_call(
        pack_kernel,
        out_shape=[out, out],
        in_specs=[SMEM, ANY, ANY, ANY],
        out_specs=[VMEM, VMEM],
        scratch_shapes=[pltpu.SemaphoreType.DMA((8,))],
        compiler_params=WIDE,
    )(core, w_key, w_value, queries)


def output_kernel(place_ref, own_ref, sibling_ref, *refs):
    chips = (len(refs) - 1) // 2
    weights, terms, result = refs[:chips], refs[chips:-1], refs[-1]
    half = own_ref.shape[1]
    mine = pl.ds(pl.multiple_of(place_ref[1] * half, DH), half)
    other = pl.ds(pl.multiple_of((1 - place_ref[1]) * half, DH), half)
    own, sibling = own_ref[...], sibling_ref[...]
    for j, w_ref in enumerate(weights):
        total = jnp.dot(own, w_ref[mine, :], preferred_element_type=jnp.float32)
        total += jnp.dot(sibling, w_ref[other, :], preferred_element_type=jnp.float32)
        result[j] = total.astype(jnp.bfloat16)
    for i, term in enumerate(terms):
        term[...] = result[place_ref[0] ^ i]


def output_terms(place, own, sibling, weights):
    chips, shape = len(weights), (own.shape[0], weights[0].shape[1])
    return pl.pallas_call(
        output_kernel,
        out_shape=[jax.ShapeDtypeStruct(shape, jnp.bfloat16)] * chips,
        in_specs=[SMEM] + [VMEM] * (2 + chips),
        out_specs=[VMEM] * chips,
        scratch_shapes=[pltpu.VMEM((chips, *shape), jnp.bfloat16)],
        compiler_params=PARAMS,
    )(place, own, sibling, *weights)


def add_kernel(core_ref, *refs):
    terms, (own_ref, other_ref) = refs[:-2], refs[-2:]
    count = own_ref.shape[0]
    for out_ref, who in ((own_ref, core_ref[0]), (other_ref, 1 - core_ref[0])):
        lines = pl.ds(pl.multiple_of(who * count, count), count)
        total = terms[0][lines, :].astype(jnp.float32)
        for term in terms[1:]:
            total += term[lines, :].astype(jnp.float32)
        out_ref[...] = total.astype(jnp.bfloat16)


def add_terms(core, terms):
    rows, width = terms[0].shape
    out = jax.ShapeDtypeStruct((rows // CORES, width), jnp.bfloat16)
    return pl.pallas_call(
        add_kernel,
        out_shape=[out, out],
        in_specs=[SMEM] + [VMEM] * len(terms),
        out_specs=[VMEM, VMEM],
        compiler_params=PARAMS,
    )(core, *terms)


def on_device(n_dp, n_ctx, context, w_key, w_value, queries, offsets, head_gain, w_out):
    chips = n_ctx // CORES
    rows = context.shape[0]
    depth, panel = w_key.shape
    heads = panel // CORES // DH
    lat_count = queries.shape[0]
    me, mine_dp = lax.axis_index("ctx"), lax.axis_index("dp")
    chip, core = me // CORES, lax.rem(me, CORES)
    core_only = core.reshape(1)

    def across(array, bits):
        return lax.ppermute(array, "ctx", [(i, i ^ bits) for i in range(n_ctx)])

    def over_dp(array, bits):
        return lax.ppermute(array, "dp", [(d, d ^ bits) for d in range(n_dp)])

    def after(array, *others):
        return lax.optimization_barrier((array, others))[0]

    near_first = sorted(range(1, chips), key=lambda j: (j.bit_count(), -j))
    own_part, other_part = pack(core_only, w_key, w_value, queries)
    pairs = [None] * chips
    for j in near_first:
        if j & (j - 1) == 0:
            pairs[j] = (across(own_part, CORES * j), across(other_part, CORES * j + 1))
    context_sibling = across(after(context, own_part), 1)
    pairs[0] = (own_part, across(after(other_part, context_sibling), 1))

    places = jnp.stack(
        [(chip ^ j) * CORES + who for j in range(chips) for who in (core, 1 - core)]
    ).astype(jnp.int32)
    starts = places * depth
    first_acc, _ = project(starts[:CORES], context, context_sibling, pairs[0], None, depth)
    for j in near_first:
        low = j & -j
        if j != low:
            held, near = pairs[j ^ low], pairs[1]
            pairs[j] = (
                across(after(held[0], near[0]), CORES * low),
                across(after(held[1], near[1], first_acc), CORES * low),
            )
    blocks = [part for pair in pairs for part in pair]
    last = CORES * (chips - 1)
    acc, slices = project(
        starts[CORES:], context, context_sibling, blocks[CORES:last], first_acc, depth
    )
    firsts = jnp.stack([me * rows, (me ^ 1) * rows]).astype(jnp.int32)
    groups = tuple((CORES * z, CORES * z + 1) for z in range(chips))
    slot_groups = (chip ^ jnp.arange(chips)).astype(jnp.int32)
    messages = attend(
        firsts, slot_groups, places, slices, blocks, acc, offsets, groups, heads, depth
    )
    arrived = [messages[0]] + [across(messages[j], CORES * j) for j in range(1, chips)]
    shards = [after(w_out, *pairs[1], *pairs[2])] + [None] * (chips - 1)
    for j in near_first:
        low = j & -j
        shard = shards[j ^ low]
        shards[j] = across(shard if j == low else after(shard, messages[0]), CORES * low)
    normed = combine(core_only, arrived, head_gain.reshape(1, panel), heads)

    terms = output_terms(
        jnp.stack([mine_dp ^ chip, core]).astype(jnp.int32), normed, across(normed, 1), shards
    )
    terms = [terms[0]] + [over_dp(terms[i], i) for i in range(1, n_dp)]
    mine, other = add_terms(core_only, terms)
    theirs = across(other, 1)
    return jnp.where(
        core == 0, jnp.concatenate([mine, theirs], axis=1), jnp.concatenate([theirs, mine], axis=1)
    )


def solution(mesh):
    n_dp, n_ctx = mesh.shape["dp"], mesh.shape["ctx"]
    placed = (
        P("ctx", None),
        P("ctx", "dp"),
        P("ctx", "dp"),
        P("ctx", "dp"),
        P(),
        P("dp"),
        P("dp", "ctx"),
    )

    def body(*args):
        return on_device(n_dp, n_ctx, *args)

    return jax.shard_map(
        body, mesh=mesh, in_specs=placed, out_specs=P("ctx", "dp"), check_vma=False
    )
```

```python
import functools
import math

import jax
import jax.numpy as jnp
from jax import lax
from jax.experimental import pallas as pl
from jax.experimental.pallas import tpu as pltpu
from jax.sharding import PartitionSpec as P

DH = 128
NEGATIVE = -1e30
CORES = 2
STATS = 16
VMEM = pl.BlockSpec(memory_space=pltpu.VMEM)
SMEM = pl.BlockSpec(memory_space=pltpu.SMEM)
ANY = pl.BlockSpec(memory_space=pl.ANY)
PARAMS = pltpu.CompilerParams(vmem_limit_bytes=40 * 2**20)
WIDE = pltpu.CompilerParams(vmem_limit_bytes=60 * 2**20)


def three_parts(value):
    high = value.astype(jnp.bfloat16).astype(jnp.float32)
    rest = value - high
    middle = rest.astype(jnp.bfloat16).astype(jnp.float32)
    low = (rest - middle).astype(jnp.bfloat16).astype(jnp.float32)
    return [high, middle, low]


def start_slices(starts_ref, skip, contexts, buffer, sems, count, depth):
    copies = []
    for b in range(count):
        first = pl.multiple_of(starts_ref[skip + b], DH)
        for which in range(CORES):
            slot = b * CORES + which
            copies.append(
                pltpu.make_async_copy(
                    contexts[which].at[:, pl.ds(first, depth)], buffer.at[slot],
                    sems.at[skip * CORES + slot],
                )
            )
    for copy in copies:
        copy.start()
    return copies


def add_products(copies, buffer, blocks, acc_ref, rows, depth, fresh):
    for b, block in enumerate(blocks):
        for which in range(CORES):
            slot = b * CORES + which
            if copies is not None:
                copies[slot].wait()
            product = jnp.dot(buffer[slot], block[:depth, :], preferred_element_type=jnp.float32)
            place = slice(which * rows, (which + 1) * rows)
            if fresh and b == 0:
                acc_ref[place, :] = product
            else:
                acc_ref[place, :] += product


def project_kernel(count, extra, has_acc, depth, *refs):
    starts_ref, own_ref, sibling_ref = refs[:3]
    blocks = refs[3 : 3 + count]
    acc_in = refs[3 + count] if has_acc else None
    acc_ref, later_ref, buffer, sems = refs[-4:]
    contexts = (own_ref, sibling_ref)
    copies = start_slices(starts_ref, 0, contexts, buffer, sems, count, depth)
    later = start_slices(starts_ref, count, contexts, later_ref, sems, extra, depth)
    if has_acc:
        acc_ref[...] = acc_in[...]
    add_products(copies, buffer, blocks, acc_ref, own_ref.shape[0], depth, not has_acc)
    for copy in later:
        copy.wait()


def project(starts, own, sibling, blocks, acc, depth):
    count, extra = len(blocks), starts.shape[0] - len(blocks)
    rows = own.shape[0]
    width = blocks[0].shape[1]
    operands = [starts, own, sibling, *blocks] + ([acc] if acc is not None else [])
    return pl.pallas_call(
        functools.partial(project_kernel, count, extra, acc is not None, depth),
        out_shape=[
            jax.ShapeDtypeStruct((CORES * rows, width), jnp.float32),
            jax.ShapeDtypeStruct((max(extra, 1) * CORES, rows if extra else 16, depth), own.dtype),
        ],
        in_specs=[SMEM, ANY, ANY] + [VMEM] * (len(operands) - 3),
        out_specs=[VMEM, VMEM],
        scratch_shapes=[
            pltpu.VMEM((count * CORES, rows, depth), own.dtype),
            pltpu.SemaphoreType.DMA(((count + extra) * CORES,)),
        ],
        compiler_params=PARAMS,
        cost_estimate=pl.CostEstimate(
            flops=2 * count * CORES * rows * depth * width,
            bytes_accessed=2 * count * CORES * rows * depth,
            transcendentals=0,
        ),
    )(*operands)


def attend_kernel(count, heads, depth, groups, slots, *refs):
    firsts_ref, slots_ref, places_ref, slices_ref = refs[:4]
    blocks = refs[4 : 4 + count]
    acc_in, offsets_ref = refs[4 + count : 6 + count]
    messages = refs[6 + count : 6 + count + slots]
    acc_ref, query_ref, group_ref = refs[6 + count + slots :]
    rows = slices_ref.shape[1]
    half = heads * DH
    lines = blocks[0].shape[0] - depth
    acc_ref[...] = acc_in[...]
    for b, block in enumerate(blocks):
        query_ref[places_ref[b], :lines, :] = block[depth:, :half]
        query_ref[places_ref[b], lines:, :] = block[depth:, half:]
    add_products(None, slices_ref, blocks[-CORES:], acc_ref, rows, depth, False)
    score_scale = 1.0 / math.sqrt(DH)
    line = lax.broadcasted_iota(jnp.int32, (CORES * rows, 1), 0)
    positions = jnp.where(line < rows, firsts_ref[0] + line, firsts_ref[1] + line - rows)
    for h in range(heads):
        keys = acc_ref[:, h * DH : (h + 1) * DH].astype(jnp.bfloat16)
        values = acc_ref[:, half + h * DH : half + (h + 1) * DH].T.astype(jnp.bfloat16)
        for g, members in enumerate(groups):
            query = jnp.concatenate(
                [query_ref[c, :, h * DH : (h + 1) * DH] for c in members], axis=0
            )
            scores = lax.dot_general(
                keys, query, (((1,), (1,)), ((), ())), preferred_element_type=jnp.float32
            ) * score_scale
            live = positions <= offsets_ref[g : g + 1, :]
            masked = jnp.where(live, scores, NEGATIVE)
            peak = jnp.max(masked, axis=0, keepdims=True)
            weights = jnp.where(live, jnp.exp(masked - peak), 0.0).astype(jnp.bfloat16)
            total = jnp.sum(weights.astype(jnp.float32), axis=0, keepdims=True)
            numerator = jnp.dot(values, weights, preferred_element_type=jnp.float32)
            stats = three_parts(peak) + three_parts(total)
            stats.append(jnp.zeros((STATS - len(stats), peak.shape[1]), jnp.float32))
            base = h * (DH + STATS)
            group_ref[g, base : base + DH, :] = numerator.astype(jnp.bfloat16)
            group_ref[g, base + DH : base + DH + STATS, :] = jnp.concatenate(
                stats, axis=0
            ).astype(jnp.bfloat16)
    for m in range(slots):
        messages[m][...] = group_ref[slots_ref[m]]


def attend(firsts, slot_groups, places, slices, blocks, acc, offsets, groups, heads, depth):
    count, slots = len(blocks), slot_groups.shape[0]
    rows, width = slices.shape[1], blocks[0].shape[1]
    lat_count = 2 * (blocks[0].shape[0] - depth)
    group = lat_count * len(groups[0])
    length = heads * (DH + STATS)
    group_offsets = jnp.stack(
        [
            jnp.concatenate([offsets[c * lat_count : (c + 1) * lat_count] for c in members])
            for members in groups
        ]
    )
    return pl.pallas_call(
        functools.partial(attend_kernel, count, heads, depth, groups, slots),
        out_shape=[jax.ShapeDtypeStruct((length, group), jnp.bfloat16)] * slots,
        in_specs=[SMEM] * 3 + [VMEM] * (count + 3),
        out_specs=[VMEM] * slots,
        scratch_shapes=[
            pltpu.VMEM((CORES * rows, width), jnp.float32),
            pltpu.VMEM((count, lat_count, heads * DH), jnp.bfloat16),
            pltpu.VMEM((len(groups), length, group), jnp.bfloat16),
        ],
        compiler_params=PARAMS,
        cost_estimate=pl.CostEstimate(
            flops=8 * CORES * rows * group * len(groups) * heads * DH,
            bytes_accessed=2 * CORES * CORES * rows * depth,
            transcendentals=CORES * rows * group * len(groups) * heads,
        ),
    )(firsts, slot_groups, places, slices, *blocks, acc, group_offsets)


def normed_head(messages, base):
    peaks, totals = [], []
    for message in messages:
        stats = message[base + DH : base + DH + STATS, :].astype(jnp.float32)
        peaks.append(stats[0:1] + stats[1:2] + stats[2:3])
        totals.append(stats[3:4] + stats[4:5] + stats[5:6])
    top = functools.reduce(jnp.maximum, peaks)
    total, numerator = 0.0, 0.0
    for message, peak, part in zip(messages, peaks, totals):
        scale = jnp.exp(peak - top)
        total += part * scale
        numerator += message[base : base + DH, :].astype(jnp.float32) * scale
    attended = numerator / total
    mean_square = jnp.mean(attended * attended, axis=0, keepdims=True)
    return (attended * lax.rsqrt(mean_square + 1e-05)).T


def combine_kernel(heads, core_ref, *refs):
    messages, gain_ref, out_ref = refs[:-2], refs[-2], refs[-1]
    half = out_ref.shape[1]
    for h in range(heads):
        place = pl.ds(pl.multiple_of(core_ref[0] * half, DH) + h * DH, DH)
        normed = normed_head(messages, h * (DH + STATS))
        normed = normed * gain_ref[:, place].astype(jnp.float32)
        out_ref[:, h * DH : (h + 1) * DH] = normed.astype(jnp.bfloat16)


def combine(core, messages, gain, heads):
    return pl.pallas_call(
        functools.partial(combine_kernel, heads),
        out_shape=jax.ShapeDtypeStruct((messages[0].shape[1], heads * DH), jnp.bfloat16),
        in_specs=[SMEM] + [VMEM] * (len(messages) + 1),
        out_specs=VMEM,
        compiler_params=PARAMS,
    )(core, *messages, gain)


def pack_kernel(core_ref, key_ref, value_ref, query_ref, own_ref, other_ref, sems):
    depth, half = key_ref.shape[0], key_ref.shape[1] // CORES
    lines = query_ref.shape[0] // 2
    copies = []
    for out_ref, who in ((own_ref, core_ref[0]), (other_ref, 1 - core_ref[0])):
        place = pl.ds(pl.multiple_of(who * half, DH), half)
        for source, target in (
            (key_ref.at[:, place], out_ref.at[pl.ds(0, depth), pl.ds(0, half)]),
            (value_ref.at[:, place], out_ref.at[pl.ds(0, depth), pl.ds(half, half)]),
            (query_ref.at[pl.ds(0, lines), place], out_ref.at[pl.ds(depth, lines), pl.ds(0, half)]),
            (query_ref.at[pl.ds(lines, lines), place], out_ref.at[pl.ds(depth, lines), pl.ds(half, half)]),
        ):
            copies.append(pltpu.make_async_copy(source, target, sems.at[len(copies)]))
            copies[-1].start()
    for copy in copies:
        copy.wait()


def pack(core, w_key, w_value, queries):
    depth, panel = w_key.shape
    out = jax.ShapeDtypeStruct((depth + queries.shape[0] // 2, panel), w_key.dtype)
    return pl.pallas_call(
        pack_kernel,
        out_shape=[out, out],
        in_specs=[SMEM, ANY, ANY, ANY],
        out_specs=[VMEM, VMEM],
        scratch_shapes=[pltpu.SemaphoreType.DMA((8,))],
        compiler_params=WIDE,
    )(core, w_key, w_value, queries)


def output_kernel(place_ref, own_ref, sibling_ref, *refs):
    chips = (len(refs) - 1) // 2
    weights, terms, result = refs[:chips], refs[chips:-1], refs[-1]
    half = own_ref.shape[1]
    mine = pl.ds(pl.multiple_of(place_ref[1] * half, DH), half)
    other = pl.ds(pl.multiple_of((1 - place_ref[1]) * half, DH), half)
    own, sibling = own_ref[...], sibling_ref[...]
    for j, w_ref in enumerate(weights):
        total = jnp.dot(own, w_ref[mine, :], preferred_element_type=jnp.float32)
        total += jnp.dot(sibling, w_ref[other, :], preferred_element_type=jnp.float32)
        result[j] = total.astype(jnp.bfloat16)
    for i, term in enumerate(terms):
        term[...] = result[place_ref[0] ^ i]


def output_terms(place, own, sibling, weights):
    chips, shape = len(weights), (own.shape[0], weights[0].shape[1])
    return pl.pallas_call(
        output_kernel,
        out_shape=[jax.ShapeDtypeStruct(shape, jnp.bfloat16)] * chips,
        in_specs=[SMEM] + [VMEM] * (2 + chips),
        out_specs=[VMEM] * chips,
        scratch_shapes=[pltpu.VMEM((chips, *shape), jnp.bfloat16)],
        compiler_params=PARAMS,
    )(place, own, sibling, *weights)


def add_kernel(core_ref, *refs):
    terms, (own_ref, other_ref) = refs[:-2], refs[-2:]
    count = own_ref.shape[0]
    for out_ref, who in ((own_ref, core_ref[0]), (other_ref, 1 - core_ref[0])):
        lines = pl.ds(pl.multiple_of(who * count, count), count)
        total = terms[0][lines, :].astype(jnp.float32)
        for term in terms[1:]:
            total += term[lines, :].astype(jnp.float32)
        out_ref[...] = total.astype(jnp.bfloat16)


def add_terms(core, terms):
    rows, width = terms[0].shape
    out = jax.ShapeDtypeStruct((rows // CORES, width), jnp.bfloat16)
    return pl.pallas_call(
        add_kernel,
        out_shape=[out, out],
        in_specs=[SMEM] + [VMEM] * len(terms),
        out_specs=[VMEM, VMEM],
        compiler_params=PARAMS,
    )(core, *terms)


def on_device(n_dp, n_ctx, context, w_key, w_value, queries, offsets, head_gain, w_out):
    chips = n_ctx // CORES
    rows = context.shape[0]
    depth, panel = w_key.shape
    heads = panel // CORES // DH
    lat_count = queries.shape[0]
    me, mine_dp = lax.axis_index("ctx"), lax.axis_index("dp")
    chip, core = me // CORES, lax.rem(me, CORES)
    core_only = core.reshape(1)

    def across(array, bits):
        return lax.ppermute(array, "ctx", [(i, i ^ bits) for i in range(n_ctx)])

    def over_dp(array, bits):
        return lax.ppermute(array, "dp", [(d, d ^ bits) for d in range(n_dp)])

    def after(array, *others):
        return lax.optimization_barrier((array, others))[0]

    near_first = sorted(range(1, chips), key=lambda j: (j.bit_count(), -j))
    own_part, other_part = pack(core_only, w_key, w_value, queries)
    pairs = [None] * chips
    for j in near_first:
        if j & (j - 1) == 0:
            pairs[j] = (across(own_part, CORES * j), across(other_part, CORES * j + 1))
    context_sibling = across(after(context, own_part), 1)
    pairs[0] = (own_part, across(after(other_part, context_sibling), 1))

    places = jnp.stack(
        [(chip ^ j) * CORES + who for j in range(chips) for who in (core, 1 - core)]
    ).astype(jnp.int32)
    starts = places * depth
    first_acc, _ = project(starts[:CORES], context, context_sibling, pairs[0], None, depth)
    for j in near_first:
        low = j & -j
        if j != low:
            held, near = pairs[j ^ low], pairs[1]
            pairs[j] = (
                across(after(held[0], near[0]), CORES * low),
                across(after(held[1], near[1], first_acc), CORES * low),
            )
    blocks = [part for pair in pairs for part in pair]
    last = CORES * (chips - 1)
    acc, slices = project(
        starts[CORES:], context, context_sibling, blocks[CORES:last], first_acc, depth
    )
    firsts = jnp.stack([me * rows, (me ^ 1) * rows]).astype(jnp.int32)
    groups = tuple((CORES * z, CORES * z + 1) for z in range(chips))
    slot_groups = (chip ^ jnp.arange(chips)).astype(jnp.int32)
    messages = attend(
        firsts, slot_groups, places, slices, blocks, acc, offsets, groups, heads, depth
    )
    arrived = [messages[0]] + [across(messages[j], CORES * j) for j in range(1, chips)]
    shards = [after(w_out, first_acc, *pairs[1], *pairs[2])] + [None] * (chips - 1)
    for j in near_first:
        low = j & -j
        shard = shards[j ^ low]
        shards[j] = across(shard if j == low else after(shard, acc, *pairs[-1]), CORES * low)
    normed = combine(core_only, arrived, head_gain.reshape(1, panel), heads)

    terms = output_terms(
        jnp.stack([mine_dp ^ chip, core]).astype(jnp.int32), normed, across(normed, 1), shards
    )
    terms = [terms[0]] + [over_dp(terms[i], i) for i in range(1, n_dp)]
    mine, other = add_terms(core_only, terms)
    theirs = across(other, 1)
    return jnp.where(
        core == 0, jnp.concatenate([mine, theirs], axis=1), jnp.concatenate([theirs, mine], axis=1)
    )


def solution(mesh):
    n_dp, n_ctx = mesh.shape["dp"], mesh.shape["ctx"]
    placed = (
        P("ctx", None),
        P("ctx", "dp"),
        P("ctx", "dp"),
        P("ctx", "dp"),
        P(),
        P("dp"),
        P("dp", "ctx"),
    )

    def body(*args):
        return on_device(n_dp, n_ctx, *args)

    return jax.shard_map(
        body, mesh=mesh, in_specs=placed, out_specs=P("ctx", "dp"), check_vma=False
    )
```

```python
import functools
import math

import jax
import jax.numpy as jnp
from jax import lax
from jax.experimental import pallas as pl
from jax.experimental.pallas import tpu as pltpu
from jax.sharding import PartitionSpec as P

DH = 128
NEGATIVE = -1e30
CORES = 2
STATS = 16
VMEM = pl.BlockSpec(memory_space=pltpu.VMEM)
SMEM = pl.BlockSpec(memory_space=pltpu.SMEM)
ANY = pl.BlockSpec(memory_space=pl.ANY)
PARAMS = pltpu.CompilerParams(vmem_limit_bytes=40 * 2**20)
WIDE = pltpu.CompilerParams(vmem_limit_bytes=60 * 2**20)


def three_parts(value):
    high = value.astype(jnp.bfloat16).astype(jnp.float32)
    rest = value - high
    middle = rest.astype(jnp.bfloat16).astype(jnp.float32)
    low = (rest - middle).astype(jnp.bfloat16).astype(jnp.float32)
    return [high, middle, low]


def start_slices(starts_ref, skip, contexts, buffer, sems, count, depth):
    copies = []
    for b in range(count):
        first = pl.multiple_of(starts_ref[skip + b], DH)
        for which in range(CORES):
            slot = b * CORES + which
            copies.append(
                pltpu.make_async_copy(
                    contexts[which].at[:, pl.ds(first, depth)], buffer.at[slot],
                    sems.at[skip * CORES + slot],
                )
            )
    for copy in copies:
        copy.start()
    return copies


def add_products(copies, buffer, blocks, acc_ref, rows, depth, fresh):
    for b, block in enumerate(blocks):
        for which in range(CORES):
            slot = b * CORES + which
            if copies is not None:
                copies[slot].wait()
            product = jnp.dot(buffer[slot], block[:depth, :], preferred_element_type=jnp.float32)
            place = slice(which * rows, (which + 1) * rows)
            if fresh and b == 0:
                acc_ref[place, :] = product
            else:
                acc_ref[place, :] += product


def project_kernel(count, extra, has_acc, depth, *refs):
    starts_ref, own_ref, sibling_ref = refs[:3]
    blocks = refs[3 : 3 + count]
    acc_in = refs[3 + count] if has_acc else None
    acc_ref, later_ref, buffer, sems = refs[-4:]
    contexts = (own_ref, sibling_ref)
    copies = start_slices(starts_ref, 0, contexts, buffer, sems, count, depth)
    later = start_slices(starts_ref, count, contexts, later_ref, sems, extra, depth)
    if has_acc:
        acc_ref[...] = acc_in[...]
    add_products(copies, buffer, blocks, acc_ref, own_ref.shape[0], depth, not has_acc)
    for copy in later:
        copy.wait()


def project(starts, own, sibling, blocks, acc, depth):
    count, extra = len(blocks), starts.shape[0] - len(blocks)
    rows = own.shape[0]
    width = blocks[0].shape[1]
    operands = [starts, own, sibling, *blocks] + ([acc] if acc is not None else [])
    return pl.pallas_call(
        functools.partial(project_kernel, count, extra, acc is not None, depth),
        out_shape=[
            jax.ShapeDtypeStruct((CORES * rows, width), jnp.float32),
            jax.ShapeDtypeStruct((max(extra, 1) * CORES, rows if extra else 16, depth), own.dtype),
        ],
        in_specs=[SMEM, ANY, ANY] + [VMEM] * (len(operands) - 3),
        out_specs=[VMEM, VMEM],
        scratch_shapes=[
            pltpu.VMEM((count * CORES, rows, depth), own.dtype),
            pltpu.SemaphoreType.DMA(((count + extra) * CORES,)),
        ],
        compiler_params=PARAMS,
        cost_estimate=pl.CostEstimate(
            flops=2 * count * CORES * rows * depth * width,
            bytes_accessed=2 * count * CORES * rows * depth,
            transcendentals=0,
        ),
    )(*operands)


def attend_kernel(count, heads, depth, groups, slots, *refs):
    firsts_ref, slots_ref, places_ref, slices_ref = refs[:4]
    blocks = refs[4 : 4 + count]
    acc_in, offsets_ref = refs[4 + count : 6 + count]
    messages = refs[6 + count : 6 + count + slots]
    acc_ref, query_ref, group_ref = refs[6 + count + slots :]
    rows = slices_ref.shape[1]
    half = heads * DH
    lines = blocks[0].shape[0] - depth
    acc_ref[...] = acc_in[...]
    for b, block in enumerate(blocks):
        query_ref[places_ref[b], :lines, :] = block[depth:, :half]
        query_ref[places_ref[b], lines:, :] = block[depth:, half:]
    add_products(None, slices_ref, blocks[-CORES:], acc_ref, rows, depth, False)
    score_scale = 1.0 / math.sqrt(DH)
    line = lax.broadcasted_iota(jnp.int32, (CORES * rows, 1), 0)
    positions = jnp.where(line < rows, firsts_ref[0] + line, firsts_ref[1] + line - rows)
    for h in range(heads):
        keys = acc_ref[:, h * DH : (h + 1) * DH].astype(jnp.bfloat16)
        values = acc_ref[:, half + h * DH : half + (h + 1) * DH].T.astype(jnp.bfloat16)
        for g, members in enumerate(groups):
            query = jnp.concatenate(
                [query_ref[c, :, h * DH : (h + 1) * DH] for c in members], axis=0
            )
            scores = lax.dot_general(
                keys, query, (((1,), (1,)), ((), ())), preferred_element_type=jnp.float32
            ) * score_scale
            live = positions <= offsets_ref[g : g + 1, :]
            masked = jnp.where(live, scores, NEGATIVE)
            peak = jnp.max(masked, axis=0, keepdims=True)
            weights = jnp.where(live, jnp.exp(masked - peak), 0.0).astype(jnp.bfloat16)
            total = jnp.sum(weights.astype(jnp.float32), axis=0, keepdims=True)
            numerator = jnp.dot(values, weights, preferred_element_type=jnp.float32)
            stats = three_parts(peak) + three_parts(total)
            stats.append(jnp.zeros((STATS - len(stats), peak.shape[1]), jnp.float32))
            base = h * (DH + STATS)
            group_ref[g, base : base + DH, :] = numerator.astype(jnp.bfloat16)
            group_ref[g, base + DH : base + DH + STATS, :] = jnp.concatenate(
                stats, axis=0
            ).astype(jnp.bfloat16)
    for m in range(slots):
        messages[m][...] = group_ref[slots_ref[m]]


def attend(firsts, slot_groups, places, slices, blocks, acc, offsets, groups, heads, depth):
    count, slots = len(blocks), slot_groups.shape[0]
    rows, width = slices.shape[1], blocks[0].shape[1]
    lat_count = 2 * (blocks[0].shape[0] - depth)
    group = lat_count * len(groups[0])
    length = heads * (DH + STATS)
    group_offsets = jnp.stack(
        [
            jnp.concatenate([offsets[c * lat_count : (c + 1) * lat_count] for c in members])
            for members in groups
        ]
    )
    return pl.pallas_call(
        functools.partial(attend_kernel, count, heads, depth, groups, slots),
        out_shape=[jax.ShapeDtypeStruct((length, group), jnp.bfloat16)] * slots,
        in_specs=[SMEM] * 3 + [VMEM] * (count + 3),
        out_specs=[VMEM] * slots,
        scratch_shapes=[
            pltpu.VMEM((CORES * rows, width), jnp.float32),
            pltpu.VMEM((count, lat_count, heads * DH), jnp.bfloat16),
            pltpu.VMEM((len(groups), length, group), jnp.bfloat16),
        ],
        compiler_params=PARAMS,
        cost_estimate=pl.CostEstimate(
            flops=8 * CORES * rows * group * len(groups) * heads * DH,
            bytes_accessed=2 * CORES * CORES * rows * depth,
            transcendentals=CORES * rows * group * len(groups) * heads,
        ),
    )(firsts, slot_groups, places, slices, *blocks, acc, group_offsets)


def normed_head(messages, base):
    peaks, totals = [], []
    for message in messages:
        stats = message[base + DH : base + DH + STATS, :].astype(jnp.float32)
        peaks.append(stats[0:1] + stats[1:2] + stats[2:3])
        totals.append(stats[3:4] + stats[4:5] + stats[5:6])
    top = functools.reduce(jnp.maximum, peaks)
    total, numerator = 0.0, 0.0
    for message, peak, part in zip(messages, peaks, totals):
        scale = jnp.exp(peak - top)
        total += part * scale
        numerator += message[base : base + DH, :].astype(jnp.float32) * scale
    attended = numerator / total
    mean_square = jnp.mean(attended * attended, axis=0, keepdims=True)
    return (attended * lax.rsqrt(mean_square + 1e-05)).T


def combine_kernel(heads, core_ref, *refs):
    messages, gain_ref, out_ref = refs[:-2], refs[-2], refs[-1]
    half = out_ref.shape[1]
    for h in range(heads):
        place = pl.ds(pl.multiple_of(core_ref[0] * half, DH) + h * DH, DH)
        normed = normed_head(messages, h * (DH + STATS))
        normed = normed * gain_ref[:, place].astype(jnp.float32)
        out_ref[:, h * DH : (h + 1) * DH] = normed.astype(jnp.bfloat16)


def combine(core, messages, gain, heads):
    return pl.pallas_call(
        functools.partial(combine_kernel, heads),
        out_shape=jax.ShapeDtypeStruct((messages[0].shape[1], heads * DH), jnp.bfloat16),
        in_specs=[SMEM] + [VMEM] * (len(messages) + 1),
        out_specs=VMEM,
        compiler_params=PARAMS,
    )(core, *messages, gain)


def pack_kernel(core_ref, key_ref, value_ref, query_ref, own_ref, other_ref, sems):
    depth, half = key_ref.shape[0], key_ref.shape[1] // CORES
    lines = query_ref.shape[0] // 2
    copies = []
    for out_ref, who in ((own_ref, core_ref[0]), (other_ref, 1 - core_ref[0])):
        place = pl.ds(pl.multiple_of(who * half, DH), half)
        for source, target in (
            (key_ref.at[:, place], out_ref.at[pl.ds(0, depth), pl.ds(0, half)]),
            (value_ref.at[:, place], out_ref.at[pl.ds(0, depth), pl.ds(half, half)]),
            (query_ref.at[pl.ds(0, lines), place], out_ref.at[pl.ds(depth, lines), pl.ds(0, half)]),
            (query_ref.at[pl.ds(lines, lines), place], out_ref.at[pl.ds(depth, lines), pl.ds(half, half)]),
        ):
            copies.append(pltpu.make_async_copy(source, target, sems.at[len(copies)]))
            copies[-1].start()
    for copy in copies:
        copy.wait()


def pack(core, w_key, w_value, queries):
    depth, panel = w_key.shape
    out = jax.ShapeDtypeStruct((depth + queries.shape[0] // 2, panel), w_key.dtype)
    return pl.pallas_call(
        pack_kernel,
        out_shape=[out, out],
        in_specs=[SMEM, ANY, ANY, ANY],
        out_specs=[VMEM, VMEM],
        scratch_shapes=[pltpu.SemaphoreType.DMA((8,))],
        compiler_params=WIDE,
    )(core, w_key, w_value, queries)


def output_kernel(place_ref, own_ref, sibling_ref, *refs):
    chips = (len(refs) - 1) // 2
    weights, terms, result = refs[:chips], refs[chips:-1], refs[-1]
    half = own_ref.shape[1]
    mine = pl.ds(pl.multiple_of(place_ref[1] * half, DH), half)
    other = pl.ds(pl.multiple_of((1 - place_ref[1]) * half, DH), half)
    own, sibling = own_ref[...], sibling_ref[...]
    for j, w_ref in enumerate(weights):
        total = jnp.dot(own, w_ref[mine, :], preferred_element_type=jnp.float32)
        total += jnp.dot(sibling, w_ref[other, :], preferred_element_type=jnp.float32)
        result[j] = total.astype(jnp.bfloat16)
    for i, term in enumerate(terms):
        term[...] = result[place_ref[0] ^ i]


def output_terms(place, own, sibling, weights):
    chips, shape = len(weights), (own.shape[0], weights[0].shape[1])
    return pl.pallas_call(
        output_kernel,
        out_shape=[jax.ShapeDtypeStruct(shape, jnp.bfloat16)] * chips,
        in_specs=[SMEM] + [VMEM] * (2 + chips),
        out_specs=[VMEM] * chips,
        scratch_shapes=[pltpu.VMEM((chips, *shape), jnp.bfloat16)],
        compiler_params=PARAMS,
    )(place, own, sibling, *weights)


def add_kernel(core_ref, *refs):
    terms, (own_ref, other_ref) = refs[:-2], refs[-2:]
    count = own_ref.shape[0]
    for out_ref, who in ((own_ref, core_ref[0]), (other_ref, 1 - core_ref[0])):
        lines = pl.ds(pl.multiple_of(who * count, count), count)
        total = terms[0][lines, :].astype(jnp.float32)
        for term in terms[1:]:
            total += term[lines, :].astype(jnp.float32)
        out_ref[...] = total.astype(jnp.bfloat16)


def add_terms(core, terms):
    rows, width = terms[0].shape
    out = jax.ShapeDtypeStruct((rows // CORES, width), jnp.bfloat16)
    return pl.pallas_call(
        add_kernel,
        out_shape=[out, out],
        in_specs=[SMEM] + [VMEM] * len(terms),
        out_specs=[VMEM, VMEM],
        compiler_params=PARAMS,
    )(core, *terms)


def on_device(n_dp, n_ctx, context, w_key, w_value, queries, offsets, head_gain, w_out):
    chips = n_ctx // CORES
    rows = context.shape[0]
    depth, panel = w_key.shape
    heads = panel // CORES // DH
    lat_count = queries.shape[0]
    me, mine_dp = lax.axis_index("ctx"), lax.axis_index("dp")
    chip, core = me // CORES, lax.rem(me, CORES)
    core_only = core.reshape(1)

    def across(array, bits):
        return lax.ppermute(array, "ctx", [(i, i ^ bits) for i in range(n_ctx)])

    def over_dp(array, bits):
        return lax.ppermute(array, "dp", [(d, d ^ bits) for d in range(n_dp)])

    def after(array, *others):
        return lax.optimization_barrier((array, others))[0]

    near_first = sorted(range(1, chips), key=lambda j: (j.bit_count(), -j))
    own_part, other_part = pack(core_only, w_key, w_value, queries)
    pairs = [None] * chips
    for j in near_first:
        if j & (j - 1) == 0:
            pairs[j] = (across(own_part, CORES * j), across(other_part, CORES * j + 1))
    context_sibling = across(after(context, own_part), 1)
    pairs[0] = (own_part, across(after(other_part, context_sibling), 1))

    places = jnp.stack(
        [(chip ^ j) * CORES + who for j in range(chips) for who in (core, 1 - core)]
    ).astype(jnp.int32)
    starts = places * depth
    first_acc, _ = project(starts[:CORES], context, context_sibling, pairs[0], None, depth)
    for j in near_first:
        low = j & -j
        if j != low:
            held, near = pairs[j ^ low], pairs[1]
            pairs[j] = (
                across(after(held[0], near[0]), CORES * low),
                across(after(held[1], near[1], first_acc), CORES * low),
            )
    blocks = [part for pair in pairs for part in pair]
    last = CORES * (chips - 1)
    acc, slices = project(
        starts[CORES:], context, context_sibling, blocks[CORES:last], first_acc, depth
    )
    firsts = jnp.stack([me * rows, (me ^ 1) * rows]).astype(jnp.int32)
    groups = tuple((CORES * z, CORES * z + 1) for z in range(chips))
    slot_groups = (chip ^ jnp.arange(chips)).astype(jnp.int32)
    messages = attend(
        firsts, slot_groups, places, slices, blocks, acc, offsets, groups, heads, depth
    )
    arrived = [messages[0]] + [across(messages[j], CORES * j) for j in range(1, chips)]
    shards = [after(w_out, *pairs[1], *pairs[2])] + [None] * (chips - 1)
    for j in near_first:
        low = j & -j
        shard = shards[j ^ low]
        shards[j] = across(shard if j == low else after(shard, *arrived[1:]), CORES * low)
    normed = combine(core_only, arrived, head_gain.reshape(1, panel), heads)

    terms = output_terms(
        jnp.stack([mine_dp ^ chip, core]).astype(jnp.int32), normed, across(normed, 1), shards
    )
    terms = [terms[0]] + [over_dp(terms[i], i) for i in range(1, n_dp)]
    mine, other = add_terms(core_only, terms)
    theirs = across(other, 1)
    return jnp.where(
        core == 0, jnp.concatenate([mine, theirs], axis=1), jnp.concatenate([theirs, mine], axis=1)
    )


def solution(mesh):
    n_dp, n_ctx = mesh.shape["dp"], mesh.shape["ctx"]
    placed = (
        P("ctx", None),
        P("ctx", "dp"),
        P("ctx", "dp"),
        P("ctx", "dp"),
        P(),
        P("dp"),
        P("dp", "ctx"),
    )

    def body(*args):
        return on_device(n_dp, n_ctx, *args)

    return jax.shard_map(
        body, mesh=mesh, in_specs=placed, out_specs=P("ctx", "dp"), check_vma=False
    )
```

```python
import functools
import math

import jax
import jax.numpy as jnp
from jax import lax
from jax.experimental import pallas as pl
from jax.experimental.pallas import tpu as pltpu
from jax.sharding import PartitionSpec as P

DH = 128
NEGATIVE = -1e30
CORES = 2
STATS = 16
VMEM = pl.BlockSpec(memory_space=pltpu.VMEM)
SMEM = pl.BlockSpec(memory_space=pltpu.SMEM)
ANY = pl.BlockSpec(memory_space=pl.ANY)
PARAMS = pltpu.CompilerParams(vmem_limit_bytes=40 * 2**20)
WIDE = pltpu.CompilerParams(vmem_limit_bytes=60 * 2**20)


def three_parts(value):
    high = value.astype(jnp.bfloat16).astype(jnp.float32)
    rest = value - high
    middle = rest.astype(jnp.bfloat16).astype(jnp.float32)
    low = (rest - middle).astype(jnp.bfloat16).astype(jnp.float32)
    return [high, middle, low]


def start_slices(starts_ref, skip, contexts, buffer, sems, count, depth):
    copies = []
    for b in range(count):
        first = pl.multiple_of(starts_ref[skip + b], DH)
        for which in range(CORES):
            slot = b * CORES + which
            copies.append(
                pltpu.make_async_copy(
                    contexts[which].at[:, pl.ds(first, depth)], buffer.at[slot],
                    sems.at[skip * CORES + slot],
                )
            )
    for copy in copies:
        copy.start()
    return copies


def add_products(copies, buffer, blocks, acc_ref, rows, depth, fresh):
    for b, block in enumerate(blocks):
        for which in range(CORES):
            slot = b * CORES + which
            if copies is not None:
                copies[slot].wait()
            product = jnp.dot(buffer[slot], block[:depth, :], preferred_element_type=jnp.float32)
            place = slice(which * rows, (which + 1) * rows)
            if fresh and b == 0:
                acc_ref[place, :] = product
            else:
                acc_ref[place, :] += product


def project_kernel(count, extra, has_acc, depth, *refs):
    starts_ref, own_ref, sibling_ref = refs[:3]
    blocks = refs[3 : 3 + count]
    acc_in = refs[3 + count] if has_acc else None
    acc_ref, later_ref, buffer, sems = refs[-4:]
    contexts = (own_ref, sibling_ref)
    copies = start_slices(starts_ref, 0, contexts, buffer, sems, count, depth)
    later = start_slices(starts_ref, count, contexts, later_ref, sems, extra, depth)
    if has_acc:
        acc_ref[...] = acc_in[...]
    add_products(copies, buffer, blocks, acc_ref, own_ref.shape[0], depth, not has_acc)
    for copy in later:
        copy.wait()


def project(starts, own, sibling, blocks, acc, depth):
    count, extra = len(blocks), starts.shape[0] - len(blocks)
    rows = own.shape[0]
    width = blocks[0].shape[1]
    operands = [starts, own, sibling, *blocks] + ([acc] if acc is not None else [])
    return pl.pallas_call(
        functools.partial(project_kernel, count, extra, acc is not None, depth),
        out_shape=[
            jax.ShapeDtypeStruct((CORES * rows, width), jnp.float32),
            jax.ShapeDtypeStruct((max(extra, 1) * CORES, rows if extra else 16, depth), own.dtype),
        ],
        in_specs=[SMEM, ANY, ANY] + [VMEM] * (len(operands) - 3),
        out_specs=[VMEM, VMEM],
        scratch_shapes=[
            pltpu.VMEM((count * CORES, rows, depth), own.dtype),
            pltpu.SemaphoreType.DMA(((count + extra) * CORES,)),
        ],
        compiler_params=PARAMS,
        cost_estimate=pl.CostEstimate(
            flops=2 * count * CORES * rows * depth * width,
            bytes_accessed=2 * count * CORES * rows * depth,
            transcendentals=0,
        ),
    )(*operands)


def attend_kernel(count, heads, depth, groups, slots, *refs):
    firsts_ref, slots_ref, places_ref, slices_ref = refs[:4]
    blocks = refs[4 : 4 + count]
    acc_in, offsets_ref = refs[4 + count : 6 + count]
    messages = refs[6 + count : 6 + count + slots]
    acc_ref, query_ref, group_ref = refs[6 + count + slots :]
    rows = slices_ref.shape[1]
    half = heads * DH
    lines = blocks[0].shape[0] - depth
    acc_ref[...] = acc_in[...]
    for b, block in enumerate(blocks):
        query_ref[places_ref[b], :lines, :] = block[depth:, :half]
        query_ref[places_ref[b], lines:, :] = block[depth:, half:]
    add_products(None, slices_ref, blocks[-CORES:], acc_ref, rows, depth, False)
    score_scale = 1.0 / math.sqrt(DH)
    line = lax.broadcasted_iota(jnp.int32, (CORES * rows, 1), 0)
    positions = jnp.where(line < rows, firsts_ref[0] + line, firsts_ref[1] + line - rows)
    for h in range(heads):
        keys = acc_ref[:, h * DH : (h + 1) * DH].astype(jnp.bfloat16)
        values = acc_ref[:, half + h * DH : half + (h + 1) * DH].T.astype(jnp.bfloat16)
        for g, members in enumerate(groups):
            query = jnp.concatenate(
                [query_ref[c, :, h * DH : (h + 1) * DH] for c in members], axis=0
            )
            scores = lax.dot_general(
                keys, query, (((1,), (1,)), ((), ())), preferred_element_type=jnp.float32
            ) * score_scale
            live = positions <= offsets_ref[g : g + 1, :]
            masked = jnp.where(live, scores, NEGATIVE)
            peak = jnp.max(masked, axis=0, keepdims=True)
            weights = jnp.where(live, jnp.exp(masked - peak), 0.0).astype(jnp.bfloat16)
            total = jnp.sum(weights.astype(jnp.float32), axis=0, keepdims=True)
            numerator = jnp.dot(values, weights, preferred_element_type=jnp.float32)
            stats = three_parts(peak) + three_parts(total)
            stats.append(jnp.zeros((STATS - len(stats), peak.shape[1]), jnp.float32))
            base = h * (DH + STATS)
            group_ref[g, base : base + DH, :] = numerator.astype(jnp.bfloat16)
            group_ref[g, base + DH : base + DH + STATS, :] = jnp.concatenate(
                stats, axis=0
            ).astype(jnp.bfloat16)
    for m in range(slots):
        messages[m][...] = group_ref[slots_ref[m]]


def attend(firsts, slot_groups, places, slices, blocks, acc, offsets, groups, heads, depth):
    count, slots = len(blocks), slot_groups.shape[0]
    rows, width = slices.shape[1], blocks[0].shape[1]
    lat_count = 2 * (blocks[0].shape[0] - depth)
    group = lat_count * len(groups[0])
    length = heads * (DH + STATS)
    group_offsets = jnp.stack(
        [
            jnp.concatenate([offsets[c * lat_count : (c + 1) * lat_count] for c in members])
            for members in groups
        ]
    )
    return pl.pallas_call(
        functools.partial(attend_kernel, count, heads, depth, groups, slots),
        out_shape=[jax.ShapeDtypeStruct((length, group), jnp.bfloat16)] * slots,
        in_specs=[SMEM] * 3 + [VMEM] * (count + 3),
        out_specs=[VMEM] * slots,
        scratch_shapes=[
            pltpu.VMEM((CORES * rows, width), jnp.float32),
            pltpu.VMEM((count, lat_count, heads * DH), jnp.bfloat16),
            pltpu.VMEM((len(groups), length, group), jnp.bfloat16),
        ],
        compiler_params=PARAMS,
        cost_estimate=pl.CostEstimate(
            flops=8 * CORES * rows * group * len(groups) * heads * DH,
            bytes_accessed=2 * CORES * CORES * rows * depth,
            transcendentals=CORES * rows * group * len(groups) * heads,
        ),
    )(firsts, slot_groups, places, slices, *blocks, acc, group_offsets)


def normed_head(messages, base):
    peaks, totals = [], []
    for message in messages:
        stats = message[base + DH : base + DH + STATS, :].astype(jnp.float32)
        peaks.append(stats[0:1] + stats[1:2] + stats[2:3])
        totals.append(stats[3:4] + stats[4:5] + stats[5:6])
    top = functools.reduce(jnp.maximum, peaks)
    total, numerator = 0.0, 0.0
    for message, peak, part in zip(messages, peaks, totals):
        scale = jnp.exp(peak - top)
        total += part * scale
        numerator += message[base : base + DH, :].astype(jnp.float32) * scale
    attended = numerator / total
    mean_square = jnp.mean(attended * attended, axis=0, keepdims=True)
    return (attended * lax.rsqrt(mean_square + 1e-05)).T


def combine_kernel(heads, core_ref, *refs):
    messages, gain_ref, out_ref = refs[:-2], refs[-2], refs[-1]
    half = out_ref.shape[1]
    for h in range(heads):
        place = pl.ds(pl.multiple_of(core_ref[0] * half, DH) + h * DH, DH)
        normed = normed_head(messages, h * (DH + STATS))
        normed = normed * gain_ref[:, place].astype(jnp.float32)
        out_ref[:, h * DH : (h + 1) * DH] = normed.astype(jnp.bfloat16)


def combine(core, messages, gain, heads):
    return pl.pallas_call(
        functools.partial(combine_kernel, heads),
        out_shape=jax.ShapeDtypeStruct((messages[0].shape[1], heads * DH), jnp.bfloat16),
        in_specs=[SMEM] + [VMEM] * (len(messages) + 1),
        out_specs=VMEM,
        compiler_params=PARAMS,
    )(core, *messages, gain)


def pack_kernel(core_ref, key_ref, value_ref, query_ref, own_ref, other_ref, sems):
    depth, half = key_ref.shape[0], key_ref.shape[1] // CORES
    lines = query_ref.shape[0] // 2
    copies = []
    for out_ref, who in ((own_ref, core_ref[0]), (other_ref, 1 - core_ref[0])):
        place = pl.ds(pl.multiple_of(who * half, DH), half)
        for source, target in (
            (key_ref.at[:, place], out_ref.at[pl.ds(0, depth), pl.ds(0, half)]),
            (value_ref.at[:, place], out_ref.at[pl.ds(0, depth), pl.ds(half, half)]),
            (query_ref.at[pl.ds(0, lines), place], out_ref.at[pl.ds(depth, lines), pl.ds(0, half)]),
            (query_ref.at[pl.ds(lines, lines), place], out_ref.at[pl.ds(depth, lines), pl.ds(half, half)]),
        ):
            copies.append(pltpu.make_async_copy(source, target, sems.at[len(copies)]))
            copies[-1].start()
    for copy in copies:
        copy.wait()


def pack(core, w_key, w_value, queries):
    depth, panel = w_key.shape
    out = jax.ShapeDtypeStruct((depth + queries.shape[0] // 2, panel), w_key.dtype)
    return pl.pallas_call(
        pack_kernel,
        out_shape=[out, out],
        in_specs=[SMEM, ANY, ANY, ANY],
        out_specs=[VMEM, VMEM],
        scratch_shapes=[pltpu.SemaphoreType.DMA((8,))],
        compiler_params=WIDE,
    )(core, w_key, w_value, queries)


def output_kernel(place_ref, own_ref, sibling_ref, *refs):
    chips = (len(refs) - 1) // 2
    weights, terms, result = refs[:chips], refs[chips:-1], refs[-1]
    half = own_ref.shape[1]
    mine = pl.ds(pl.multiple_of(place_ref[1] * half, DH), half)
    other = pl.ds(pl.multiple_of((1 - place_ref[1]) * half, DH), half)
    own, sibling = own_ref[...], sibling_ref[...]
    for j, w_ref in enumerate(weights):
        total = jnp.dot(own, w_ref[mine, :], preferred_element_type=jnp.float32)
        total += jnp.dot(sibling, w_ref[other, :], preferred_element_type=jnp.float32)
        result[j] = total.astype(jnp.bfloat16)
    for i, term in enumerate(terms):
        term[...] = result[place_ref[0] ^ i]


def output_terms(place, own, sibling, weights):
    chips, shape = len(weights), (own.shape[0], weights[0].shape[1])
    return pl.pallas_call(
        output_kernel,
        out_shape=[jax.ShapeDtypeStruct(shape, jnp.bfloat16)] * chips,
        in_specs=[SMEM] + [VMEM] * (2 + chips),
        out_specs=[VMEM] * chips,
        scratch_shapes=[pltpu.VMEM((chips, *shape), jnp.bfloat16)],
        compiler_params=PARAMS,
    )(place, own, sibling, *weights)


def add_kernel(core_ref, *refs):
    terms, (own_ref, other_ref) = refs[:-2], refs[-2:]
    count = own_ref.shape[0]
    for out_ref, who in ((own_ref, core_ref[0]), (other_ref, 1 - core_ref[0])):
        lines = pl.ds(pl.multiple_of(who * count, count), count)
        total = terms[0][lines, :].astype(jnp.float32)
        for term in terms[1:]:
            total += term[lines, :].astype(jnp.float32)
        out_ref[...] = total.astype(jnp.bfloat16)


def add_terms(core, terms):
    rows, width = terms[0].shape
    out = jax.ShapeDtypeStruct((rows // CORES, width), jnp.bfloat16)
    return pl.pallas_call(
        add_kernel,
        out_shape=[out, out],
        in_specs=[SMEM] + [VMEM] * len(terms),
        out_specs=[VMEM, VMEM],
        compiler_params=PARAMS,
    )(core, *terms)


def on_device(n_dp, n_ctx, context, w_key, w_value, queries, offsets, head_gain, w_out):
    chips = n_ctx // CORES
    rows = context.shape[0]
    depth, panel = w_key.shape
    heads = panel // CORES // DH
    lat_count = queries.shape[0]
    me, mine_dp = lax.axis_index("ctx"), lax.axis_index("dp")
    chip, core = me // CORES, lax.rem(me, CORES)
    core_only = core.reshape(1)

    def across(array, bits):
        return lax.ppermute(array, "ctx", [(i, i ^ bits) for i in range(n_ctx)])

    def over_dp(array, bits):
        return lax.ppermute(array, "dp", [(d, d ^ bits) for d in range(n_dp)])

    def after(array, *others):
        return lax.optimization_barrier((array, others))[0]

    near_first = sorted(range(1, chips), key=lambda j: (j.bit_count(), -j))
    own_part, other_part = pack(core_only, w_key, w_value, queries)
    pairs = [None] * chips
    for j in near_first:
        if j & (j - 1) == 0:
            pairs[j] = (across(own_part, CORES * j), across(other_part, CORES * j + 1))
    context_sibling = across(after(context, own_part), 1)
    pairs[0] = (own_part, across(after(other_part, context_sibling), 1))

    places = jnp.stack(
        [(chip ^ j) * CORES + who for j in range(chips) for who in (core, 1 - core)]
    ).astype(jnp.int32)
    starts = places * depth
    first_acc, _ = project(starts[:CORES], context, context_sibling, pairs[0], None, depth)
    for j in near_first:
        low = j & -j
        if j != low:
            held, near = pairs[j ^ low], pairs[1]
            pairs[j] = (
                across(after(held[0], near[0]), CORES * low),
                across(after(held[1], near[1], first_acc), CORES * low),
            )
    blocks = [part for pair in pairs for part in pair]
    last = CORES * (chips - 1)
    acc, slices = project(
        starts[CORES:], context, context_sibling, blocks[CORES:last], first_acc, depth
    )
    firsts = jnp.stack([me * rows, (me ^ 1) * rows]).astype(jnp.int32)
    groups = tuple((CORES * z, CORES * z + 1) for z in range(chips))
    slot_groups = (chip ^ jnp.arange(chips)).astype(jnp.int32)
    messages = attend(
        firsts, slot_groups, places, slices, blocks, acc, offsets, groups, heads, depth
    )
    arrived = [messages[0]] + [across(messages[j], CORES * j) for j in range(1, chips)]
    shards = [after(w_out, *pairs[1], *pairs[2])] + [None] * (chips - 1)
    for j in near_first:
        low = j & -j
        shard = shards[j ^ low]
        shards[j] = across(shard if j == low else after(shard, shards[1], *arrived[1:]), CORES * low)
    normed = combine(core_only, arrived, head_gain.reshape(1, panel), heads)

    terms = output_terms(
        jnp.stack([mine_dp ^ chip, core]).astype(jnp.int32), normed, across(normed, 1), shards
    )
    terms = [terms[0]] + [over_dp(terms[i], i) for i in range(1, n_dp)]
    mine, other = add_terms(core_only, terms)
    theirs = across(other, 1)
    return jnp.where(
        core == 0, jnp.concatenate([mine, theirs], axis=1), jnp.concatenate([theirs, mine], axis=1)
    )


def solution(mesh):
    n_dp, n_ctx = mesh.shape["dp"], mesh.shape["ctx"]
    placed = (
        P("ctx", None),
        P("ctx", "dp"),
        P("ctx", "dp"),
        P("ctx", "dp"),
        P(),
        P("dp"),
        P("dp", "ctx"),
    )

    def body(*args):
        return on_device(n_dp, n_ctx, *args)

    return jax.shard_map(
        body, mesh=mesh, in_specs=placed, out_specs=P("ctx", "dp"), check_vma=False
    )
```

```python
import functools
import math

import jax
import jax.numpy as jnp
from jax import lax
from jax.experimental import pallas as pl
from jax.experimental.pallas import tpu as pltpu
from jax.sharding import PartitionSpec as P

DH = 128
NEGATIVE = -1e30
CORES = 2
STATS = 16
VMEM = pl.BlockSpec(memory_space=pltpu.VMEM)
SMEM = pl.BlockSpec(memory_space=pltpu.SMEM)
ANY = pl.BlockSpec(memory_space=pl.ANY)
PARAMS = pltpu.CompilerParams(vmem_limit_bytes=40 * 2**20)
WIDE = pltpu.CompilerParams(vmem_limit_bytes=60 * 2**20)


def three_parts(value):
    high = value.astype(jnp.bfloat16).astype(jnp.float32)
    rest = value - high
    middle = rest.astype(jnp.bfloat16).astype(jnp.float32)
    low = (rest - middle).astype(jnp.bfloat16).astype(jnp.float32)
    return [high, middle, low]


def start_slices(starts_ref, skip, contexts, buffer, sems, count, depth):
    copies = []
    for b in range(count):
        first = pl.multiple_of(starts_ref[skip + b], DH)
        for which in range(CORES):
            slot = b * CORES + which
            copies.append(
                pltpu.make_async_copy(
                    contexts[which].at[:, pl.ds(first, depth)], buffer.at[slot],
                    sems.at[skip * CORES + slot],
                )
            )
    for copy in copies:
        copy.start()
    return copies


def add_products(copies, buffer, blocks, base_ref, acc_ref, rows, depth):
    for which in range(CORES):
        place = slice(which * rows, (which + 1) * rows)
        total = None if base_ref is None else base_ref[place, :]
        for b, block in enumerate(blocks):
            slot = b * CORES + which
            if copies is not None:
                copies[slot].wait()
            product = jnp.dot(buffer[slot], block[:depth, :], preferred_element_type=jnp.float32)
            total = product if total is None else total + product
        acc_ref[place, :] = total


def project_kernel(count, extra, has_acc, depth, *refs):
    starts_ref, own_ref, sibling_ref = refs[:3]
    blocks = refs[3 : 3 + count]
    acc_in = refs[3 + count] if has_acc else None
    acc_ref, later_ref, buffer, sems = refs[-4:]
    contexts = (own_ref, sibling_ref)
    copies = start_slices(starts_ref, 0, contexts, buffer, sems, count, depth)
    later = start_slices(starts_ref, count, contexts, later_ref, sems, extra, depth)
    add_products(copies, buffer, blocks, acc_in, acc_ref, own_ref.shape[0], depth)
    for copy in later:
        copy.wait()


def project(starts, own, sibling, blocks, acc, depth):
    count, extra = len(blocks), starts.shape[0] - len(blocks)
    rows = own.shape[0]
    width = blocks[0].shape[1]
    operands = [starts, own, sibling, *blocks] + ([acc] if acc is not None else [])
    return pl.pallas_call(
        functools.partial(project_kernel, count, extra, acc is not None, depth),
        out_shape=[
            jax.ShapeDtypeStruct((CORES * rows, width), jnp.float32),
            jax.ShapeDtypeStruct((max(extra, 1) * CORES, rows if extra else 16, depth), own.dtype),
        ],
        in_specs=[SMEM, ANY, ANY] + [VMEM] * (len(operands) - 3),
        out_specs=[VMEM, VMEM],
        scratch_shapes=[
            pltpu.VMEM((count * CORES, rows, depth), own.dtype),
            pltpu.SemaphoreType.DMA(((count + extra) * CORES,)),
        ],
        compiler_params=PARAMS,
        cost_estimate=pl.CostEstimate(
            flops=2 * count * CORES * rows * depth * width,
            bytes_accessed=2 * count * CORES * rows * depth,
            transcendentals=0,
        ),
    )(*operands)


def attend_kernel(count, heads, depth, groups, slots, *refs):
    firsts_ref, slots_ref, places_ref, slices_ref = refs[:4]
    blocks = refs[4 : 4 + count]
    acc_in, offsets_ref = refs[4 + count : 6 + count]
    messages = refs[6 + count : 6 + count + slots]
    acc_ref, query_ref, group_ref = refs[6 + count + slots :]
    rows = slices_ref.shape[1]
    half = heads * DH
    lines = blocks[0].shape[0] - depth
    for b, block in enumerate(blocks):
        query_ref[places_ref[b], :lines, :] = block[depth:, :half]
        query_ref[places_ref[b], lines:, :] = block[depth:, half:]
    add_products(None, slices_ref, blocks[-CORES:], acc_in, acc_ref, rows, depth)
    score_scale = 1.0 / math.sqrt(DH)
    line = lax.broadcasted_iota(jnp.int32, (CORES * rows, 1), 0)
    positions = jnp.where(line < rows, firsts_ref[0] + line, firsts_ref[1] + line - rows)
    for h in range(heads):
        keys = acc_ref[:, h * DH : (h + 1) * DH].astype(jnp.bfloat16)
        values = acc_ref[:, half + h * DH : half + (h + 1) * DH].T.astype(jnp.bfloat16)
        for g, members in enumerate(groups):
            query = jnp.concatenate(
                [query_ref[c, :, h * DH : (h + 1) * DH] for c in members], axis=0
            )
            scores = lax.dot_general(
                keys, query, (((1,), (1,)), ((), ())), preferred_element_type=jnp.float32
            ) * score_scale
            live = positions <= offsets_ref[g : g + 1, :]
            masked = jnp.where(live, scores, NEGATIVE)
            peak = jnp.max(masked, axis=0, keepdims=True)
            weights = jnp.where(live, jnp.exp(masked - peak), 0.0).astype(jnp.bfloat16)
            total = jnp.sum(weights.astype(jnp.float32), axis=0, keepdims=True)
            numerator = jnp.dot(values, weights, preferred_element_type=jnp.float32)
            stats = three_parts(peak) + three_parts(total)
            stats.append(jnp.zeros((STATS - len(stats), peak.shape[1]), jnp.float32))
            base = h * (DH + STATS)
            group_ref[g, base : base + DH, :] = numerator.astype(jnp.bfloat16)
            group_ref[g, base + DH : base + DH + STATS, :] = jnp.concatenate(
                stats, axis=0
            ).astype(jnp.bfloat16)
    for m in range(slots):
        messages[m][...] = group_ref[slots_ref[m]]


def attend(firsts, slot_groups, places, slices, blocks, acc, offsets, groups, heads, depth):
    count, slots = len(blocks), slot_groups.shape[0]
    rows, width = slices.shape[1], blocks[0].shape[1]
    lat_count = 2 * (blocks[0].shape[0] - depth)
    group = lat_count * len(groups[0])
    length = heads * (DH + STATS)
    group_offsets = jnp.stack(
        [
            jnp.concatenate([offsets[c * lat_count : (c + 1) * lat_count] for c in members])
            for members in groups
        ]
    )
    return pl.pallas_call(
        functools.partial(attend_kernel, count, heads, depth, groups, slots),
        out_shape=[jax.ShapeDtypeStruct((length, group), jnp.bfloat16)] * slots,
        in_specs=[SMEM] * 3 + [VMEM] * (count + 3),
        out_specs=[VMEM] * slots,
        scratch_shapes=[
            pltpu.VMEM((CORES * rows, width), jnp.float32),
            pltpu.VMEM((count, lat_count, heads * DH), jnp.bfloat16),
            pltpu.VMEM((len(groups), length, group), jnp.bfloat16),
        ],
        compiler_params=PARAMS,
        cost_estimate=pl.CostEstimate(
            flops=8 * CORES * rows * group * len(groups) * heads * DH,
            bytes_accessed=2 * CORES * CORES * rows * depth,
            transcendentals=CORES * rows * group * len(groups) * heads,
        ),
    )(firsts, slot_groups, places, slices, *blocks, acc, group_offsets)


def normed_head(messages, base):
    peaks, totals = [], []
    for message in messages:
        stats = message[base + DH : base + DH + STATS, :].astype(jnp.float32)
        peaks.append(stats[0:1] + stats[1:2] + stats[2:3])
        totals.append(stats[3:4] + stats[4:5] + stats[5:6])
    top = functools.reduce(jnp.maximum, peaks)
    total, numerator = 0.0, 0.0
    for message, peak, part in zip(messages, peaks, totals):
        scale = jnp.exp(peak - top)
        total += part * scale
        numerator += message[base : base + DH, :].astype(jnp.float32) * scale
    attended = numerator / total
    mean_square = jnp.mean(attended * attended, axis=0, keepdims=True)
    return (attended * lax.rsqrt(mean_square + 1e-05)).T


def combine_kernel(heads, core_ref, *refs):
    messages, gain_ref, out_ref = refs[:-2], refs[-2], refs[-1]
    half = out_ref.shape[1]
    for h in range(heads):
        place = pl.ds(pl.multiple_of(core_ref[0] * half, DH) + h * DH, DH)
        normed = normed_head(messages, h * (DH + STATS))
        normed = normed * gain_ref[:, place].astype(jnp.float32)
        out_ref[:, h * DH : (h + 1) * DH] = normed.astype(jnp.bfloat16)


def combine(core, messages, gain, heads):
    return pl.pallas_call(
        functools.partial(combine_kernel, heads),
        out_shape=jax.ShapeDtypeStruct((messages[0].shape[1], heads * DH), jnp.bfloat16),
        in_specs=[SMEM] + [VMEM] * (len(messages) + 1),
        out_specs=VMEM,
        compiler_params=PARAMS,
    )(core, *messages, gain)


def pack_kernel(core_ref, key_ref, value_ref, query_ref, own_ref, other_ref, sems):
    depth, half = key_ref.shape[0], key_ref.shape[1] // CORES
    lines = query_ref.shape[0] // 2
    copies = []
    for out_ref, who in ((own_ref, core_ref[0]), (other_ref, 1 - core_ref[0])):
        place = pl.ds(pl.multiple_of(who * half, DH), half)
        for source, target in (
            (key_ref.at[:, place], out_ref.at[pl.ds(0, depth), pl.ds(0, half)]),
            (value_ref.at[:, place], out_ref.at[pl.ds(0, depth), pl.ds(half, half)]),
            (query_ref.at[pl.ds(0, lines), place], out_ref.at[pl.ds(depth, lines), pl.ds(0, half)]),
            (query_ref.at[pl.ds(lines, lines), place], out_ref.at[pl.ds(depth, lines), pl.ds(half, half)]),
        ):
            copies.append(pltpu.make_async_copy(source, target, sems.at[len(copies)]))
            copies[-1].start()
    for copy in copies:
        copy.wait()


def pack(core, w_key, w_value, queries):
    depth, panel = w_key.shape
    out = jax.ShapeDtypeStruct((depth + queries.shape[0] // 2, panel), w_key.dtype)
    return pl.pallas_call(
        pack_kernel,
        out_shape=[out, out],
        in_specs=[SMEM, ANY, ANY, ANY],
        out_specs=[VMEM, VMEM],
        scratch_shapes=[pltpu.SemaphoreType.DMA((8,))],
        compiler_params=WIDE,
    )(core, w_key, w_value, queries)


def output_kernel(place_ref, own_ref, sibling_ref, *refs):
    chips = (len(refs) - 1) // 2
    weights, terms, result = refs[:chips], refs[chips:-1], refs[-1]
    half = own_ref.shape[1]
    mine = pl.ds(pl.multiple_of(place_ref[1] * half, DH), half)
    other = pl.ds(pl.multiple_of((1 - place_ref[1]) * half, DH), half)
    own, sibling = own_ref[...], sibling_ref[...]
    for j, w_ref in enumerate(weights):
        total = jnp.dot(own, w_ref[mine, :], preferred_element_type=jnp.float32)
        total += jnp.dot(sibling, w_ref[other, :], preferred_element_type=jnp.float32)
        result[j] = total.astype(jnp.bfloat16)
    for i, term in enumerate(terms):
        term[...] = result[place_ref[0] ^ i]


def output_terms(place, own, sibling, weights):
    chips, shape = len(weights), (own.shape[0], weights[0].shape[1])
    return pl.pallas_call(
        output_kernel,
        out_shape=[jax.ShapeDtypeStruct(shape, jnp.bfloat16)] * chips,
        in_specs=[SMEM] + [VMEM] * (2 + chips),
        out_specs=[VMEM] * chips,
        scratch_shapes=[pltpu.VMEM((chips, *shape), jnp.bfloat16)],
        compiler_params=PARAMS,
    )(place, own, sibling, *weights)


def add_kernel(core_ref, *refs):
    terms, (own_ref, other_ref) = refs[:-2], refs[-2:]
    count = own_ref.shape[0]
    for out_ref, who in ((own_ref, core_ref[0]), (other_ref, 1 - core_ref[0])):
        lines = pl.ds(pl.multiple_of(who * count, count), count)
        total = terms[0][lines, :].astype(jnp.float32)
        for term in terms[1:]:
            total += term[lines, :].astype(jnp.float32)
        out_ref[...] = total.astype(jnp.bfloat16)


def add_terms(core, terms):
    rows, width = terms[0].shape
    out = jax.ShapeDtypeStruct((rows // CORES, width), jnp.bfloat16)
    return pl.pallas_call(
        add_kernel,
        out_shape=[out, out],
        in_specs=[SMEM] + [VMEM] * len(terms),
        out_specs=[VMEM, VMEM],
        compiler_params=PARAMS,
    )(core, *terms)


def on_device(n_dp, n_ctx, context, w_key, w_value, queries, offsets, head_gain, w_out):
    chips = n_ctx // CORES
    rows = context.shape[0]
    depth, panel = w_key.shape
    heads = panel // CORES // DH
    lat_count = queries.shape[0]
    me, mine_dp = lax.axis_index("ctx"), lax.axis_index("dp")
    chip, core = me // CORES, lax.rem(me, CORES)
    core_only = core.reshape(1)

    def across(array, bits):
        return lax.ppermute(array, "ctx", [(i, i ^ bits) for i in range(n_ctx)])

    def over_dp(array, bits):
        return lax.ppermute(array, "dp", [(d, d ^ bits) for d in range(n_dp)])

    def after(array, *others):
        return lax.optimization_barrier((array, others))[0]

    near_first = sorted(range(1, chips), key=lambda j: (j.bit_count(), -j))
    own_part, other_part = pack(core_only, w_key, w_value, queries)
    pairs = [None] * chips
    for j in near_first:
        if j & (j - 1) == 0:
            pairs[j] = (across(own_part, CORES * j), across(other_part, CORES * j + 1))
    context_sibling = across(after(context, own_part), 1)
    pairs[0] = (own_part, across(after(other_part, context_sibling), 1))

    places = jnp.stack(
        [(chip ^ j) * CORES + who for j in range(chips) for who in (core, 1 - core)]
    ).astype(jnp.int32)
    starts = places * depth
    first_acc, _ = project(starts[:CORES], context, context_sibling, pairs[0], None, depth)
    for j in near_first:
        low = j & -j
        if j != low:
            held, near = pairs[j ^ low], pairs[1]
            pairs[j] = (
                across(after(held[0], near[0]), CORES * low),
                across(after(held[1], near[1], first_acc), CORES * low),
            )
    blocks = [part for pair in pairs for part in pair]
    last = CORES * (chips - 1)
    acc, slices = project(
        starts[CORES:], context, context_sibling, blocks[CORES:last], first_acc, depth
    )
    firsts = jnp.stack([me * rows, (me ^ 1) * rows]).astype(jnp.int32)
    groups = tuple((CORES * z, CORES * z + 1) for z in range(chips))
    slot_groups = (chip ^ jnp.arange(chips)).astype(jnp.int32)
    messages = attend(
        firsts, slot_groups, places, slices, blocks, acc, offsets, groups, heads, depth
    )
    arrived = [messages[0]] + [across(messages[j], CORES * j) for j in range(1, chips)]
    shards = [after(w_out, acc)] + [None] * (chips - 1)
    for j in near_first:
        low = j & -j
        shard = shards[j ^ low]
        shards[j] = across(shard if j == low else after(shard, messages[0]), CORES * low)
    normed = combine(core_only, arrived, head_gain.reshape(1, panel), heads)

    terms = output_terms(
        jnp.stack([mine_dp ^ chip, core]).astype(jnp.int32), normed, across(normed, 1), shards
    )
    terms = [terms[0]] + [over_dp(terms[i], i) for i in range(1, n_dp)]
    mine, other = add_terms(core_only, terms)
    theirs = across(other, 1)
    return jnp.where(
        core == 0, jnp.concatenate([mine, theirs], axis=1), jnp.concatenate([theirs, mine], axis=1)
    )


def solution(mesh):
    n_dp, n_ctx = mesh.shape["dp"], mesh.shape["ctx"]
    placed = (
        P("ctx", None),
        P("ctx", "dp"),
        P("ctx", "dp"),
        P("ctx", "dp"),
        P(),
        P("dp"),
        P("dp", "ctx"),
    )

    def body(*args):
        return on_device(n_dp, n_ctx, *args)

    return jax.shard_map(
        body, mesh=mesh, in_specs=placed, out_specs=P("ctx", "dp"), check_vma=False
    )
```

```python
import functools
import math

import jax
import jax.numpy as jnp
from jax import lax
from jax.experimental import pallas as pl
from jax.experimental.pallas import tpu as pltpu
from jax.sharding import PartitionSpec as P

DH = 128
NEGATIVE = -1e30
CORES = 2
STATS = 16
VMEM = pl.BlockSpec(memory_space=pltpu.VMEM)
SMEM = pl.BlockSpec(memory_space=pltpu.SMEM)
ANY = pl.BlockSpec(memory_space=pl.ANY)
PARAMS = pltpu.CompilerParams(vmem_limit_bytes=40 * 2**20)
WIDE = pltpu.CompilerParams(vmem_limit_bytes=60 * 2**20)


def three_parts(value):
    high = value.astype(jnp.bfloat16).astype(jnp.float32)
    rest = value - high
    middle = rest.astype(jnp.bfloat16).astype(jnp.float32)
    low = (rest - middle).astype(jnp.bfloat16).astype(jnp.float32)
    return [high, middle, low]


def start_slices(starts_ref, skip, contexts, buffer, sems, count, depth):
    copies = []
    for b in range(count):
        first = pl.multiple_of(starts_ref[skip + b], DH)
        for which in range(CORES):
            slot = b * CORES + which
            copies.append(
                pltpu.make_async_copy(
                    contexts[which].at[:, pl.ds(first, depth)], buffer.at[slot],
                    sems.at[skip * CORES + slot],
                )
            )
    for copy in copies:
        copy.start()
    return copies


def add_products(copies, buffer, blocks, base_ref, acc_ref, rows, depth):
    for which in range(CORES):
        place = slice(which * rows, (which + 1) * rows)
        total = None if base_ref is None else base_ref[place, :]
        for b, block in enumerate(blocks):
            slot = b * CORES + which
            if copies is not None:
                copies[slot].wait()
            product = jnp.dot(buffer[slot], block[:depth, :], preferred_element_type=jnp.float32)
            total = product if total is None else total + product
        acc_ref[place, :] = total


def project_kernel(count, extra, has_acc, depth, *refs):
    starts_ref, own_ref, sibling_ref = refs[:3]
    blocks = refs[3 : 3 + count]
    acc_in = refs[3 + count] if has_acc else None
    acc_ref, later_ref, buffer, sems = refs[-4:]
    contexts = (own_ref, sibling_ref)
    copies = start_slices(starts_ref, 0, contexts, buffer, sems, count, depth)
    later = start_slices(starts_ref, count, contexts, later_ref, sems, extra, depth)
    add_products(copies, buffer, blocks, acc_in, acc_ref, own_ref.shape[0], depth)
    for copy in later:
        copy.wait()


def project(starts, own, sibling, blocks, acc, depth):
    count, extra = len(blocks), starts.shape[0] - len(blocks)
    rows = own.shape[0]
    width = blocks[0].shape[1]
    operands = [starts, own, sibling, *blocks] + ([acc] if acc is not None else [])
    return pl.pallas_call(
        functools.partial(project_kernel, count, extra, acc is not None, depth),
        out_shape=[
            jax.ShapeDtypeStruct((CORES * rows, width), jnp.float32),
            jax.ShapeDtypeStruct((max(extra, 1) * CORES, rows if extra else 16, depth), own.dtype),
        ],
        in_specs=[SMEM, ANY, ANY] + [VMEM] * (len(operands) - 3),
        out_specs=[VMEM, VMEM],
        scratch_shapes=[
            pltpu.VMEM((count * CORES, rows, depth), own.dtype),
            pltpu.SemaphoreType.DMA(((count + extra) * CORES,)),
        ],
        compiler_params=PARAMS,
        cost_estimate=pl.CostEstimate(
            flops=2 * count * CORES * rows * depth * width,
            bytes_accessed=2 * count * CORES * rows * depth,
            transcendentals=0,
        ),
    )(*operands)


def attend_kernel(count, heads, depth, groups, slots, *refs):
    firsts_ref, slots_ref, places_ref, slices_ref = refs[:4]
    blocks = refs[4 : 4 + count]
    acc_in, offsets_ref = refs[4 + count : 6 + count]
    messages = refs[6 + count : 6 + count + slots]
    acc_ref, query_ref, group_ref = refs[6 + count + slots :]
    rows = slices_ref.shape[1]
    half = heads * DH
    lines = blocks[0].shape[0] - depth
    for b, block in enumerate(blocks):
        query_ref[places_ref[b], :lines, :] = block[depth:, :half]
        query_ref[places_ref[b], lines:, :] = block[depth:, half:]
    add_products(None, slices_ref, blocks[-CORES:], acc_in, acc_ref, rows, depth)
    score_scale = 1.0 / math.sqrt(DH)
    line = lax.broadcasted_iota(jnp.int32, (CORES * rows, 1), 0)
    positions = jnp.where(line < rows, firsts_ref[0] + line, firsts_ref[1] + line - rows)
    for h in range(heads):
        keys = acc_ref[:, h * DH : (h + 1) * DH].astype(jnp.bfloat16)
        values = acc_ref[:, half + h * DH : half + (h + 1) * DH].T.astype(jnp.bfloat16)
        for g, members in enumerate(groups):
            query = jnp.concatenate(
                [query_ref[c, :, h * DH : (h + 1) * DH] for c in members], axis=0
            )
            scores = lax.dot_general(
                keys, query, (((1,), (1,)), ((), ())), preferred_element_type=jnp.float32
            ) * score_scale
            live = positions <= offsets_ref[g : g + 1, :]
            masked = jnp.where(live, scores, NEGATIVE)
            peak = jnp.max(masked, axis=0, keepdims=True)
            weights = jnp.where(live, jnp.exp(masked - peak), 0.0).astype(jnp.bfloat16)
            total = jnp.sum(weights.astype(jnp.float32), axis=0, keepdims=True)
            numerator = jnp.dot(values, weights, preferred_element_type=jnp.float32)
            stats = three_parts(peak) + three_parts(total)
            stats.append(jnp.zeros((STATS - len(stats), peak.shape[1]), jnp.float32))
            base = h * (DH + STATS)
            group_ref[g, base : base + DH, :] = numerator.astype(jnp.bfloat16)
            group_ref[g, base + DH : base + DH + STATS, :] = jnp.concatenate(
                stats, axis=0
            ).astype(jnp.bfloat16)
    for m in range(slots):
        messages[m][...] = group_ref[slots_ref[m]]


def attend(firsts, slot_groups, places, slices, blocks, acc, offsets, groups, heads, depth):
    count, slots = len(blocks), slot_groups.shape[0]
    rows, width = slices.shape[1], blocks[0].shape[1]
    lat_count = 2 * (blocks[0].shape[0] - depth)
    group = lat_count * len(groups[0])
    length = heads * (DH + STATS)
    group_offsets = jnp.stack(
        [
            jnp.concatenate([offsets[c * lat_count : (c + 1) * lat_count] for c in members])
            for members in groups
        ]
    )
    return pl.pallas_call(
        functools.partial(attend_kernel, count, heads, depth, groups, slots),
        out_shape=[jax.ShapeDtypeStruct((length, group), jnp.bfloat16)] * slots,
        in_specs=[SMEM] * 3 + [VMEM] * (count + 3),
        out_specs=[VMEM] * slots,
        scratch_shapes=[
            pltpu.VMEM((CORES * rows, width), jnp.float32),
            pltpu.VMEM((count, lat_count, heads * DH), jnp.bfloat16),
            pltpu.VMEM((len(groups), length, group), jnp.bfloat16),
        ],
        compiler_params=PARAMS,
        cost_estimate=pl.CostEstimate(
            flops=8 * CORES * rows * group * len(groups) * heads * DH,
            bytes_accessed=2 * CORES * CORES * rows * depth,
            transcendentals=CORES * rows * group * len(groups) * heads,
        ),
    )(firsts, slot_groups, places, slices, *blocks, acc, group_offsets)


def normed_head(messages, base):
    peaks, totals = [], []
    for message in messages:
        stats = message[base + DH : base + DH + STATS, :].astype(jnp.float32)
        peaks.append(stats[0:1] + stats[1:2] + stats[2:3])
        totals.append(stats[3:4] + stats[4:5] + stats[5:6])
    top = functools.reduce(jnp.maximum, peaks)
    total, numerator = 0.0, 0.0
    for message, peak, part in zip(messages, peaks, totals):
        scale = jnp.exp(peak - top)
        total += part * scale
        numerator += message[base : base + DH, :].astype(jnp.float32) * scale
    attended = numerator / total
    mean_square = jnp.mean(attended * attended, axis=0, keepdims=True)
    return (attended * lax.rsqrt(mean_square + 1e-05)).T


def combine_kernel(heads, core_ref, *refs):
    messages, gain_ref, out_ref = refs[:-2], refs[-2], refs[-1]
    half = out_ref.shape[1]
    for h in range(heads):
        place = pl.ds(pl.multiple_of(core_ref[0] * half, DH) + h * DH, DH)
        normed = normed_head(messages, h * (DH + STATS))
        normed = normed * gain_ref[:, place].astype(jnp.float32)
        out_ref[:, h * DH : (h + 1) * DH] = normed.astype(jnp.bfloat16)


def combine(core, messages, gain, heads):
    return pl.pallas_call(
        functools.partial(combine_kernel, heads),
        out_shape=jax.ShapeDtypeStruct((messages[0].shape[1], heads * DH), jnp.bfloat16),
        in_specs=[SMEM] + [VMEM] * (len(messages) + 1),
        out_specs=VMEM,
        compiler_params=PARAMS,
    )(core, *messages, gain)


def pack_kernel(core_ref, key_ref, value_ref, query_ref, own_ref, other_ref, sems):
    depth, half = key_ref.shape[0], key_ref.shape[1] // CORES
    lines = query_ref.shape[0] // 2
    copies = []
    for out_ref, who in ((own_ref, core_ref[0]), (other_ref, 1 - core_ref[0])):
        place = pl.ds(pl.multiple_of(who * half, DH), half)
        for source, target in (
            (key_ref.at[:, place], out_ref.at[pl.ds(0, depth), pl.ds(0, half)]),
            (value_ref.at[:, place], out_ref.at[pl.ds(0, depth), pl.ds(half, half)]),
            (query_ref.at[pl.ds(0, lines), place], out_ref.at[pl.ds(depth, lines), pl.ds(0, half)]),
            (query_ref.at[pl.ds(lines, lines), place], out_ref.at[pl.ds(depth, lines), pl.ds(half, half)]),
        ):
            copies.append(pltpu.make_async_copy(source, target, sems.at[len(copies)]))
            copies[-1].start()
    for copy in copies:
        copy.wait()


def pack(core, w_key, w_value, queries):
    depth, panel = w_key.shape
    out = jax.ShapeDtypeStruct((depth + queries.shape[0] // 2, panel), w_key.dtype)
    return pl.pallas_call(
        pack_kernel,
        out_shape=[out, out],
        in_specs=[SMEM, ANY, ANY, ANY],
        out_specs=[VMEM, VMEM],
        scratch_shapes=[pltpu.SemaphoreType.DMA((8,))],
        compiler_params=WIDE,
    )(core, w_key, w_value, queries)


def output_kernel(place_ref, own_ref, sibling_ref, *refs):
    chips = (len(refs) - 1) // 2
    weights, terms, result = refs[:chips], refs[chips:-1], refs[-1]
    own, sibling = own_ref[...], sibling_ref[...]
    first = place_ref[1] == 0
    rows = jnp.concatenate([jnp.where(first, own, sibling), jnp.where(first, sibling, own)], axis=1)
    for j, w_ref in enumerate(weights):
        total = jnp.dot(rows, w_ref[...], preferred_element_type=jnp.float32)
        result[j] = total.astype(jnp.bfloat16)
    for i, term in enumerate(terms):
        term[...] = result[place_ref[0] ^ i]


def output_terms(place, own, sibling, weights):
    chips, shape = len(weights), (own.shape[0], weights[0].shape[1])
    return pl.pallas_call(
        output_kernel,
        out_shape=[jax.ShapeDtypeStruct(shape, jnp.bfloat16)] * chips,
        in_specs=[SMEM] + [VMEM] * (2 + chips),
        out_specs=[VMEM] * chips,
        scratch_shapes=[pltpu.VMEM((chips, *shape), jnp.bfloat16)],
        compiler_params=PARAMS,
    )(place, own, sibling, *weights)


def add_kernel(core_ref, *refs):
    terms, (own_ref, other_ref) = refs[:-2], refs[-2:]
    count = own_ref.shape[0]
    for out_ref, who in ((own_ref, core_ref[0]), (other_ref, 1 - core_ref[0])):
        lines = pl.ds(pl.multiple_of(who * count, count), count)
        total = terms[0][lines, :].astype(jnp.float32)
        for term in terms[1:]:
            total += term[lines, :].astype(jnp.float32)
        out_ref[...] = total.astype(jnp.bfloat16)


def add_terms(core, terms):
    rows, width = terms[0].shape
    out = jax.ShapeDtypeStruct((rows // CORES, width), jnp.bfloat16)
    return pl.pallas_call(
        add_kernel,
        out_shape=[out, out],
        in_specs=[SMEM] + [VMEM] * len(terms),
        out_specs=[VMEM, VMEM],
        compiler_params=PARAMS,
    )(core, *terms)


def place_kernel(core_ref, mine_ref, theirs_ref, out_ref):
    width = mine_ref.shape[1]
    for part_ref, who in ((mine_ref, core_ref[0]), (theirs_ref, 1 - core_ref[0])):
        out_ref[:, pl.ds(pl.multiple_of(who * width, DH), width)] = part_ref[...]


def place_lanes(core, mine, theirs):
    rows, width = mine.shape
    return pl.pallas_call(
        place_kernel,
        out_shape=jax.ShapeDtypeStruct((rows, CORES * width), mine.dtype),
        in_specs=[SMEM, VMEM, VMEM],
        out_specs=VMEM,
        compiler_params=PARAMS,
    )(core, mine, theirs)


def on_device(n_dp, n_ctx, context, w_key, w_value, queries, offsets, head_gain, w_out):
    chips = n_ctx // CORES
    rows = context.shape[0]
    depth, panel = w_key.shape
    heads = panel // CORES // DH
    lat_count = queries.shape[0]
    me, mine_dp = lax.axis_index("ctx"), lax.axis_index("dp")
    chip, core = me // CORES, lax.rem(me, CORES)
    core_only = core.reshape(1)

    def across(array, bits):
        return lax.ppermute(array, "ctx", [(i, i ^ bits) for i in range(n_ctx)])

    def over_dp(array, bits):
        return lax.ppermute(array, "dp", [(d, d ^ bits) for d in range(n_dp)])

    def after(array, *others):
        return lax.optimization_barrier((array, others))[0]

    near_first = sorted(range(1, chips), key=lambda j: (j.bit_count(), -j))
    own_part, other_part = pack(core_only, w_key, w_value, queries)
    pairs = [None] * chips
    for j in near_first:
        if j & (j - 1) == 0:
            pairs[j] = (across(own_part, CORES * j), across(other_part, CORES * j + 1))
    context_sibling = across(after(context, own_part), 1)
    pairs[0] = (own_part, across(after(other_part, context_sibling), 1))

    places = jnp.stack(
        [(chip ^ j) * CORES + who for j in range(chips) for who in (core, 1 - core)]
    ).astype(jnp.int32)
    starts = places * depth
    first_acc, _ = project(starts[:CORES], context, context_sibling, pairs[0], None, depth)
    for j in near_first:
        low = j & -j
        if j != low:
            held, near = pairs[j ^ low], pairs[1]
            pairs[j] = (
                across(after(held[0], near[0]), CORES * low),
                across(after(held[1], near[1], first_acc), CORES * low),
            )
    blocks = [part for pair in pairs for part in pair]
    last = CORES * (chips - 1)
    acc, slices = project(
        starts[CORES:], context, context_sibling, blocks[CORES:last], first_acc, depth
    )
    firsts = jnp.stack([me * rows, (me ^ 1) * rows]).astype(jnp.int32)
    groups = tuple((CORES * z, CORES * z + 1) for z in range(chips))
    slot_groups = (chip ^ jnp.arange(chips)).astype(jnp.int32)
    messages = attend(
        firsts, slot_groups, places, slices, blocks, acc, offsets, groups, heads, depth
    )
    arrived = [messages[0]] + [across(messages[j], CORES * j) for j in range(1, chips)]
    shards = [after(w_out, acc)] + [None] * (chips - 1)
    for j in near_first:
        low = j & -j
        shard = shards[j ^ low]
        shards[j] = across(shard if j == low else after(shard, messages[0]), CORES * low)
    normed = combine(core_only, arrived, head_gain.reshape(1, panel), heads)

    terms = output_terms(
        jnp.stack([mine_dp ^ chip, core]).astype(jnp.int32), normed, across(normed, 1), shards
    )
    terms = [terms[0]] + [over_dp(terms[i], i) for i in range(1, n_dp)]
    mine, other = add_terms(core_only, terms)
    theirs = across(other, 1)
    return place_lanes(core_only, mine, theirs)


def solution(mesh):
    n_dp, n_ctx = mesh.shape["dp"], mesh.shape["ctx"]
    placed = (
        P("ctx", None),
        P("ctx", "dp"),
        P("ctx", "dp"),
        P("ctx", "dp"),
        P(),
        P("dp"),
        P("dp", "ctx"),
    )

    def body(*args):
        return on_device(n_dp, n_ctx, *args)

    return jax.shard_map(
        body, mesh=mesh, in_specs=placed, out_specs=P("ctx", "dp"), check_vma=False
    )
```
